128 devices in a mesh: store: 32 (over y, x, core), frame: 4 (over z).
Axes of the slice: x: 4, y: 4, z: 4, core: 2. Of those that a mesh axis runs over, the one named last changes fastest.
Arguments:
- act: bfloat16 [16384, 2048], P(('store', 'frame')), may hold values from -6 to 6
- cache_rows: bfloat16 [16384, 128], P(('store', 'frame')), may hold values from -6 to 6
- row_dest: int32 [16384], P(('store', 'frame')), may hold values from 0 to 31, as said below
- time_index: int32 [32], P('store'), may hold values from 0 to 999
- w_embed: bfloat16 [64, 2048], replicated, may hold values from -0.75 to 0.75
- norm_gain: float32 [2048], replicated, may hold values from 0.5 to 8
- w_qkv: bfloat16 [3, 2048, 2048], P(None, None, 'frame'), may hold values from -0.125 to 0.125
- w_out_attn: bfloat16 [2048, 2048], P('frame'), may hold values from -0.125 to 0.125
- w_head: bfloat16 [2048, 64], replicated, may hold values from -0.125 to 0.125
Outputs:
- frame_loss: float32 [32, 4], P('store', 'frame')
- grad_qkv: float32 [3, 2048, 2048], P(None, None, 'frame')
- grad_out_attn: float32 [2048, 2048], P('frame')
The draws below stay inside these ranges and needn't reach their ends.
Inputs may be any that keep to these rules, and one draw needn't show every extreme that they name: `row_dest`: over the devices of one frame index, each store index is named by exactly 128 rows. The rows of one device name any one store index at most 8 times, and some store index exactly 8 times.
All inputs are finite; a program needn't handle non-finite values.
Results may differ from the reference program's by a relative error of at most 0.02.
The reference program's roundings to bfloat16 on the way (of `pair`, `noised`, `normed`, `probs_b`, `attended` and `upstream`) count: a program that leaves them out, or rounds other values in their place, can miss the bound.
Values may be sent and summed in bfloat16 or wider, within the bound.
No kernel may reach another device: no remote copies, remote signals or barrier semaphores. Data moves between devices by JAX's collectives and lax.ppermute only.
A program may use at most 128 MiB of HBM per device.

```python
import math
import jax
import jax.numpy as jnp
import numpy as np
from jax import lax

D = 2048
HEADS = 16
HEAD_DIM = 128
PATCH = 64
TIMESTEPS = 1000
TOK_DEV = 128
CAP = 8
CLIPS = 32
TOKENS = 16384
N_STORE = 32
N_FRAME = 4


def draw_row_dest(key, part):
    store_count = N_STORE
    frame_count = N_FRAME
    token_count = TOK_DEV
    capacity = CAP
    others = store_count - 1
    leftover = token_count - capacity
    base_each = leftover // others
    extra_count = leftover % others
    table = np.array([capacity] + [base_each + 1] * extra_count + [base_each] * (others - extra_count), dtype=np.int32)
    key_shuffle, key_order = jax.random.split(key, 2)
    shuffle_keys = jax.random.split(key_shuffle, frame_count)
    shuffles = jax.vmap(lambda item: jax.random.permutation(item, store_count))(shuffle_keys)
    loads = jnp.asarray(table)[shuffles]
    bounds = jnp.cumsum(loads, axis=1)
    items = jnp.arange(token_count, dtype=jnp.int32)
    offset_of = jnp.sum((bounds[:, None, :] <= items[None, :, None]).astype(jnp.int32), axis=2)
    order_keys = jax.random.split(key_order, store_count * frame_count)
    orders = jax.vmap(lambda item: jax.random.permutation(item, token_count))(order_keys)
    orders = orders.reshape(store_count, frame_count, token_count)
    spread = jnp.broadcast_to(offset_of[None, :, :], (store_count, frame_count, token_count))
    offsets = jnp.take_along_axis(spread, orders, axis=2)
    holders = jnp.arange(store_count, dtype=jnp.int32)[:, None, None]
    dests = (holders + offsets) % store_count
    return dests.reshape(store_count * frame_count * token_count).astype(jnp.int32)


def draw_norm_gain(key, part):
    key_base = jax.random.fold_in(key, 0)
    gains = jnp.exp(jax.random.uniform(key_base, (D,), jnp.float32, math.log(0.5), math.log(2.0)))
    return gains.astype(jnp.float32)


def with_ends(drawn, rng, smallest, largest):
    longest = drawn.shape.index(max(drawn.shape))
    spots = []
    for shift in (0, 1):
        where = [jax.random.randint(jax.random.fold_in(rng, axis), (), 0, length) for axis, length in enumerate(drawn.shape)]
        where[longest] = (where[longest] + shift) % drawn.shape[longest]
        spots.append(tuple(where))
    return drawn.at[spots[0]].set(smallest).at[spots[1]].set(largest)


def levels(stream_key, dims, shards, least, top_value):
    gain = 1.0
    for dim, blocks in shards:
        draws = jax.random.uniform(jax.random.fold_in(jax.random.fold_in(stream_key, 6), dim), (blocks,), jnp.float32, least / len(shards), top_value / len(shards))
        gain = gain * jnp.repeat(jnp.exp(draws), dims[dim] // blocks).reshape((-1,) + (1,) * (len(dims) - 1 - dim))
    return gain


def normal_values(rng, extent, deviation, reach, pieces=(), kind=jnp.bfloat16):
    values = deviation * jax.random.normal(rng, extent, jnp.float32)
    if pieces:
        values = values * levels(rng, extent, pieces, -0.22, 0.18)
    return jnp.clip(values, -reach, reach).astype(kind)


def setup_inputs(seed: int = 0) -> dict:
    key_list = jax.random.split(jax.random.key(seed), 10)
    act = normal_values(key_list[0], (TOKENS, D), 1.0, 6.0, ((0, 128),))
    cache_rows = normal_values(key_list[1], (TOKENS, 2 * PATCH), 1.0, 6.0, ((0, 128),))
    row_dest = draw_row_dest(jax.random.fold_in(key_list[9], 71), 0)
    time_index = with_ends(jax.random.randint(key_list[3], (CLIPS,), 0, TIMESTEPS), jax.random.fold_in(key_list[3], 1), 0, TIMESTEPS - 1).astype(jnp.int32)
    w_embed = normal_values(key_list[4], (PATCH, D), PATCH ** -0.5, 0.75)
    norm_gain = draw_norm_gain(jax.random.fold_in(key_list[9], 71), 0)
    w_qkv = normal_values(key_list[6], (3, D, HEADS * HEAD_DIM), D ** -0.5, 0.125, ((2, 4),))
    w_out_attn = normal_values(key_list[7], (HEADS * HEAD_DIM, D), (HEADS * HEAD_DIM) ** -0.5, 0.125, ((0, 4),))
    w_head = normal_values(key_list[8], (D, PATCH), D ** -0.5, 0.125)
    return {"act": act, "cache_rows": cache_rows, "row_dest": row_dest, "time_index": time_index, "w_embed": w_embed, "norm_gain": norm_gain, "w_qkv": w_qkv, "w_out_attn": w_out_attn, "w_head": w_head}


highest = lax.Precision.HIGHEST

def fetch_rows(cache_rows, row_dest):
    width_two = 2 * PATCH
    dests = row_dest.reshape(N_STORE, N_FRAME, TOK_DEV).transpose(1, 0, 2).reshape(N_FRAME, N_STORE * TOK_DEV)
    stored = cache_rows.reshape(N_STORE, N_FRAME, TOK_DEV, width_two).transpose(1, 0, 2, 3)
    stored = stored.reshape(N_FRAME, N_STORE * TOK_DEV, width_two)
    orders = jnp.argsort(dests, axis=1, stable=True)
    arranged = jnp.take_along_axis(stored, orders[:, :, None], axis=1)
    arranged = arranged.reshape(N_FRAME, N_STORE, TOK_DEV, width_two).transpose(1, 0, 2, 3)
    return arranged.reshape(N_STORE, N_FRAME * TOK_DEV, width_two)

def clip_pass(act_clip, pair, tindex, w_embed, norm_gain, w_qkv, w_out_attn, w_head):
    f32 = jnp.float32
    bf16 = jnp.bfloat16
    moment = (tindex.astype(f32) + 0.5) / TIMESTEPS
    noise = pair[:, :PATCH].astype(f32)
    endpoint = pair[:, PATCH:].astype(f32)
    noised = ((1.0 - moment) * noise + moment * endpoint).astype(bf16)
    velocity = endpoint - noise
    hidden = act_clip.astype(f32) + jnp.dot(noised, w_embed, preferred_element_type=f32)
    normed = (hidden * lax.rsqrt(lax.optimization_barrier(jnp.mean(hidden * hidden, axis=1, keepdims=True)) + 1e-06) * norm_gain).astype(bf16)
    shape4 = (N_FRAME, TOK_DEV, HEADS, HEAD_DIM)
    query = jnp.dot(normed, w_qkv[0], preferred_element_type=f32).astype(bf16)
    keyset = jnp.dot(normed, w_qkv[1], preferred_element_type=f32).astype(bf16)
    valueset = jnp.dot(normed, w_qkv[2], preferred_element_type=f32).astype(bf16)
    query_f = query.reshape(shape4).astype(f32)
    key_f = keyset.reshape(shape4).astype(f32)
    value_f = valueset.reshape(shape4).astype(f32)
    inv_root = 1.0 / math.sqrt(HEAD_DIM)
    scores = jnp.einsum('fphd,gphd->phfg', query_f, key_f) * inv_root
    probs = jax.nn.softmax(scores, axis=-1)
    probs_b = lax.optimization_barrier(probs.astype(bf16)).astype(f32)
    attended = jnp.einsum('phfg,gphd->fphd', probs_b, value_f).astype(bf16)
    attended = attended.reshape(N_FRAME * TOK_DEV, HEADS * HEAD_DIM)
    block_out = hidden + jnp.dot(attended, w_out_attn, preferred_element_type=f32)
    head_f32 = w_head.astype(f32)
    predicted = jnp.dot(block_out, head_f32, precision=highest)
    error = predicted - velocity
    losses = lax.optimization_barrier(jnp.mean((error * error).reshape(N_FRAME, TOK_DEV * PATCH), axis=1))
    slope = 2.0 * error / N_STORE
    upstream = jnp.dot(slope, head_f32.T, precision=highest).astype(bf16)
    grad_att = jnp.dot(upstream, w_out_attn.T, preferred_element_type=f32)
    contraction = (((0,), (0,)), ((), ()))
    term_out = lax.dot_general(attended, upstream, contraction, preferred_element_type=f32)
    grad4 = grad_att.reshape(shape4)
    dprob = jnp.einsum('fphd,gphd->phfg', grad4, value_f)
    dvalue = jnp.einsum('phfg,fphd->gphd', probs_b, grad4)
    dscore = probs * (dprob - lax.optimization_barrier(jnp.sum(dprob * probs, axis=-1, keepdims=True)))
    dquery = jnp.einsum('phfg,gphd->fphd', dscore, key_f) * inv_root
    dkey = jnp.einsum('phfg,fphd->gphd', dscore, query_f) * inv_root
    terms = []
    for derivative in (dquery, dkey, dvalue):
        flat = derivative.astype(bf16).reshape(N_FRAME * TOK_DEV, HEADS * HEAD_DIM)
        terms.append(lax.dot_general(normed, flat, contraction, preferred_element_type=f32))
    term_qkv = jnp.stack(terms)
    return (losses, term_qkv, term_out)

def reference(act, cache_rows, row_dest, time_index, w_embed, norm_gain, w_qkv, w_out_attn, w_head):
    fetched = fetch_rows(cache_rows, row_dest)
    acts = act.reshape(N_STORE, N_FRAME * TOK_DEV, D)

    def step(carry, inputs):
        act_clip, pair, tindex = inputs
        losses, term_qkv, term_out = clip_pass(act_clip, pair, tindex, w_embed, norm_gain, w_qkv, w_out_attn, w_head)
        round_qkv = lax.optimization_barrier(term_qkv.astype(jnp.bfloat16))
        round_out = lax.optimization_barrier(term_out.astype(jnp.bfloat16))
        return ((carry[0] + round_qkv.astype(jnp.float32), carry[1] + round_out.astype(jnp.float32)), losses)
    start = (jnp.zeros((3, D, HEADS * HEAD_DIM), jnp.float32), jnp.zeros((HEADS * HEAD_DIM, D), jnp.float32))
    totals, losses = lax.scan(step, start, (acts, fetched, time_index))
    return (losses, totals[0], totals[1])
```

```python
import math

import jax
import jax.numpy as jnp
from jax import lax
from jax.experimental import pallas as pl
from jax.experimental.pallas import tpu as pltpu
from jax.sharding import Mesh, PartitionSpec as P

HEAD_DIM = 128
TIMESTEPS = 1000
UNUSED = 64.0
f32 = jnp.float32
bf16 = jnp.bfloat16
HIGHEST = lax.Precision.HIGHEST
INV_ROOT = 1.0 / math.sqrt(HEAD_DIM)


def shift(value, axis, offset):
    size = lax.axis_size(axis)
    return lax.ppermute(value, axis, [(i, (i + offset) % size) for i in range(size)])


def bucket_rows(cache_rows, row_dest):
    rows = row_dest.shape[0]
    index = jnp.arange(rows, dtype=jnp.int32)
    same = (row_dest[:, None] == row_dest[None, :]) & (index[None, :] < index[:, None])
    slot = row_dest * 8 + jnp.sum(same.astype(jnp.int32), axis=1)
    onehot = jnp.arange(256, dtype=jnp.int32)[:, None] == slot[None, :]
    moved = jnp.dot(onehot.astype(bf16), cache_rows, preferred_element_type=f32)
    used = jnp.any(onehot, axis=1, keepdims=True)
    return jnp.where(used, moved, UNUSED).astype(bf16)


def compact(arrived):
    slots = arrived.shape[1]
    half = (jnp.arange(slots) % 16) // 8
    valid = arrived[:, :, 0] < 32.0
    mine = valid[None] & (half[None, None, :] == jnp.arange(2)[:, None, None])
    order = jnp.arange(slots)
    before = (order[None, :] < order[:, None]).astype(bf16)
    rank = jnp.einsum("kfs,ts->kft", mine.astype(bf16), before, preferred_element_type=f32)
    rank = jnp.where(mine, rank, -1.0)
    pick = rank[:, :, None, :] == jnp.arange(128, dtype=f32)[None, None, :, None]
    return jnp.einsum(
        "kfrs,fsc->kfrc", pick.astype(bf16), arrived, preferred_element_type=f32
    ).astype(bf16)


def forward(arrived, act8, moments, w_embed, norm_gain, w_t, mix):
    pair = compact(arrived)
    noise = pair[..., :64].astype(f32)
    endpoint = pair[..., 64:].astype(f32)
    t = moments.reshape(2, 1, 1, 1)
    noised = ((1.0 - t) * noise + t * endpoint).astype(bf16).reshape(1024, 64)
    hidden = act8.astype(f32) + jnp.dot(noised, w_embed, preferred_element_type=f32)
    normed = (
        hidden * lax.rsqrt(jnp.mean(hidden * hidden, axis=1, keepdims=True) + 1e-06) * norm_gain
    ).astype(bf16)
    proj = lax.dot_general(
        w_t, normed, (((1,), (1,)), ((), ())), preferred_element_type=f32
    ).astype(bf16)
    query, key, value = (proj.reshape(2, 3, 128, 2, 4, 128)[:, j].astype(f32) for j in range(3))
    scores = jnp.einsum("hdkfp,hdkgp->hkfgp", query, key) * INV_ROOT
    probs = jax.nn.softmax(scores, axis=3)
    probs_b = probs.astype(bf16).astype(f32)
    attended = jnp.einsum("hkfgp,hdkgp->hdkfp", probs_b, value).astype(bf16).reshape(256, 1024)
    part = lax.dot_general(
        mix, attended.astype(f32), (((0,), (0,)), ((), ())), precision=HIGHEST
    )
    velocity = (endpoint - noise).reshape(1024, 64)
    return hidden, normed, proj, probs, attended, part, velocity


def backward(error, normed, proj, probs, attended, mix, x, y):
    slope = error * (2.0 / 32.0)
    grad = jnp.dot(mix, slope, precision=HIGHEST).reshape(2, 128, 2, 4, 128)
    query, key, value = (proj.reshape(2, 3, 128, 2, 4, 128)[:, j].astype(f32) for j in range(3))
    probs_b = probs.astype(bf16).astype(f32)
    dprob = jnp.einsum("hdkfp,hdkgp->hkfgp", grad, value)
    dvalue = jnp.einsum("hkfgp,hdkfp->hdkgp", probs_b, grad)
    dscore = probs * (dprob - jnp.sum(dprob * probs, axis=3, keepdims=True))
    dquery = jnp.einsum("hkfgp,hdkgp->hdkfp", dscore, key) * INV_ROOT
    dkey = jnp.einsum("hkfgp,hdkfp->hdkgp", dscore, query) * INV_ROOT
    delta = jnp.stack([dquery, dkey, dvalue], axis=1).astype(bf16).reshape(2, 384, 1024)
    pieces = []
    for h, me in ((0, x), (1, y)):
        factor = lax.dot_general(
            slope, attended[h * 128 : h * 128 + 128].astype(f32), (((1,), (1,)), ((), ())), precision=HIGHEST
        ).astype(bf16)
        factor = jnp.concatenate([factor[i * 16 : i * 16 + 16] for i in range(4)], axis=1)
        row = []
        for o in range(4):
            cols = lax.dynamic_slice(normed, (0, lax.rem(me + o, 4) * 512), (1024, 512))
            grads = jnp.dot(delta[h], cols, preferred_element_type=f32).astype(bf16)
            row.append(jnp.concatenate([grads, factor], axis=0))
        pieces.append(row)
    return pieces


def total(parts):
    out = parts[0].astype(f32)
    for p in parts[1:]:
        out = out + p.astype(f32)
    return out.astype(bf16)


def second_pieces(summed, me):
    factor = jnp.concatenate([summed[384:, i * 128 : i * 128 + 128] for i in range(4)], axis=0)
    out = []
    for o in range(4):
        cols = lax.dynamic_slice(summed, (0, lax.rem(me + o, 4) * 128), (384, 128))
        out.append(jnp.concatenate([cols, factor], axis=0))
    return out


def assemble_kernel(place, mine, theirs, out):
    n = pl.program_id(0)
    x, y, core = place[0], place[1], place[2]
    for h, (a, b) in ((0, (x, y)), (1, (y, x))):
        first = (a + 4 - n // 4) % 4
        second = (b + 4 - n % 4) % 4
        for source, half in ((mine, core), (theirs, 1 - core)):
            start = pl.multiple_of(half * 256 + h * 128, 128)
            out[:, :, pl.ds(start, 128)] = source[h, first, second].astype(f32)


def assemble(mine, theirs, place):
    return pl.pallas_call(
        assemble_kernel,
        grid_spec=pltpu.PrefetchScalarGridSpec(
            num_scalar_prefetch=1,
            grid=(16,),
            in_specs=[pl.BlockSpec((2, 4, 4, 3, 128, 128), lambda n, p: (0,) * 6)] * 2,
            out_specs=pl.BlockSpec((3, 128, 512), lambda n, p: (0, n, 0)),
        ),
        out_shape=jax.ShapeDtypeStruct((3, 2048, 512), f32),
        compiler_params=pltpu.CompilerParams(vmem_limit_bytes=40 << 20),
    )(place, mine, theirs)


def shards(act, cache_rows, row_dest, time_index, w_embed, norm_gain, w_qkv, w_out, w_head):
    x, y, core, frame = (lax.axis_index(a) for a in ("x", "y", "core", "frame"))
    act8 = lax.all_gather(act, ("core", "frame"), axis=0, tiled=True)
    bucket = bucket_rows(cache_rows, row_dest).reshape(1, 16, 1, 16, 128)
    sent = jnp.broadcast_to(bucket, (4, 16, 2, 16, 128)).reshape(128, 16, 128)
    arrived = lax.all_to_all(sent, ("frame", "y", "x", "core"), 0, 0, tiled=True)
    arrived = arrived.reshape(4, 512, 128)
    moment = (time_index.astype(f32) + 0.5) / TIMESTEPS
    other = shift(moment, "core", 1)
    moments = jnp.where(core == 0, jnp.concatenate([moment, other]), jnp.concatenate([other, moment]))

    w_c = lax.dynamic_slice(w_qkv, (0, 0, core * 256), (3, 2048, 256))
    w_t = w_c.reshape(3, 2048, 2, 128).transpose(2, 0, 3, 1).reshape(768, 2048)
    w_out_c = lax.dynamic_slice(w_out, (core * 256, 0), (256, 2048))
    mix = jnp.dot(w_out_c, w_head, preferred_element_type=f32)

    hidden, normed, proj, probs, attended, part, velocity = forward(
        arrived, act8, moments, w_embed, norm_gain, w_t, mix
    )
    own = (core * 4 + frame) * 128
    hidden_own = lax.dynamic_slice(hidden, (own, 0), (128, 2048))
    velocity_own = lax.dynamic_slice(velocity, (own, 0), (128, 64))
    rest = jnp.dot(hidden_own, w_head.astype(f32), precision=HIGHEST) - velocity_own
    blocks = part.reshape(64, 8, 128).transpose(1, 0, 2)
    blocks = lax.all_to_all(blocks, ("core", "frame"), 0, 0, tiled=True)
    error_own = jnp.sum(blocks, axis=0) + rest.T
    frame_loss = jnp.mean(error_own * error_own).reshape(1, 1)
    errors = lax.all_to_all(
        jnp.broadcast_to(error_own[None], (8, 64, 128)), ("core", "frame"), 0, 0, tiled=True
    )
    error = errors.transpose(1, 0, 2).reshape(64, 1024)

    first = backward(error, normed, proj, probs, attended, mix, x, y)
    axes = (("x", "y"), ("y", "x"))
    moved = [[shift(first[h][o], axes[h][0], o) for o in (1, 3, 2)] for h in range(2)]
    summed = [total([first[h][0], *moved[h]]) for h in range(2)]
    second = [second_pieces(summed[0], y), second_pieces(summed[1], x)]
    moved = [[shift(second[h][o], axes[h][1], o) for o in (1, 3, 2)] for h in range(2)]
    final = [total([second[h][0], *moved[h]]) for h in range(2)]
    owned = [final[h][:384].reshape(3, 128, 128).transpose(0, 2, 1) for h in range(2)]
    factor = jnp.stack([final[h][384:] for h in range(2)])
    back = [{o: shift(owned[h], axes[h][1], o) for o in (1, 3, 2)} for h in range(2)]
    line = [jnp.stack([owned[h], back[h][1], back[h][2], back[h][3]]) for h in range(2)]
    wide = [{o: shift(line[h], axes[h][0], o) for o in (1, 3, 2)} for h in range(2)]
    mine = jnp.stack(
        [jnp.stack([line[h], wide[h][1], wide[h][2], wide[h][3]]) for h in range(2)]
    )
    theirs = shift(mine, "core", 1)
    factor_theirs = shift(factor, "core", 1)
    grad_qkv = assemble(mine, theirs, jnp.stack([x, y, core]).astype(jnp.int32))
    f_low = jnp.where(core == 0, factor, factor_theirs)
    f_high = jnp.where(core == 0, factor_theirs, factor)
    factors = jnp.concatenate([f_low, f_high]).transpose(0, 2, 1).reshape(512, 64)
    grad_out = lax.dot_general(
        factors, w_head, (((1,), (1,)), ((), ())), preferred_element_type=f32
    )
    return frame_loss, grad_qkv, grad_out


def solution(mesh):
    fine = Mesh(mesh.devices.reshape(4, 4, 2, 4), ("y", "x", "core", "frame"))
    store = ("y", "x", "core")
    in_specs = (
        P((*store, "frame"), None),
        P((*store, "frame"), None),
        P((*store, "frame")),
        P(store),
        P(),
        P(),
        P(None, None, "frame"),
        P("frame", None),
        P(),
    )
    out_specs = (P(store, "frame"), P(None, None, "frame"), P("frame", None))
    return jax.shard_map(shards, mesh=fine, in_specs=in_specs, out_specs=out_specs, check_vma=False)
```

```python
import functools
import math

import jax
import jax.numpy as jnp
from jax import lax
from jax.experimental import pallas as pl
from jax.experimental.pallas import tpu as pltpu
from jax.sharding import Mesh, PartitionSpec as P

HEAD_DIM = 128
TIMESTEPS = 1000
UNUSED = 64.0
f32 = jnp.float32
bf16 = jnp.bfloat16
HIGHEST = lax.Precision.HIGHEST
INV_ROOT = 1.0 / math.sqrt(HEAD_DIM)
NN = (((1,), (0,)), ((), ()))
NT = (((1,), (1,)), ((), ()))
TN = (((0,), (0,)), ((), ()))
ORDER = (0, 1, 3, 2)
SPOT = {r: i for i, r in enumerate(ORDER)}
VMEM = pl.BlockSpec(memory_space=pltpu.VMEM)
SMEM = pl.BlockSpec(memory_space=pltpu.SMEM)


def params(mib):
    return pltpu.CompilerParams(vmem_limit_bytes=mib << 20)


def cost(flops, moved):
    return pl.CostEstimate(flops=flops, bytes_accessed=moved, transcendentals=0)


def dot(a, b, dims=NN, precision=None):
    return lax.dot_general(a, b, dims, preferred_element_type=f32, precision=precision)


def shift(value, axis, offset):
    size = lax.axis_size(axis)
    return lax.ppermute(value, axis, [(i, (i + offset) % size) for i in range(size)])


def shape(dims, kind):
    return jax.ShapeDtypeStruct(dims, kind)


def bucket_kernel(rows, dest_row, dest_col, out):
    earlier = lax.broadcasted_iota(jnp.int32, (128, 128), 0) < lax.broadcasted_iota(
        jnp.int32, (128, 128), 1
    )
    same = jnp.where((dest_col[...] == dest_row[...]) & earlier, 1.0, 0.0)
    slot = dest_row[...] * 8 + jnp.sum(same, axis=0, keepdims=True).astype(jnp.int32)
    hot = jnp.where(lax.broadcasted_iota(jnp.int32, (256, 128), 0) == slot, 1.0, 0.0)
    used = jnp.max(hot, axis=1, keepdims=True)
    moved = dot(hot.astype(bf16), rows[...]) + (1.0 - used) * UNUSED
    bucket = moved.astype(bf16).reshape(16, 16, 128)
    for frame in range(4):
        for core in range(2):
            out[frame, :, core] = bucket


def prepare_kernel(place, w, w_out, head_t, w_t, mix, mix_t):
    for h in range(2):
        w_t[h, 0] = w[0, :, h * 128 : h * 128 + 128].T

    @pl.when(pl.program_id(0) == 0)
    def _():
        mix[...] = dot(w_out[...], head_t[...], NT)
        mix_t[...] = dot(head_t[...], w_out[...], NT)


def fetch_kernel(place, arrived, pairs):
    frame, core = place[0], place[1]
    slots = 512
    before = jnp.where(
        lax.broadcasted_iota(jnp.int32, (slots, slots), 1)
        < lax.broadcasted_iota(jnp.int32, (slots, slots), 0),
        1.0,
        0.0,
    ).astype(bf16)
    half = (lax.broadcasted_iota(jnp.int32, (slots, 128), 0) // 8) % 2
    lane = lax.broadcasted_iota(jnp.int32, (slots, 128), 1).astype(f32)
    for i, r in enumerate(ORDER):
        rows = arrived[(frame + 4 - r) % 4]
        valid = jnp.broadcast_to(rows[:, 0:1].astype(f32), (slots, 128)) < 32.0
        for other in range(2):
            clip = core + other - 2 * core * other
            mine = jnp.where(valid & (half == clip), 1.0, 0.0)
            rank = dot(before, mine.astype(bf16))
            pick = jnp.where(rank == lane, mine, 0.0)
            pairs[2 * i + other] = dot(pick.astype(bf16), rows, TN).astype(bf16)


def embed_kernel(first, count, moments, *refs):
    acts, refs = refs[:count], refs[count:]
    pairs, w_embed, gain, w_t, head_t = refs[:5]
    normed, proj = refs[5:7]
    for b in range(count):
        pair = pairs[first + b].astype(f32)
        t = moments[b % 2]
        noised = ((1.0 - t) * pair[:, :64] + t * pair[:, 64:]).astype(bf16)
        hidden = acts[b][...].astype(f32) + dot(noised, w_embed[...])
        scale = lax.rsqrt(jnp.mean(hidden * hidden, axis=1, keepdims=True) + 1e-06)
        normed[b * 128 : b * 128 + 128] = (hidden * scale * gain[...]).astype(bf16)
        if first + b == 0:
            turned = pair.T
            rest = dot(head_t[...].astype(f32), hidden, NT, HIGHEST)
            refs[7][...] = rest - (turned[64:] - turned[:64])
    for i in range(3):
        rows = slice(i * 256, i * 256 + 256)
        proj[rows] = dot(w_t[rows], normed[...], NT).astype(bf16)


def part_of(proj_a, proj_b, row, i, other):
    ref, column = (proj_a, 2 * i + other) if i < 3 else (proj_b, other)
    return ref[row : row + 128, column * 128 : column * 128 + 128].astype(f32)


def lanes(i, other):
    return slice((2 * i + other) * 128, (2 * i + other) * 128 + 128)


def attend_kernel(proj_a, proj_b, mix_t, rest, attended, probs, part_own, part_other):
    for h in range(2):
        for other in range(2):
            read = functools.partial(part_of, proj_a, proj_b)
            keys = [read(h * 384 + 128, g, other) for g in range(4)]
            values = [read(h * 384 + 256, g, other) for g in range(4)]
            for f in range(4):
                query = read(h * 384, f, other)
                scores = [jnp.sum(query * k, axis=0, keepdims=True) * INV_ROOT for k in keys]
                top = jnp.maximum(jnp.maximum(scores[0], scores[1]), jnp.maximum(scores[2], scores[3]))
                powers = [jnp.exp(s - top) for s in scores]
                whole = powers[0] + powers[1] + powers[2] + powers[3]
                prob = [p / whole for p in powers]
                rounded = [p.astype(bf16).astype(f32) for p in prob]
                out = rounded[0] * values[0]
                for g in range(1, 4):
                    out = out + rounded[g] * values[g]
                attended[h * 128 : h * 128 + 128, lanes(f, other)] = out.astype(bf16)
                for g in range(4):
                    probs[h * 2 + other, f * 4 + g : f * 4 + g + 1] = prob[g]
    for other, part in ((0, part_own), (1, part_other)):
        for f in range(4):
            here = attended[:, lanes(f, other)].astype(f32)
            value = dot(mix_t[...], here, NN, HIGHEST)
            if other == 0 and f == 0:
                value = value + rest[...]
            part[:, f * 128 : f * 128 + 128] = value


def gradient_piece(delta, normed_a, normed_b, h, block):
    columns = pl.ds(pl.multiple_of(block * 512, 512), 512)
    rows = slice(h * 384, h * 384 + 384)
    return (
        dot(delta[rows, :768], normed_a[:, columns]) + dot(delta[rows, 768:], normed_b[:, columns])
    ).astype(bf16)


def backward_kernel(
    place, error_own, error_other, proj_a, proj_b, normed_a, normed_b, probs, attended, mix, *refs
):
    pieces, delta, own_factor = refs[:6], refs[6], refs[7]
    slope, grad = refs[8:]
    for i in range(4):
        for other, error in ((0, error_own), (1, error_other)):
            slope[:, lanes(i, other)] = error[:, i * 128 : i * 128 + 128] * (2.0 / 32.0)
    grad[...] = dot(mix[...], slope[...], NN, HIGHEST)
    for h in range(2):
        for other in range(2):
            read = functools.partial(part_of, proj_a, proj_b)
            grads = [grad[h * 128 : h * 128 + 128, lanes(f, other)] for f in range(4)]
            score = [[None] * 4 for _ in range(4)]
            for f in range(4):
                prob = [probs[h * 2 + other, f * 4 + g : f * 4 + g + 1] for g in range(4)]
                dprob = [
                    jnp.sum(grads[f] * read(h * 384 + 256, g, other), axis=0, keepdims=True)
                    for g in range(4)
                ]
                mean = sum(d * p for d, p in zip(dprob, prob))
                for g in range(4):
                    score[f][g] = prob[g] * (dprob[g] - mean) * INV_ROOT
            for g in range(4):
                value = sum(
                    probs[h * 2 + other, f * 4 + g : f * 4 + g + 1].astype(bf16).astype(f32) * grads[f]
                    for f in range(4)
                )
                query = sum(score[g][i] * read(h * 384 + 128, i, other) for i in range(4))
                key = sum(score[f][g] * read(h * 384, f, other) for f in range(4))
                for j, out in enumerate((query, key, value)):
                    row = h * 384 + j * 128
                    delta[row : row + 128, lanes(g, other)] = out.astype(bf16)
    for h in range(2):
        factor = dot(slope[...], attended[h * 128 : h * 128 + 128].astype(f32), NT, HIGHEST)
        factor = factor.astype(bf16)
        own_factor[h] = factor
        for k, o in enumerate((1, 3, 2)):
            out = pieces[h * 3 + k]
            out[:384] = gradient_piece(delta, normed_a, normed_b, h, (place[h] + o) % 4)
            for i in range(4):
                out[384:, i * 128 : i * 128 + 128] = factor[i * 16 : i * 16 + 16]


def keep_kernel(place, delta, normed_a, normed_b, own_factor, out_x, out_y):
    for h, out in ((0, out_x), (1, out_y)):
        out[:384] = gradient_piece(delta, normed_a, normed_b, h, place[h])
        for i in range(4):
            out[384:, i * 128 : i * 128 + 128] = own_factor[h, i * 16 : i * 16 + 16]


def add_first_kernel(place, *refs):
    parts, outs, both = refs[:4], refs[4:8], refs[8]
    total = parts[0][...].astype(f32)
    for part in parts[1:]:
        total = total + part[...].astype(f32)
    both[...] = total.astype(bf16)
    for o, out in enumerate(outs):
        columns = pl.ds(pl.multiple_of(((place[0] + o) % 4) * 128, 128), 128)
        out[:384] = both[:384, columns]
        for i in range(4):
            out[384 + i * 16 : 400 + i * 16] = both[384:, i * 128 : i * 128 + 128]


def add_second_kernel(*refs):
    parts, owned, factor = refs[:4], refs[4], refs[5]
    total = parts[0][...].astype(f32)
    for part in parts[1:]:
        total = total + part[...].astype(f32)
    for j in range(3):
        owned[j] = total[j * 128 : j * 128 + 128].T.astype(bf16)
    factor[...] = total[384:].T.astype(bf16)


def assemble_kernel(chosen, aliased, place, *refs):
    count = len(chosen) * 4
    pieces, out = refs[:count], refs[count + aliased]
    held, ready, done, sems = refs[count + aliased + 1 :]
    loads = [pltpu.make_async_copy(p, held.at[k], sems.at[k]) for k, p in enumerate(pieces)]
    for load in loads:
        load.start()
    stores = [None, None]
    for k in range(count):
        o, theirs, h = chosen[k // 4], (k // 2) % 2, k % 2
        slot = k % 2
        loads[k].wait()
        if stores[slot] is not None:
            stores[slot].wait()
        first = (place[h] + 4 - o) % 4
        for inner in range(4):
            second = (place[1 - h] + 4 - inner) % 4
            ready[slot, :, pl.ds(pl.multiple_of(second * 128, 128), 128)] = held[k, inner].astype(f32)
        core = place[2] if theirs == 0 else 1 - place[2]
        stores[slot] = pltpu.make_async_copy(
            ready.at[slot],
            out.at[
                :,
                pl.ds(pl.multiple_of(first * 512, 512), 512),
                pl.ds(pl.multiple_of(core * 256 + h * 128, 128), 128),
            ],
            done.at[slot],
        )
        stores[slot].start()
    for store in stores:
        store.wait()


def assemble(place, pieces, chosen, onto=None):
    count = len(chosen) * 4
    anywhere = pl.BlockSpec(memory_space=pl.ANY)
    given = [] if onto is None else [onto]
    return pl.pallas_call(
        functools.partial(assemble_kernel, chosen, len(given)),
        in_specs=[SMEM] + [anywhere] * (count + len(given)),
        out_specs=anywhere,
        out_shape=shape((3, 2048, 512), f32),
        scratch_shapes=[
            pltpu.VMEM((count, 4, 3, 128, 128), bf16),
            pltpu.VMEM((2, 3, 512, 128), f32),
            pltpu.SemaphoreType.DMA((2,)),
            pltpu.SemaphoreType.DMA((count,)),
        ],
        input_output_aliases={1 + count: 0} if given else {},
        compiler_params=params(16),
        cost_estimate=cost(0, count * 3 * 393216),
    )(place, *pieces, *given)


def shards(act, cache_rows, row_dest, time_index, w_embed, norm_gain, w_qkv, w_out, w_head):
    x, y, core, frame = (lax.axis_index(a).astype(jnp.int32) for a in ("x", "y", "core", "frame"))
    here = jnp.stack([frame, core])
    square = jnp.stack([x, y, core])

    act_by = {0: act, **{o: shift(act, "frame", o) for o in (1, 3, 2)}}
    act_other = {r: shift(act_by[r], "core", 1) for r in ORDER}

    sent = pl.pallas_call(
        bucket_kernel,
        in_specs=[VMEM] * 3,
        out_specs=VMEM,
        out_shape=shape((4, 16, 2, 16, 128), bf16),
    )(cache_rows, row_dest.reshape(1, 128), row_dest.reshape(128, 1))
    arrived = lax.all_to_all(
        sent.reshape(128, 16, 128), ("frame", "y", "x", "core"), 0, 0, tiled=True
    ).reshape(4, 512, 128)
    moment = (time_index.astype(f32) + 0.5) / TIMESTEPS
    moments = jnp.concatenate([moment, shift(moment, "core", 1)])

    head_t = w_head.T
    w_t, mix, mix_t = pl.pallas_call(
        prepare_kernel,
        grid_spec=pltpu.PrefetchScalarGridSpec(
            num_scalar_prefetch=1,
            grid=(3,),
            in_specs=[
                pl.BlockSpec((1, 2048, 256), lambda j, p: (j, 0, p[1])),
                pl.BlockSpec((256, 2048), lambda j, p: (p[1], 0)),
                pl.BlockSpec((64, 2048), lambda j, p: (0, 0)),
            ],
            out_specs=[
                pl.BlockSpec((2, 1, 128, 2048), lambda j, p: (0, j, 0, 0)),
                pl.BlockSpec((256, 64), lambda j, p: (0, 0)),
                pl.BlockSpec((64, 256), lambda j, p: (0, 0)),
            ],
        ),
        out_shape=[shape((2, 3, 128, 2048), bf16), shape((256, 64), f32), shape((64, 256), f32)],
        compiler_params=params(20),
        cost_estimate=cost(2 * 2 * 256 * 2048 * 64, 8 << 20),
    )(here, w_qkv, w_out, head_t)
    w_t = w_t.reshape(768, 2048)

    pairs = pl.pallas_call(
        fetch_kernel,
        in_specs=[SMEM, VMEM],
        out_specs=VMEM,
        out_shape=shape((8, 128, 128), bf16),
        compiler_params=params(12),
        cost_estimate=cost(600_000_000, 1 << 20),
    )(here, arrived)

    def embed(first, order):
        blocks = [a for r in order for a in (act_by[r], act_other[r])]
        count = len(blocks)
        out = [shape((count * 128, 2048), bf16), shape((768, count * 128), bf16)]
        if first == 0:
            out.append(shape((64, 128), f32))
        return pl.pallas_call(
            functools.partial(embed_kernel, first, count),
            in_specs=[SMEM] + [VMEM] * (count + 5),
            out_specs=[VMEM] * len(out),
            out_shape=out,
            compiler_params=params(40),
            cost_estimate=cost(count * 128 * 2048 * 768 * 2, count * (1 << 20) + (3 << 20)),
        )(moments, *blocks, pairs, w_embed, norm_gain.reshape(1, 2048), w_t, head_t)

    normed_a, proj_a, rest = embed(0, ORDER[:3])
    normed_b, proj_b = embed(6, ORDER[3:])
    attended, probs, part_own, part_other = pl.pallas_call(
        attend_kernel,
        in_specs=[VMEM] * 4,
        out_specs=[VMEM] * 4,
        out_shape=[
            shape((256, 1024), bf16),
            shape((4, 16, 128), f32),
            shape((64, 512), f32),
            shape((64, 512), f32),
        ],
        compiler_params=params(24),
    )(proj_a, proj_b, mix_t, rest)

    clip_part = part_own + shift(part_other, "core", 1)
    heard = {0: clip_part, **{o: shift(clip_part, "frame", o) for o in (1, 3, 2)}}
    error_own = jnp.concatenate(
        [
            sum(
                heard[o][:, SPOT[(r - o) % 4] * 128 : SPOT[(r - o) % 4] * 128 + 128]
                for o in range(4)
            )
            for r in ORDER
        ],
        axis=1,
    )
    frame_loss = jnp.mean(error_own[:, :128] * error_own[:, :128]).reshape(1, 1)
    error_other = shift(error_own, "core", 1)

    *first, delta, own_factor = pl.pallas_call(
        backward_kernel,
        in_specs=[SMEM] + [VMEM] * 9,
        out_specs=[VMEM] * 8,
        out_shape=[shape((400, 512), bf16)] * 6
        + [shape((768, 1024), bf16), shape((2, 64, 128), bf16)],
        scratch_shapes=[pltpu.VMEM((64, 1024), f32), pltpu.VMEM((256, 1024), f32)],
        compiler_params=params(40),
    )(square, error_own, error_other, proj_a, proj_b, normed_a, normed_b, probs, attended, mix)
    axes = (("x", "y"), ("y", "x"))
    moved = [[shift(first[h * 3 + k], axes[h][0], o) for k, o in enumerate((1, 3, 2))] for h in range(2)]
    kept = pl.pallas_call(
        keep_kernel,
        in_specs=[SMEM] + [VMEM] * 4,
        out_specs=[VMEM] * 2,
        out_shape=[shape((400, 512), bf16)] * 2,
        compiler_params=params(32),
        cost_estimate=cost(2 * 2 * 384 * 1024 * 512, 8 << 20),
    )(square, delta, normed_a, normed_b, own_factor)

    owned, factor = [], []
    second = [
        pl.pallas_call(
            add_first_kernel,
            in_specs=[SMEM] + [VMEM] * 4,
            out_specs=[VMEM] * 4,
            out_shape=[shape((448, 128), bf16)] * 4,
            scratch_shapes=[pltpu.VMEM((400, 512), bf16)],
        )(jnp.stack([(y, x)[h]]), kept[h], *moved[h])
        for h in range(2)
    ]
    moved = [[shift(second[h][o], axes[h][1], o) for o in (1, 3, 2)] for h in range(2)]
    for h in range(2):
        o, f = pl.pallas_call(
            add_second_kernel,
            in_specs=[VMEM] * 4,
            out_specs=[VMEM] * 2,
            out_shape=[shape((3, 128, 128), bf16), shape((128, 64), bf16)],
        )(second[h][0], *moved[h])
        owned.append(o)
        factor.append(f)
    back = [{o: shift(owned[h], axes[h][1], o) for o in (1, 3, 2)} for h in range(2)]
    line = [jnp.stack([owned[h], back[h][1], back[h][2], back[h][3]]) for h in range(2)]
    wide = [{0: line[h], **{o: shift(line[h], axes[h][0], o) for o in (1, 3, 2)}} for h in range(2)]
    theirs = [{o: shift(wide[h][o], "core", 1) for o in (0, 1, 3, 2)} for h in range(2)]

    factor = jnp.concatenate(factor)
    factor_theirs = shift(factor, "core", 1)
    factors = jnp.concatenate(
        [jnp.where(core == 0, factor, factor_theirs), jnp.where(core == 0, factor_theirs, factor)]
    )
    grad_out = dot(factors, head_t)

    def pieces(chosen):
        return [side[h][o] for o in chosen for side in (wide, theirs) for h in range(2)]

    grad_qkv = assemble(square, pieces((0, 1, 3)), (0, 1, 3))
    grad_qkv = assemble(square, pieces((2,)), (2,), grad_qkv)
    return frame_loss, grad_qkv, grad_out


def solution(mesh):
    fine = Mesh(mesh.devices.reshape(4, 4, 2, 4), ("y", "x", "core", "frame"))
    store = ("y", "x", "core")
    in_specs = (
        P((*store, "frame"), None),
        P((*store, "frame"), None),
        P((*store, "frame")),
        P(store),
        P(),
        P(),
        P(None, None, "frame"),
        P("frame", None),
        P(),
    )
    out_specs = (P(store, "frame"), P(None, None, "frame"), P("frame", None))
    return jax.shard_map(shards, mesh=fine, in_specs=in_specs, out_specs=out_specs, check_vma=False)
```

```python
import functools
import math

import jax
import jax.numpy as jnp
from jax import lax
from jax.experimental import pallas as pl
from jax.experimental.pallas import tpu as pltpu
from jax.sharding import Mesh, PartitionSpec as P

HEAD_DIM = 128
TIMESTEPS = 1000
UNUSED = 64.0
SPLIT = 208
f32 = jnp.float32
bf16 = jnp.bfloat16
HIGHEST = lax.Precision.HIGHEST
INV_ROOT = 1.0 / math.sqrt(HEAD_DIM)
NN = (((1,), (0,)), ((), ()))
NT = (((1,), (1,)), ((), ()))
TN = (((0,), (0,)), ((), ()))
ORDER = (0, 1, 3, 2)
SPOT = {r: i for i, r in enumerate(ORDER)}
VMEM = pl.BlockSpec(memory_space=pltpu.VMEM)
SMEM = pl.BlockSpec(memory_space=pltpu.SMEM)


def params(mib):
    return pltpu.CompilerParams(vmem_limit_bytes=mib << 20)


def cost(flops, moved):
    return pl.CostEstimate(flops=flops, bytes_accessed=moved, transcendentals=0)


TINY = cost(0, 1024)


def dot(a, b, dims=NN, precision=None):
    return lax.dot_general(a, b, dims, preferred_element_type=f32, precision=precision)


def shift(value, axis, offset):
    size = lax.axis_size(axis)
    return lax.ppermute(value, axis, [(i, (i + offset) % size) for i in range(size)])


def shape(dims, kind):
    return jax.ShapeDtypeStruct(dims, kind)


def bucket_kernel(rows, dest_row, out):
    dest_col = jnp.broadcast_to(dest_row[...].astype(f32), (128, 128)).T
    earlier = lax.broadcasted_iota(jnp.int32, (128, 128), 0) < lax.broadcasted_iota(
        jnp.int32, (128, 128), 1
    )
    same = jnp.where((dest_col == dest_row[...].astype(f32)) & earlier, 1.0, 0.0)
    slot = dest_row[...] * 8 + jnp.sum(same, axis=0, keepdims=True).astype(jnp.int32)
    hot = jnp.where(lax.broadcasted_iota(jnp.int32, (256, 128), 0) == slot, 1.0, 0.0)
    used = jnp.max(hot, axis=1, keepdims=True)
    moved = dot(hot.astype(bf16), rows[...]) + (1.0 - used) * UNUSED
    bucket = moved.astype(bf16).reshape(16, 16, 128)
    for frame in range(4):
        for core in range(2):
            out[frame, :, core] = bucket


def prepare_kernel(place, w, w_out, head_t, w_t, mix, mix_t):
    for h in range(2):
        w_t[h, 0] = w[0, :, h * 128 : h * 128 + 128].T

    @pl.when(pl.program_id(0) == 0)
    def _():
        mix[...] = dot(w_out[...], head_t[...], NT)
        mix_t[...] = dot(head_t[...], w_out[...], NT)


def fetch_kernel(place, arrived, pairs):
    frame, core = place[0], place[1]
    slots = 512
    before = jnp.where(
        lax.broadcasted_iota(jnp.int32, (slots, slots), 1)
        < lax.broadcasted_iota(jnp.int32, (slots, slots), 0),
        1.0,
        0.0,
    ).astype(bf16)
    half = (lax.broadcasted_iota(jnp.int32, (slots, 128), 0) // 8) % 2
    lane = lax.broadcasted_iota(jnp.int32, (slots, 128), 1).astype(f32)
    for i, r in enumerate(ORDER):
        rows = arrived[(frame + 4 - r) % 4]
        valid = jnp.broadcast_to(rows[:, 0:1].astype(f32), (slots, 128)) < 32.0
        for other in range(2):
            clip = core + other - 2 * core * other
            mine = jnp.where(valid & (half == clip), 1.0, 0.0)
            rank = dot(before, mine.astype(bf16))
            pick = jnp.where(rank == lane, mine, 0.0)
            pairs[2 * i + other] = dot(pick.astype(bf16), rows, TN).astype(bf16)


def sides_kernel(before, after, unused, top, bottom, both):
    top[...] = before[:64]
    bottom[...] = after[64:]
    both[0] = before[...]
    both[1] = after[...]


def act_kernel(top, bottom, unused, out):
    out[:64] = top[...]
    out[64:] = bottom[...]


def embed_kernel(first, arrays, picks, moments, *refs):
    acts, refs = refs[:arrays], refs[arrays:]
    pairs, w_embed, gain, w_t, head_t = refs[:5]
    normed, proj = refs[5:7]
    for b, (array, place) in enumerate(picks):
        pair = pairs[first + b].astype(f32)
        act = acts[array][...] if place is None else acts[array][place]
        t = moments[b % 2]
        noised = ((1.0 - t) * pair[:, :64] + t * pair[:, 64:]).astype(bf16)
        hidden = act.astype(f32) + dot(noised, w_embed[...])
        scale = lax.rsqrt(jnp.mean(hidden * hidden, axis=1, keepdims=True) + 1e-06)
        normed[b * 128 : b * 128 + 128] = (hidden * scale * gain[...]).astype(bf16)
        if first + b == 0:
            turned = pair.T
            rest = dot(head_t[...].astype(f32), hidden, NT, HIGHEST)
            refs[7][...] = rest - (turned[64:] - turned[:64])
    for i in range(3):
        rows = slice(i * 256, i * 256 + 256)
        proj[rows] = dot(w_t[rows], normed[...], NT).astype(bf16)


def part_of(proj_a, proj_b, row, i, other):
    ref, column = (proj_a, 2 * i + other) if i < 3 else (proj_b, other)
    return ref[row : row + 128, column * 128 : column * 128 + 128].astype(f32)


def lanes(i, other):
    return slice((2 * i + other) * 128, (2 * i + other) * 128 + 128)


def attend_kernel(proj_a, proj_b, mix_t, rest, attended, probs, part_own, part_other):
    for h in range(2):
        for other in range(2):
            read = functools.partial(part_of, proj_a, proj_b)
            keys = [read(h * 384 + 128, g, other) for g in range(4)]
            values = [read(h * 384 + 256, g, other) for g in range(4)]
            for f in range(4):
                query = read(h * 384, f, other)
                scores = [jnp.sum(query * k, axis=0, keepdims=True) * INV_ROOT for k in keys]
                top = jnp.maximum(jnp.maximum(scores[0], scores[1]), jnp.maximum(scores[2], scores[3]))
                powers = [jnp.exp(s - top) for s in scores]
                whole = powers[0] + powers[1] + powers[2] + powers[3]
                prob = [p / whole for p in powers]
                rounded = [p.astype(bf16).astype(f32) for p in prob]
                out = rounded[0] * values[0]
                for g in range(1, 4):
                    out = out + rounded[g] * values[g]
                attended[h * 128 : h * 128 + 128, lanes(f, other)] = out.astype(bf16)
                for g in range(4):
                    probs[h * 2 + other, f * 4 + g : f * 4 + g + 1] = prob[g]
    for other, part in ((0, part_own), (1, part_other)):
        for f in range(4):
            here = attended[:, lanes(f, other)].astype(f32)
            value = dot(mix_t[...], here, NN, HIGHEST)
            if other == 0 and f == 0:
                value = value + rest[...]
            part[:, f * 128 : f * 128 + 128] = value


def gradient_piece(delta, normed_a, normed_b, h, block):
    columns = pl.ds(pl.multiple_of(block * 512, 512), 512)
    rows = slice(h * 384, h * 384 + 384)
    return (
        dot(delta[rows, :768], normed_a[:, columns]) + dot(delta[rows, 768:], normed_b[:, columns])
    ).astype(bf16)


def backward_kernel(
    place, error_own, error_other, proj_a, proj_b, normed_a, normed_b, probs, attended, mix, *refs
):
    pieces, delta, own_factor = refs[:4], refs[4], refs[5]
    slope, grad = refs[6:]
    for i in range(4):
        for other, error in ((0, error_own), (1, error_other)):
            slope[:, lanes(i, other)] = error[:, i * 128 : i * 128 + 128] * (2.0 / 32.0)
    grad[...] = dot(mix[...], slope[...], NN, HIGHEST)
    for h in range(2):
        for other in range(2):
            read = functools.partial(part_of, proj_a, proj_b)
            grads = [grad[h * 128 : h * 128 + 128, lanes(f, other)] for f in range(4)]
            score = [[None] * 4 for _ in range(4)]
            for f in range(4):
                prob = [probs[h * 2 + other, f * 4 + g : f * 4 + g + 1] for g in range(4)]
                dprob = [
                    jnp.sum(grads[f] * read(h * 384 + 256, g, other), axis=0, keepdims=True)
                    for g in range(4)
                ]
                mean = sum(d * p for d, p in zip(dprob, prob))
                for g in range(4):
                    score[f][g] = prob[g] * (dprob[g] - mean) * INV_ROOT
            for g in range(4):
                value = sum(
                    probs[h * 2 + other, f * 4 + g : f * 4 + g + 1].astype(bf16).astype(f32) * grads[f]
                    for f in range(4)
                )
                query = sum(score[g][i] * read(h * 384 + 128, i, other) for i in range(4))
                key = sum(score[f][g] * read(h * 384, f, other) for f in range(4))
                for j, out in enumerate((query, key, value)):
                    row = h * 384 + j * 128
                    delta[row : row + 128, lanes(g, other)] = out.astype(bf16)
    for h in range(2):
        factor = dot(slope[...], attended[h * 128 : h * 128 + 128].astype(f32), NT, HIGHEST)
        factor = factor.astype(bf16)
        own_factor[h] = factor
        ahead, behind = pieces[2 * h : 2 * h + 2]
        piece = gradient_piece(delta, normed_a, normed_b, h, (place[h] + 2) % 4)
        ahead[...] = piece[:SPLIT]
        behind[: 384 - SPLIT] = piece[SPLIT:]
        for i in range(4):
            behind[384 - SPLIT :, i * 128 : i * 128 + 128] = factor[i * 16 : i * 16 + 16]


def near_kernel(place, delta, normed_a, normed_b, own_factor, *outs):
    for h in range(2):
        for k, o in enumerate((0, 1, 3)):
            out = outs[h * 3 + k]
            out[:384] = gradient_piece(delta, normed_a, normed_b, h, (place[h] + o) % 4)
            for i in range(4):
                out[384:, i * 128 : i * 128 + 128] = own_factor[h, i * 16 : i * 16 + 16]


def relay_kernel(*refs):
    for h in range(2):
        following, previous, ahead, behind = refs[4 * h : 4 * h + 4]
        out_following, out_previous = refs[8 + 2 * h : 10 + 2 * h]
        out_following[SPLIT:] = following[SPLIT:]
        out_following[:SPLIT] = (following[:SPLIT].astype(f32) + ahead[...].astype(f32)).astype(bf16)
        out_previous[:SPLIT] = previous[:SPLIT]
        out_previous[SPLIT:] = (previous[SPLIT:].astype(f32) + behind[...].astype(f32)).astype(bf16)


def add_first_kernel(place, *refs):
    both = refs[14]
    for h in range(2):
        parts, outs = refs[3 * h : 3 * h + 3], refs[6 + 4 * h : 10 + 4 * h]
        total = parts[0][...].astype(f32)
        for part in parts[1:]:
            total = total + part[...].astype(f32)
        both[...] = total.astype(bf16)
        for o, out in enumerate(outs):
            columns = pl.ds(pl.multiple_of(((place[1 - h] + o) % 4) * 128, 128), 128)
            out[:384] = both[:384, columns]
            for i in range(4):
                out[384 + i * 16 : 400 + i * 16] = both[384:, i * 128 : i * 128 + 128]


def add_second_kernel(*refs):
    factor = refs[10]
    for h in range(2):
        parts, owned = refs[4 * h : 4 * h + 4], refs[8 + h]
        total = parts[0][...].astype(f32)
        for part in parts[1:]:
            total = total + part[...].astype(f32)
        for j in range(3):
            owned[j] = total[j * 128 : j * 128 + 128].T.astype(bf16)
        factor[h * 128 : h * 128 + 128] = total[384:].T.astype(bf16)


def line_kernel(*refs):
    lines, both = refs[8:10], refs[10]
    for h in range(2):
        for o in range(4):
            piece = refs[4 * h + o][...]
            lines[h][o] = piece
            both[h, o] = piece


def pass_kernel(*refs):
    all_near = refs[8]
    for h in range(2):
        before, after = refs[2 * h : 2 * h + 2]
        refs[4 + 2 * h][...] = before[:2]
        refs[5 + 2 * h][...] = after[2:]
        all_near[h] = before[...]
        all_near[2 + h] = after[...]


def join_kernel(a, b, c, d, unused, out):
    for k, ref in enumerate((a, b, c, d)):
        out[k] = ref[...]


def assemble_kernel(tags, aliased, with_out, place, *refs):
    arrays = 1 + max(tag[0] for tag in tags)
    count = len(tags)
    sources, refs = refs[:arrays], refs[arrays + aliased :]
    if with_out:
        factors, head_t, out, grad_out, held, ready, done, sems, whole, sent = refs
    else:
        out, held, ready, done, sems = refs
    loads = []
    for k, tag in enumerate(tags):
        source = sources[tag[0]] if tag[1] is None else sources[tag[0]].at[tag[1]]
        loads.append(pltpu.make_async_copy(source, held.at[k], sems.at[k]))
        loads[-1].start()
    if with_out:
        whole[...] = dot(factors[...], head_t[...])
        leave = pltpu.make_async_copy(whole, grad_out, sent.at[0])
        leave.start()
    stores = [None, None]
    slot = 1
    for k, tag in enumerate(tags):
        o, theirs, h, inners = tag[2:]
        loads[k].wait()
        if k == 0 or tags[k - 1][2:5] != tag[2:5]:
            slot = 1 - slot
            if stores[slot] is not None:
                stores[slot].wait()
        first = (place[h] + 4 - o) % 4
        for i, inner in enumerate(inners):
            second = (place[1 - h] + 4 - inner) % 4
            ready[slot, :, pl.ds(pl.multiple_of(second * 128, 128), 128)] = held[k, i].astype(f32)
        if k + 1 < count and tags[k + 1][2:5] == tag[2:5]:
            continue
        core = place[2] if theirs == 0 else 1 - place[2]
        stores[slot] = pltpu.make_async_copy(
            ready.at[slot],
            out.at[
                :,
                pl.ds(pl.multiple_of(first * 512, 512), 512),
                pl.ds(pl.multiple_of(core * 256 + h * 128, 128), 128),
            ],
            done.at[slot],
        )
        stores[slot].start()
    for store in stores:
        store.wait()
    if with_out:
        leave.wait()


def assemble(place, arrays, tags, onto=None, product=()):
    tags = tuple(sorted(tags, key=lambda t: t[2:]))
    anywhere = pl.BlockSpec(memory_space=pl.ANY)
    given = [] if onto is None else [onto]
    out_shape = [shape((3, 2048, 512), f32)]
    scratch = [
        pltpu.VMEM((len(tags), *arrays[0].shape[-4:]), bf16),
        pltpu.VMEM((2, 3, 512, 128), f32),
        pltpu.SemaphoreType.DMA((2,)),
        pltpu.SemaphoreType.DMA((len(tags),)),
    ]
    if product:
        out_shape.append(shape((512, 2048), f32))
        scratch += [pltpu.VMEM((512, 2048), f32), pltpu.SemaphoreType.DMA((1,))]
    return pl.pallas_call(
        functools.partial(assemble_kernel, tags, len(given), bool(product)),
        in_specs=[SMEM] + [anywhere] * (len(arrays) + len(given)) + [VMEM] * len(product),
        out_specs=[anywhere] * len(out_shape),
        out_shape=out_shape,
        scratch_shapes=scratch,
        input_output_aliases={1 + len(arrays): 0} if given else {},
        compiler_params=params(12),
        cost_estimate=TINY,
    )(place, *arrays, *given, *product)


def shards(act, cache_rows, row_dest, time_index, w_embed, norm_gain, w_qkv, w_out, w_head):
    x, y, core, frame = (lax.axis_index(a).astype(jnp.int32) for a in ("x", "y", "core", "frame"))
    here = jnp.stack([frame, core])
    square = jnp.stack([x, y, core])

    before, after = shift(act, "frame", 1), shift(act, "frame", 3)
    act_theirs = shift(act, "core", 1)

    sent = pl.pallas_call(
        bucket_kernel,
        in_specs=[VMEM] * 2,
        out_specs=VMEM,
        out_shape=shape((4, 16, 2, 16, 128), bf16),
    )(cache_rows, row_dest.reshape(1, 128))
    arrived = lax.all_to_all(
        sent.reshape(128, 16, 128), ("frame", "y", "x", "core"), 0, 0, tiled=True
    ).reshape(4, 512, 128)
    top, bottom, sides = pl.pallas_call(
        sides_kernel,
        in_specs=[VMEM] * 2 + [pl.BlockSpec(memory_space=pl.ANY)],
        out_specs=[VMEM] * 3,
        out_shape=[shape((64, 2048), bf16)] * 2 + [shape((2, 128, 2048), bf16)],
        cost_estimate=TINY,
    )(before, after, arrived)
    far_act = (shift(top, "frame", 1), shift(bottom, "frame", 3))
    sides_theirs = shift(sides, "core", 1)

    moment = (time_index.astype(f32) + 0.5) / TIMESTEPS
    moments = jnp.concatenate([moment, shift(moment, "core", 1)])

    head_t = w_head.T
    w_t, mix, mix_t = pl.pallas_call(
        prepare_kernel,
        grid_spec=pltpu.PrefetchScalarGridSpec(
            num_scalar_prefetch=1,
            grid=(3,),
            in_specs=[
                pl.BlockSpec((1, 2048, 256), lambda j, p: (j, 0, p[1])),
                pl.BlockSpec((256, 2048), lambda j, p: (p[1], 0)),
                pl.BlockSpec((64, 2048), lambda j, p: (0, 0)),
            ],
            out_specs=[
                pl.BlockSpec((2, 1, 128, 2048), lambda j, p: (0, j, 0, 0)),
                pl.BlockSpec((256, 64), lambda j, p: (0, 0)),
                pl.BlockSpec((64, 256), lambda j, p: (0, 0)),
            ],
        ),
        out_shape=[shape((2, 3, 128, 2048), bf16), shape((256, 64), f32), shape((64, 256), f32)],
        compiler_params=params(12),
        cost_estimate=TINY,
    )(here, w_qkv, w_out, head_t)
    w_t = w_t.reshape(768, 2048)

    pairs = pl.pallas_call(
        fetch_kernel,
        in_specs=[SMEM, VMEM],
        out_specs=VMEM,
        out_shape=shape((8, 128, 128), bf16),
        compiler_params=params(6),
        cost_estimate=TINY,
    )(here, arrived)

    def embed(first, arrays, picks):
        count = len(picks)
        out = [shape((count * 128, 2048), bf16), shape((768, count * 128), bf16)]
        if first == 0:
            out.append(shape((64, 128), f32))
        return pl.pallas_call(
            functools.partial(embed_kernel, first, len(arrays), picks),
            in_specs=[SMEM] + [VMEM] * (len(arrays) + 5),
            out_specs=[VMEM] * len(out),
            out_shape=out,
            compiler_params=params(10),
            cost_estimate=TINY,
        )(moments, *arrays, pairs, w_embed, norm_gain.reshape(1, 2048), w_t, head_t)

    normed_a, proj_a, rest = embed(
        0,
        (act, act_theirs, sides, sides_theirs),
        ((0, None), (1, None), (2, 0), (3, 0), (2, 1), (3, 1)),
    )
    far_own = pl.pallas_call(
        act_kernel,
        in_specs=[VMEM] * 2 + [pl.BlockSpec(memory_space=pl.ANY)],
        out_specs=VMEM,
        out_shape=shape((128, 2048), bf16),
        cost_estimate=TINY,
    )(*far_act, rest)
    normed_b, proj_b = embed(6, (far_own, shift(far_own, "core", 1)), ((0, None), (1, None)))
    attended, probs, part_own, part_other = pl.pallas_call(
        attend_kernel,
        in_specs=[VMEM] * 4,
        out_specs=[VMEM] * 4,
        out_shape=[
            shape((256, 1024), bf16),
            shape((4, 16, 128), f32),
            shape((64, 512), f32),
            shape((64, 512), f32),
        ],
        compiler_params=params(6),
        cost_estimate=TINY,
    )(proj_a, proj_b, mix_t, rest)

    clip_part = part_own + shift(part_other, "core", 1)
    heard = {0: clip_part, **{o: shift(clip_part, "frame", o) for o in (1, 3, 2)}}
    error_own = jnp.concatenate(
        [
            sum(
                heard[o][:, SPOT[(r - o) % 4] * 128 : SPOT[(r - o) % 4] * 128 + 128]
                for o in range(4)
            )
            for r in ORDER
        ],
        axis=1,
    )
    frame_loss = jnp.mean(error_own[:, :128] * error_own[:, :128]).reshape(1, 1)
    error_other = shift(error_own, "core", 1)

    def call(kernel, out_shape, *operands, scalars=(), scratch=(), mib=8, unused=()):
        return pl.pallas_call(
            kernel,
            in_specs=[SMEM] * len(scalars)
            + [VMEM] * len(operands)
            + [pl.BlockSpec(memory_space=pl.ANY)] * len(unused),
            out_specs=[VMEM] * len(out_shape),
            out_shape=out_shape,
            scratch_shapes=list(scratch),
            compiler_params=params(mib),
            cost_estimate=TINY,
        )(*scalars, *operands, *unused)

    piece = shape((400, 512), bf16)
    small = shape((448, 128), bf16)
    block = shape((3, 128, 128), bf16)
    line = shape((4, 3, 128, 128), bf16)
    part = shape((2, 3, 128, 128), bf16)
    *opposite, delta, own_factor = call(
        backward_kernel,
        [shape((SPLIT, 512), bf16), shape((400 - SPLIT, 512), bf16)] * 2
        + [shape((768, 1024), bf16), shape((2, 64, 128), bf16)],
        error_own, error_other, proj_a, proj_b, normed_a, normed_b, probs, attended, mix,
        scalars=(square,),
        scratch=[pltpu.VMEM((64, 1024), f32), pltpu.VMEM((256, 1024), f32)],
        mib=10,
    )
    axes = (("x", "y"), ("y", "x"))

    def around(pairs, k):
        return [
            (shift(pairs[h][0], axes[h][k], 1), shift(pairs[h][1], axes[h][k], 3)) for h in range(2)
        ]

    passed = around([opposite[:2], opposite[2:]], 0)
    near = call(near_kernel, [piece] * 6, delta, normed_a, normed_b, own_factor, scalars=(square,))
    relayed = call(
        relay_kernel,
        [piece] * 4,
        *(a for h in range(2) for a in (near[h * 3 + 1], near[h * 3 + 2], *passed[h])),
    )
    moved = around([relayed[:2], relayed[2:]], 0)
    second = call(
        add_first_kernel,
        [small] * 8,
        *(a for h in range(2) for a in (near[h * 3], *moved[h])),
        scalars=(square,),
        scratch=[pltpu.VMEM((400, 512), bf16)],
    )
    moved = [
        [shift(second[h * 4 + o], axes[h][1], o) for o in (1, 3, 2)] for h in range(2)
    ]
    *owned, factor = call(
        add_second_kernel,
        [block] * 2 + [shape((256, 64), bf16)],
        *(a for h in range(2) for a in (second[h * 4], *moved[h])),
    )
    back = [{0: owned[h], **{o: shift(owned[h], axes[h][1], o) for o in (1, 3, 2)}} for h in range(2)]
    factor_theirs = shift(factor, "core", 1)
    factors = jnp.concatenate(
        [jnp.where(core == 0, factor, factor_theirs), jnp.where(core == 0, factor_theirs, factor)]
    )
    line_x, line_y, lines = call(
        line_kernel, [line] * 2 + [shape((2, 4, 3, 128, 128), bf16)],
        *(back[h][o] for h in range(2) for o in range(4)),
    )
    every, low, high = (0, 1, 2, 3), (0, 1), (2, 3)
    beside = around([(line_x, line_x), (line_y, line_y)], 0)
    lines_theirs = shift(lines, "core", 1)
    grad_qkv, grad_out = assemble(
        square, (lines, lines_theirs), [(c, h, 0, c, h, every) for c in range(2) for h in range(2)],
        None, (factors, head_t),
    )
    *onward, all_near = call(
        pass_kernel, [part] * 4 + [shape((4, 4, 3, 128, 128), bf16)], *beside[0], *beside[1]
    )
    far = around([onward[:2], onward[2:]], 0)
    near_theirs = shift(all_near, "core", 1)
    (grad_qkv,) = assemble(
        square, (all_near, near_theirs),
        [(c, k, (1, 1, 3, 3)[k], c, k % 2, every) for c in range(2) for k in range(4)],
        grad_qkv,
    )
    (all_far,) = call(
        join_kernel, [shape((4, 2, 3, 128, 128), bf16)], *far[0], *far[1], unused=(grad_qkv,)
    )
    far_theirs = shift(all_far, "core", 1)
    for c, array in enumerate((all_far, far_theirs)):
        (grad_qkv,) = assemble(
            square, (array,),
            [(0, k, 2, c, k // 2, (low, high)[k % 2]) for k in range(4)],
            grad_qkv,
        )
    return frame_loss, grad_qkv, grad_out


def solution(mesh):
    fine = Mesh(mesh.devices.reshape(4, 4, 2, 4), ("y", "x", "core", "frame"))
    store = ("y", "x", "core")
    in_specs = (
        P((*store, "frame"), None),
        P((*store, "frame"), None),
        P((*store, "frame")),
        P(store),
        P(),
        P(),
        P(None, None, "frame"),
        P("frame", None),
        P(),
    )
    out_specs = (P(store, "frame"), P(None, None, "frame"), P("frame", None))
    return jax.shard_map(shards, mesh=fine, in_specs=in_specs, out_specs=out_specs, check_vma=False)
```

```python
import functools
import math

import jax
import jax.numpy as jnp
from jax import lax
from jax.experimental import pallas as pl
from jax.experimental.pallas import tpu as pltpu
from jax.sharding import Mesh, PartitionSpec as P

HEAD_DIM = 128
TIMESTEPS = 1000
UNUSED = 64.0
FIRST = ((0, 1), (0, 3), (0, 2), (1, 3), (1, 2))
f32 = jnp.float32
bf16 = jnp.bfloat16
HIGHEST = lax.Precision.HIGHEST
INV_ROOT = 1.0 / math.sqrt(HEAD_DIM)
NN = (((1,), (0,)), ((), ()))
NT = (((1,), (1,)), ((), ()))
TN = (((0,), (0,)), ((), ()))
ORDER = (0, 1, 3, 2)
SPOT = {r: i for i, r in enumerate(ORDER)}
VMEM = pl.BlockSpec(memory_space=pltpu.VMEM)
SMEM = pl.BlockSpec(memory_space=pltpu.SMEM)
HBM = pl.BlockSpec(memory_space=pltpu.HBM)
ANY = pl.BlockSpec(memory_space=pl.ANY)


def params(mib):
    return pltpu.CompilerParams(vmem_limit_bytes=mib << 20)


def cost(flops, moved):
    return pl.CostEstimate(flops=flops, bytes_accessed=moved, transcendentals=0)


TINY = cost(0, 1024)


def dot(a, b, dims=NN, precision=None):
    return lax.dot_general(a, b, dims, preferred_element_type=f32, precision=precision)


def shift(value, axis, offset):
    size = lax.axis_size(axis)
    return lax.ppermute(value, axis, [(i, (i + offset) % size) for i in range(size)])


def shape(dims, kind):
    return jax.ShapeDtypeStruct(dims, kind)


def bucket_kernel(rows, dest_row, out):
    dest_col = jnp.broadcast_to(dest_row[...].astype(f32), (128, 128)).T
    earlier = lax.broadcasted_iota(jnp.int32, (128, 128), 0) < lax.broadcasted_iota(
        jnp.int32, (128, 128), 1
    )
    same = jnp.where((dest_col == dest_row[...].astype(f32)) & earlier, 1.0, 0.0)
    slot = dest_row[...] * 8 + jnp.sum(same, axis=0, keepdims=True).astype(jnp.int32)
    hot = jnp.where(lax.broadcasted_iota(jnp.int32, (256, 128), 0) == slot, 1.0, 0.0)
    used = jnp.max(hot, axis=1, keepdims=True)
    moved = dot(hot.astype(bf16), rows[...]) + (1.0 - used) * UNUSED
    out[...] = moved.astype(bf16).reshape(16, 16, 128)


def prepare_kernel(place, w, w_out, head_t, w_t, mix, mix_t, held, out_rows, turned, sems, leave):
    start = pl.multiple_of(place[1] * 256, 256)
    loads = [
        pltpu.make_async_copy(w.at[j, :, pl.ds(start, 256)], held.at[j], sems.at[j]) for j in range(3)
    ]
    loads.append(pltpu.make_async_copy(w_out.at[pl.ds(start, 256)], out_rows, sems.at[3]))
    for load in loads:
        load.start()
    stores = []
    for j in range(3):
        loads[j].wait()
        for h in range(2):
            k = h * 3 + j
            turned[k] = held[j, :, h * 128 : h * 128 + 128].T
            stores.append(pltpu.make_async_copy(turned.at[k], w_t.at[pl.ds(k * 128, 128)], leave.at[k]))
            stores[-1].start()
    loads[3].wait()
    mix[...] = dot(out_rows[...], head_t[...], NT)
    mix_t[...] = dot(head_t[...], out_rows[...], NT)
    for store in stores:
        store.wait()


def sides_kernel(before, after, arrived, top, bottom, both, spread):
    top[...] = before[:64]
    bottom[...] = after[64:]
    both[0] = before[...]
    both[1] = after[...]
    for k in range(8):
        spread[k] = arrived[...]


def fetch_kernel(place, arrived, pairs):
    frame, core = place[0], place[1]
    slots = 512

    def rank_of(i):
        return ((i % 256) // 16) * 32 + (i // 256) * 16 + i % 16

    before = jnp.where(
        rank_of(lax.broadcasted_iota(jnp.int32, (slots, slots), 1))
        < rank_of(lax.broadcasted_iota(jnp.int32, (slots, slots), 0)),
        1.0,
        0.0,
    ).astype(bf16)
    half = (lax.broadcasted_iota(jnp.int32, (slots, 128), 0) // 8) % 2
    lane = lax.broadcasted_iota(jnp.int32, (slots, 128), 1).astype(f32)
    for i, r in enumerate(ORDER):
        from_frame = (frame + 4 - r) % 4
        rows = jnp.concatenate([arrived[from_frame], arrived[4 + from_frame]], axis=0)
        valid = jnp.broadcast_to(rows[:, 0:1].astype(f32), (slots, 128)) < 32.0
        for other in range(2):
            clip = core + other - 2 * core * other
            mine = jnp.where(valid & (half == clip), 1.0, 0.0)
            rank = dot(before, mine.astype(bf16))
            pick = jnp.where(rank == lane, mine, 0.0)
            pairs[2 * i + other] = dot(pick.astype(bf16), rows, TN).astype(bf16)


def lanes(i, other):
    return slice((2 * i + other) * 128, (2 * i + other) * 128 + 128)


def forward_kernel(moments, *refs):
    act, act_theirs, sides, sides_theirs, top, top_theirs, bottom, bottom_theirs = refs[:8]
    pairs, w_embed, gain, w_t_far, head_t, mix_t = refs[8:14]
    normed_far, proj_far, attended_far, probs, part_own, part_other = refs[14:20]
    w_t, normed, proj, attended, rest, sems = refs[20:]
    weights = pltpu.make_async_copy(w_t_far, w_t, sems.at[0])
    weights.start()
    work = [(0, 0, act[...]), (1, 0, act_theirs[...])]
    for side in range(2):
        work += [(2 + 2 * side, 0, sides[side]), (3 + 2 * side, 0, sides_theirs[side])]
    work += [(6, 0, top[...]), (6, 64, bottom[...]), (7, 0, top_theirs[...]), (7, 64, bottom_theirs[...])]
    for b, start, rows in work:
        pair = pairs[b, start : start + rows.shape[0]].astype(f32)
        t = moments[b % 2]
        noised = ((1.0 - t) * pair[:, :64] + t * pair[:, 64:]).astype(bf16)
        hidden = rows.astype(f32) + dot(noised, w_embed[...])
        scale = lax.rsqrt(jnp.mean(hidden * hidden, axis=1, keepdims=True) + 1e-06)
        first = b * 128 + start
        normed[first : first + rows.shape[0]] = (hidden * scale * gain[...]).astype(bf16)
        if b == 0:
            turned = pair.T
            own = dot(head_t[...].astype(f32), hidden, NT, HIGHEST)
            rest[...] = own - (turned[64:] - turned[:64])
    leave = [pltpu.make_async_copy(normed, normed_far, sems.at[1])]
    leave[0].start()
    weights.wait()
    for i in range(3):
        rows = slice(i * 256, i * 256 + 256)
        proj[rows] = dot(w_t[rows], normed[...], NT).astype(bf16)
    leave.append(pltpu.make_async_copy(proj, proj_far, sems.at[2]))
    leave[1].start()
    for h in range(2):
        for other in range(2):

            def read(j, f):
                row = h * 384 + j * 128
                return proj[row : row + 128, lanes(f, other)].astype(f32)

            keys = [read(1, g) for g in range(4)]
            values = [read(2, g) for g in range(4)]
            for f in range(4):
                query = read(0, f)
                scores = [jnp.sum(query * k, axis=0, keepdims=True) * INV_ROOT for k in keys]
                peak = jnp.maximum(jnp.maximum(scores[0], scores[1]), jnp.maximum(scores[2], scores[3]))
                powers = [jnp.exp(s - peak) for s in scores]
                whole = powers[0] + powers[1] + powers[2] + powers[3]
                prob = [p / whole for p in powers]
                rounded = [p.astype(bf16).astype(f32) for p in prob]
                out = rounded[0] * values[0]
                for g in range(1, 4):
                    out = out + rounded[g] * values[g]
                attended[h * 128 : h * 128 + 128, lanes(f, other)] = out.astype(bf16)
                for g in range(4):
                    probs[h * 2 + other, f * 4 + g : f * 4 + g + 1] = prob[g]
    leave.append(pltpu.make_async_copy(attended, attended_far, sems.at[3]))
    leave[2].start()
    for other, part in ((0, part_own), (1, part_other)):
        for f in range(4):
            value = dot(mix_t[...], attended[:, lanes(f, other)].astype(f32), NN, HIGHEST)
            if other == 0 and f == 0:
                value = value + rest[...]
            part[:, f * 128 : f * 128 + 128] = value
    for copy in leave:
        copy.wait()


def gradient_piece(delta, normed, factor, h, block, out):
    columns = pl.ds(pl.multiple_of(block * 512, 512), 512)
    out[:384] = dot(delta[h * 384 : h * 384 + 384], normed[:, columns]).astype(bf16)
    for i in range(4):
        out[384:, i * 128 : i * 128 + 128] = factor[i * 16 : i * 16 + 16]


def backward_kernel(place, error_own, error_other, probs, mix, proj_far, attended_far, normed_far, *refs):
    pieces, delta, own_factor = refs[:5], refs[5], refs[6]
    slope, grad, proj, attended, normed, sems = refs[7:]
    loads = [
        pltpu.make_async_copy(far, near, sems.at[k])
        for k, (far, near) in enumerate(((proj_far, proj), (attended_far, attended), (normed_far, normed)))
    ]
    for load in loads:
        load.start()
    for i in range(4):
        for other, error in ((0, error_own), (1, error_other)):
            slope[:, lanes(i, other)] = error[:, i * 128 : i * 128 + 128] * (2.0 / 32.0)
    grad[...] = dot(mix[...], slope[...], NN, HIGHEST)
    loads[0].wait()
    for h in range(2):
        for other in range(2):

            def read(j, f):
                row = h * 384 + j * 128
                return proj[row : row + 128, lanes(f, other)].astype(f32)

            def prob(f, g):
                return probs[h * 2 + other, f * 4 + g : f * 4 + g + 1]

            grads = [grad[h * 128 : h * 128 + 128, lanes(f, other)] for f in range(4)]
            score = [[None] * 4 for _ in range(4)]
            for f in range(4):
                dprob = [jnp.sum(grads[f] * read(2, g), axis=0, keepdims=True) for g in range(4)]
                mean = sum(dprob[g] * prob(f, g) for g in range(4))
                for g in range(4):
                    score[f][g] = prob(f, g) * (dprob[g] - mean) * INV_ROOT
            for g in range(4):
                value = sum(prob(f, g).astype(bf16).astype(f32) * grads[f] for f in range(4))
                query = sum(score[g][i] * read(1, i) for i in range(4))
                key = sum(score[f][g] * read(0, f) for f in range(4))
                for j, out in enumerate((query, key, value)):
                    row = h * 384 + j * 128
                    delta[row : row + 128, lanes(g, other)] = out.astype(bf16)
    loads[1].wait()
    for h in range(2):
        factor = dot(slope[...], attended[h * 128 : h * 128 + 128].astype(f32), NT, HIGHEST)
        own_factor[h] = factor.astype(bf16)
    loads[2].wait()
    for (h, o), out in zip(FIRST, pieces):
        gradient_piece(delta, normed, own_factor[h], h, (place[h] + o) % 4, out)


def late_kernel(place, delta, own_factor, normed_far, own_x, own_y, last, normed, sems):
    load = pltpu.make_async_copy(normed_far, normed, sems.at[0])
    load.start()
    load.wait()
    for (h, o), out in (((1, 1), last), ((0, 0), own_x), ((1, 0), own_y)):
        gradient_piece(delta, normed, own_factor[h], h, (place[h] + o) % 4, out)


def add_first_kernel(place, *refs):
    both = refs[16]
    for h in range(2):
        parts, outs = refs[4 * h : 4 * h + 4], refs[8 + 4 * h : 12 + 4 * h]
        total = parts[0][...].astype(f32)
        for part in parts[1:]:
            total = total + part[...].astype(f32)
        both[...] = total.astype(bf16)
        for o, out in enumerate(outs):
            columns = pl.ds(pl.multiple_of(((place[1 - h] + o) % 4) * 128, 128), 128)
            out[:384] = both[:384, columns]
            for i in range(4):
                out[384 + i * 16 : 400 + i * 16] = both[384:, i * 128 : i * 128 + 128]


def add_second_kernel(*refs):
    factor = refs[10]
    for h in range(2):
        parts, owned = refs[4 * h : 4 * h + 4], refs[8 + h]
        total = parts[0][...].astype(f32)
        for part in parts[1:]:
            total = total + part[...].astype(f32)
        for j in range(3):
            owned[j] = total[j * 128 : j * 128 + 128].T.astype(bf16)
        factor[h * 128 : h * 128 + 128] = total[384:].T.astype(bf16)


def line_kernel(*refs):
    lines, both = refs[8:10], refs[10]
    for h in range(2):
        for o in range(4):
            piece = refs[4 * h + o][...]
            lines[h][o] = piece
            both[h, o] = piece


def join_kernel(a, b, c, out):
    for k, ref in enumerate((a, b, c)):
        out[k] = ref[...]


def assemble_kernel(tags, aliased, with_out, place, *refs):
    arrays = 1 + max(tag[0] for tag in tags)
    count = len(tags)
    sources, refs = refs[:arrays], refs[arrays + aliased :]
    if with_out:
        factors, head_t, line, out, grad_out, line_out, held, ready, done, sems, whole, sent = refs
        line_out[...] = line[...]
    else:
        out, held, ready, done, sems = refs
    loads = []
    for k, tag in enumerate(tags):
        source = sources[tag[0]] if tag[1] is None else sources[tag[0]].at[tag[1]]
        loads.append(pltpu.make_async_copy(source, held.at[k], sems.at[k]))
        loads[-1].start()
    if with_out:
        whole[...] = dot(factors[...], head_t[...])
        leave = pltpu.make_async_copy(whole, grad_out, sent.at[0])
        leave.start()
    stores = [None, None]
    slot = 1
    for k, tag in enumerate(tags):
        o, theirs, h, inners = tag[2:]
        loads[k].wait()
        if k == 0 or tags[k - 1][2:5] != tag[2:5]:
            slot = 1 - slot
            if stores[slot] is not None:
                stores[slot].wait()
        first = (place[h] + 4 - o) % 4
        for i, inner in enumerate(inners):
            second = (place[1 - h] + 4 - inner) % 4
            ready[slot, :, pl.ds(pl.multiple_of(second * 128, 128), 128)] = held[k, i].astype(f32)
        if k + 1 < count and tags[k + 1][2:5] == tag[2:5]:
            continue
        core = place[2] if theirs == 0 else 1 - place[2]
        stores[slot] = pltpu.make_async_copy(
            ready.at[slot],
            out.at[
                :,
                pl.ds(pl.multiple_of(first * 512, 512), 512),
                pl.ds(pl.multiple_of(core * 256 + h * 128, 128), 128),
            ],
            done.at[slot],
        )
        stores[slot].start()
    for store in stores:
        store.wait()
    if with_out:
        leave.wait()


def assemble(place, arrays, tags, onto=None, product=()):
    tags = tuple(sorted(tags, key=lambda t: t[2:]))
    given = [] if onto is None else [onto]
    out_shape = [shape((3, 2048, 512), f32)]
    out_specs = [HBM]
    scratch = [
        pltpu.VMEM((len(tags), *arrays[0].shape[-4:]), bf16),
        pltpu.VMEM((2, 3, 512, 128), f32),
        pltpu.SemaphoreType.DMA((2,)),
        pltpu.SemaphoreType.DMA((len(tags),)),
    ]
    if product:
        out_shape += [shape((512, 2048), f32), shape((4, 3, 128, 128), bf16)]
        out_specs += [HBM, VMEM]
        scratch += [pltpu.VMEM((512, 2048), f32), pltpu.SemaphoreType.DMA((1,))]
    return pl.pallas_call(
        functools.partial(assemble_kernel, tags, len(given), bool(product)),
        in_specs=[SMEM] + [ANY] * len(arrays) + [HBM] * len(given) + [VMEM] * len(product),
        out_specs=out_specs,
        out_shape=out_shape,
        scratch_shapes=scratch,
        input_output_aliases={1 + len(arrays): 0} if given else {},
        compiler_params=params(12),
        cost_estimate=TINY,
    )(place, *arrays, *given, *product)


def call(kernel, out, *operands, scratch=(), mib=8):
    result = pl.pallas_call(
        kernel,
        in_specs=[spec for spec, _ in operands],
        out_specs=[spec for spec, _ in out],
        out_shape=[made for _, made in out],
        scratch_shapes=list(scratch),
        compiler_params=params(mib),
        cost_estimate=TINY,
    )(*(array for _, array in operands))
    return result


def near(*arrays):
    return [(VMEM, a) for a in arrays]


def far(*arrays):
    return [(HBM, a) for a in arrays]


def shards(act, cache_rows, row_dest, time_index, w_embed, norm_gain, w_qkv, w_out, w_head):
    x, y, core, frame = (lax.axis_index(a).astype(jnp.int32) for a in ("x", "y", "core", "frame"))
    here = (SMEM, jnp.stack([frame, core]))
    square = (SMEM, jnp.stack([x, y, core]))
    dma = pltpu.SemaphoreType.DMA

    before, after = shift(act, "frame", 1), shift(act, "frame", 3)
    act_theirs = shift(act, "core", 1)
    (sent,) = call(
        bucket_kernel, near(shape((16, 16, 128), bf16)), *near(cache_rows, row_dest.reshape(1, 128))
    )
    arrived = lax.all_to_all(sent, ("y", "x"), 0, 0, tiled=True).reshape(256, 128)
    half_act = shape((64, 2048), bf16)
    top, bottom, sides, spread = call(
        sides_kernel,
        near(half_act, half_act, shape((2, 128, 2048), bf16), shape((8, 256, 128), bf16)),
        *near(before, after, arrived),
    )
    top, bottom = shift(top, "frame", 1), shift(bottom, "frame", 3)
    sides_theirs = shift(sides, "core", 1)
    arrived = lax.all_to_all(spread, ("core", "frame"), 0, 0, tiled=True)
    moment = (time_index.astype(f32) + 0.5) / TIMESTEPS
    moments = jnp.concatenate([moment, shift(moment, "core", 1)])

    head_t = w_head.T
    w_t, mix, mix_t = call(
        prepare_kernel,
        far(shape((768, 2048), bf16)) + near(shape((256, 64), f32), shape((64, 256), f32)),
        here, *far(w_qkv, w_out), *near(head_t),
        scratch=[
            pltpu.VMEM((3, 2048, 256), bf16),
            pltpu.VMEM((256, 2048), bf16),
            pltpu.VMEM((6, 128, 2048), bf16),
            dma((4,)),
            dma((6,)),
        ],
        mib=12,
    )
    (pairs,) = call(fetch_kernel, near(shape((8, 128, 128), bf16)), here, *near(arrived))
    normed, proj, attended, probs, part_own, part_other = call(
        forward_kernel,
        far(shape((1024, 2048), bf16), shape((768, 1024), bf16), shape((256, 1024), bf16))
        + near(shape((4, 16, 128), f32), shape((64, 512), f32), shape((64, 512), f32)),
        (SMEM, moments),
        *near(act, act_theirs, sides, sides_theirs, top, shift(top, "core", 1), bottom, shift(bottom, "core", 1)),
        *near(pairs, w_embed, norm_gain.reshape(1, 2048)), *far(w_t), *near(head_t, mix_t),
        scratch=[
            pltpu.VMEM((768, 2048), bf16),
            pltpu.VMEM((1024, 2048), bf16),
            pltpu.VMEM((768, 1024), bf16),
            pltpu.VMEM((256, 1024), bf16),
            pltpu.VMEM((64, 128), f32),
            dma((4,)),
        ],
        mib=16,
    )

    clip_part = part_own + shift(part_other, "core", 1)
    heard = {0: clip_part, **{o: shift(clip_part, "frame", o) for o in (1, 3, 2)}}
    error_own = jnp.concatenate(
        [
            sum(
                heard[o][:, SPOT[(r - o) % 4] * 128 : SPOT[(r - o) % 4] * 128 + 128]
                for o in range(4)
            )
            for r in ORDER
        ],
        axis=1,
    )
    frame_loss = jnp.mean(error_own[:, :128] * error_own[:, :128]).reshape(1, 1)
    error_other = shift(error_own, "core", 1)

    piece = shape((400, 512), bf16)
    small = shape((448, 128), bf16)
    block = shape((3, 128, 128), bf16)
    line = shape((4, 3, 128, 128), bf16)
    axes = (("x", "y"), ("y", "x"))
    *first, delta, own_factor = call(
        backward_kernel,
        near(*[piece] * 5, shape((768, 1024), bf16), shape((2, 64, 128), bf16)),
        square, *near(error_own, error_other, probs, mix), *far(proj, attended, normed),
        scratch=[
            pltpu.VMEM((64, 1024), f32),
            pltpu.VMEM((256, 1024), f32),
            pltpu.VMEM((768, 1024), bf16),
            pltpu.VMEM((256, 1024), bf16),
            pltpu.VMEM((1024, 2048), bf16),
            dma((3,)),
        ],
        mib=16,
    )
    moved = [[], []]
    for (h, o), p in zip(FIRST, first):
        moved[h].append(shift(p, axes[h][0], o))
    own_x, own_y, last = call(
        late_kernel, near(*[piece] * 3), square, *near(delta, own_factor), *far(normed),
        scratch=[pltpu.VMEM((1024, 2048), bf16), dma((1,))],
    )
    moved[1].append(shift(last, axes[1][0], 1))
    second = call(
        add_first_kernel, near(*[small] * 8), square, *near(own_x, *moved[0], own_y, *moved[1]),
        scratch=[pltpu.VMEM((400, 512), bf16)],
    )
    moved = [[shift(second[h * 4 + o], axes[h][1], o) for o in (1, 3, 2)] for h in range(2)]
    *owned, factor = call(
        add_second_kernel, near(block, block, shape((256, 64), bf16)),
        *near(second[0], *moved[0], second[4], *moved[1]),
    )
    back = [
        {0: owned[h], **{o: shift(owned[h], axes[h][1], o) for o in (1, 3, 2)}} for h in range(2)
    ]
    factor_theirs = shift(factor, "core", 1)
    factors = jnp.concatenate(
        [jnp.where(core == 0, factor, factor_theirs), jnp.where(core == 0, factor_theirs, factor)]
    )
    line_x, line_y, lines = call(
        line_kernel, near(line, line, shape((2, 4, 3, 128, 128), bf16)),
        *near(*(back[h][o] for h in range(2) for o in range(4))),
    )
    every = (0, 1, 2, 3)
    wide = {(h, o): shift((line_x, line_y)[h], axes[h][0], o) for h, o in FIRST}
    grad_qkv, grad_out, line_last = assemble(
        square[1], (lines,), [(0, h, 0, 0, h, every) for h in range(2)], None, (factors, head_t, line_y)
    )
    wide[1, 1] = shift(line_last, axes[1][0], 1)
    lines_theirs = shift(lines, "core", 1)
    reach = (1, 3, 2)
    triple = near(shape((3, 4, 3, 128, 128), bf16))
    (wide_x,) = call(join_kernel, triple, *near(*(wide[0, o] for o in reach)))
    wide_x_theirs = shift(wide_x, "core", 1)
    (wide_y,) = call(join_kernel, triple, *near(*(wide[1, o] for o in reach)))
    wide_y_theirs = shift(wide_y, "core", 1)

    def placed(array, side, h):
        return [(array, k, reach[k], side, h, every) for k in range(3)]

    (grad_qkv,) = assemble(
        square[1], (lines_theirs,), [(0, h, 0, 1, h, every) for h in range(2)], grad_qkv
    )
    (grad_qkv,) = assemble(
        square[1], (wide_x, wide_x_theirs), placed(0, 0, 0) + placed(1, 1, 0), grad_qkv
    )
    (grad_qkv,) = assemble(square[1], (wide_y,), placed(0, 0, 1), grad_qkv)
    (grad_qkv,) = assemble(square[1], (wide_y_theirs,), placed(0, 1, 1), grad_qkv)
    return frame_loss, grad_qkv, grad_out


def solution(mesh):
    fine = Mesh(mesh.devices.reshape(4, 4, 2, 4), ("y", "x", "core", "frame"))
    store = ("y", "x", "core")
    in_specs = (
        P((*store, "frame"), None),
        P((*store, "frame"), None),
        P((*store, "frame")),
        P(store),
        P(),
        P(),
        P(None, None, "frame"),
        P("frame", None),
        P(),
    )
    out_specs = (P(store, "frame"), P(None, None, "frame"), P("frame", None))
    return jax.shard_map(shards, mesh=fine, in_specs=in_specs, out_specs=out_specs, check_vma=False)
```

```python
import functools
import math

import jax
import jax.numpy as jnp
from jax import lax
from jax.experimental import pallas as pl
from jax.experimental.pallas import tpu as pltpu
from jax.sharding import Mesh, PartitionSpec as P

HEAD_DIM = 128
TIMESTEPS = 1000
UNUSED = 64.0
FIRST = ((0, 1), (0, 3), (1, 1), (1, 3))
f32 = jnp.float32
bf16 = jnp.bfloat16
HIGHEST = lax.Precision.HIGHEST
INV_ROOT = 1.0 / math.sqrt(HEAD_DIM)
NN = (((1,), (0,)), ((), ()))
NT = (((1,), (1,)), ((), ()))
TN = (((0,), (0,)), ((), ()))
ORDER = (0, 1, 3, 2)
SPOT = {r: i for i, r in enumerate(ORDER)}
VMEM = pl.BlockSpec(memory_space=pltpu.VMEM)
SMEM = pl.BlockSpec(memory_space=pltpu.SMEM)
HBM = pl.BlockSpec(memory_space=pltpu.HBM)
ANY = pl.BlockSpec(memory_space=pl.ANY)


LARGE = 52


def params(mib):
    return pltpu.CompilerParams(vmem_limit_bytes=mib << 20)


def cost(flops, moved):
    return pl.CostEstimate(flops=flops, bytes_accessed=moved, transcendentals=0)


TINY = cost(0, 1024)


def dot(a, b, dims=NN, precision=None):
    return lax.dot_general(a, b, dims, preferred_element_type=f32, precision=precision)


def shift(value, axis, offset):
    size = lax.axis_size(axis)
    return lax.ppermute(value, axis, [(i, (i + offset) % size) for i in range(size)])


def shape(dims, kind):
    return jax.ShapeDtypeStruct(dims, kind)


def bucket_kernel(rows, dest_row, out):
    dest_col = jnp.broadcast_to(dest_row[...].astype(f32), (128, 128)).T
    earlier = lax.broadcasted_iota(jnp.int32, (128, 128), 0) < lax.broadcasted_iota(
        jnp.int32, (128, 128), 1
    )
    same = jnp.where((dest_col == dest_row[...].astype(f32)) & earlier, 1.0, 0.0)
    slot = dest_row[...] * 8 + jnp.sum(same, axis=0, keepdims=True).astype(jnp.int32)
    hot = jnp.where(lax.broadcasted_iota(jnp.int32, (256, 128), 0) == slot, 1.0, 0.0)
    used = jnp.max(hot, axis=1, keepdims=True)
    moved = dot(hot.astype(bf16), rows[...]) + (1.0 - used) * UNUSED
    bucket = moved.astype(bf16).reshape(16, 16, 128)
    for frame in range(4):
        for core in range(2):
            out[frame, :, core] = bucket


def prepare_kernel(place, w, w_out, head_t, w_t, mix, mix_t, held, out_rows, turned, sems, leave):
    start = pl.multiple_of(place[1] * 256, 256)
    loads = [
        pltpu.make_async_copy(w.at[j, :, pl.ds(start, 256)], held.at[j], sems.at[j]) for j in range(3)
    ]
    loads.append(pltpu.make_async_copy(w_out.at[pl.ds(start, 256)], out_rows, sems.at[3]))
    for load in loads:
        load.start()
    stores = []
    for j in range(3):
        loads[j].wait()
        for h in range(2):
            k = h * 3 + j
            turned[k] = held[j, :, h * 128 : h * 128 + 128].T
            stores.append(pltpu.make_async_copy(turned.at[k], w_t.at[pl.ds(k * 128, 128)], leave.at[k]))
            stores[-1].start()
    loads[3].wait()
    mix[...] = dot(out_rows[...], head_t[...], NT)
    mix_t[...] = dot(head_t[...], out_rows[...], NT)
    for store in stores:
        store.wait()


def fetch_kernel(place, arrived, pairs):
    frame, core = place[0], place[1]
    slots = 512
    before = jnp.where(
        lax.broadcasted_iota(jnp.int32, (slots, slots), 1)
        < lax.broadcasted_iota(jnp.int32, (slots, slots), 0),
        1.0,
        0.0,
    ).astype(bf16)
    half = (lax.broadcasted_iota(jnp.int32, (slots, 128), 0) // 8) % 2
    lane = lax.broadcasted_iota(jnp.int32, (slots, 128), 1).astype(f32)
    for i, r in enumerate(ORDER):
        rows = arrived[(frame + 4 - r) % 4]
        valid = jnp.broadcast_to(rows[:, 0:1].astype(f32), (slots, 128)) < 32.0
        for other in range(2):
            clip = core + other - 2 * core * other
            mine = jnp.where(valid & (half == clip), 1.0, 0.0)
            rank = dot(before, mine.astype(bf16))
            pick = jnp.where(rank == lane, mine, 0.0)
            pairs[2 * i + other] = dot(pick.astype(bf16), rows, TN).astype(bf16)


def lanes(i, other):
    return slice((2 * i + other) * 128, (2 * i + other) * 128 + 128)


def forward_kernel(place, moments, act_far, *refs):
    pairs, w_embed, gain, w_t_far, head_t, mix_t = refs[:6]
    normed_far, proj_far, attended_far, probs, part_own, part_other = refs[6:12]
    act, w_t, normed, proj, attended, rest, sems, arrive = refs[12:]
    frame, core = place[0], place[1]
    loads = []
    for i, r in enumerate(ORDER):
        for other in range(2):
            clip = core + other - 2 * core * other
            start = pl.multiple_of((clip * 4 + (frame + 4 - r) % 4) * 128, 128)
            b = 2 * i + other
            loads.append(pltpu.make_async_copy(act_far.at[pl.ds(start, 128)], act.at[b], arrive.at[b]))
            loads[b].start()
    weights = pltpu.make_async_copy(w_t_far, w_t, sems.at[0])
    weights.start()
    for b in range(8):
        pair = pairs[b].astype(f32)
        t = moments[b % 2]
        noised = ((1.0 - t) * pair[:, :64] + t * pair[:, 64:]).astype(bf16)
        added = dot(noised, w_embed[...])
        loads[b].wait()
        hidden = act[b].astype(f32) + added
        scale = lax.rsqrt(jnp.mean(hidden * hidden, axis=1, keepdims=True) + 1e-06)
        normed[b * 128 : b * 128 + 128] = (hidden * scale * gain[...]).astype(bf16)
        if b == 0:
            turned = pair.T
            own = dot(head_t[...].astype(f32), hidden, NT, HIGHEST)
            rest[...] = own - (turned[64:] - turned[:64])
    leave = [pltpu.make_async_copy(normed, normed_far, sems.at[1])]
    leave[0].start()
    weights.wait()
    for i in range(3):
        rows = slice(i * 256, i * 256 + 256)
        proj[rows] = dot(w_t[rows], normed[...], NT).astype(bf16)
    leave.append(pltpu.make_async_copy(proj, proj_far, sems.at[2]))
    leave[1].start()
    for h in range(2):
        for other in range(2):

            def read(j, f):
                row = h * 384 + j * 128
                return proj[row : row + 128, lanes(f, other)].astype(f32)

            keys = [read(1, g) for g in range(4)]
            values = [read(2, g) for g in range(4)]
            for f in range(4):
                query = read(0, f)
                scores = [jnp.sum(query * k, axis=0, keepdims=True) * INV_ROOT for k in keys]
                peak = jnp.maximum(jnp.maximum(scores[0], scores[1]), jnp.maximum(scores[2], scores[3]))
                powers = [jnp.exp(s - peak) for s in scores]
                whole = powers[0] + powers[1] + powers[2] + powers[3]
                prob = [p / whole for p in powers]
                rounded = [p.astype(bf16).astype(f32) for p in prob]
                out = rounded[0] * values[0]
                for g in range(1, 4):
                    out = out + rounded[g] * values[g]
                attended[h * 128 : h * 128 + 128, lanes(f, other)] = out.astype(bf16)
                for g in range(4):
                    probs[h * 2 + other, f * 4 + g : f * 4 + g + 1] = prob[g]
    leave.append(pltpu.make_async_copy(attended, attended_far, sems.at[3]))
    leave[2].start()
    for other, part in ((0, part_own), (1, part_other)):
        for f in range(4):
            value = dot(mix_t[...], attended[:, lanes(f, other)].astype(f32), NN, HIGHEST)
            if other == 0 and f == 0:
                value = value + rest[...]
            part[:, f * 128 : f * 128 + 128] = value
    for copy in leave:
        copy.wait()


def gradient_piece(delta, normed, factor, h, block, out):
    columns = pl.ds(pl.multiple_of(block * 512, 512), 512)
    out[:384] = dot(delta[h * 384 : h * 384 + 384], normed[:, columns]).astype(bf16)
    for i in range(4):
        out[384:, i * 128 : i * 128 + 128] = factor[i * 16 : i * 16 + 16]


def backward_kernel(place, error_own, error_other, probs, mix, proj_far, attended_far, normed_far, *refs):
    pieces, delta, own_factor = refs[:4], refs[4], refs[5]
    slope, grad, proj, attended, normed, sems = refs[6:]
    loads = [
        pltpu.make_async_copy(far, near, sems.at[k])
        for k, (far, near) in enumerate(((proj_far, proj), (attended_far, attended), (normed_far, normed)))
    ]
    for load in loads:
        load.start()
    for i in range(4):
        for other, error in ((0, error_own), (1, error_other)):
            slope[:, lanes(i, other)] = error[:, i * 128 : i * 128 + 128] * (2.0 / 32.0)
    grad[...] = dot(mix[...], slope[...], NN, HIGHEST)
    loads[0].wait()
    for h in range(2):
        for other in range(2):

            def read(j, f):
                row = h * 384 + j * 128
                return proj[row : row + 128, lanes(f, other)].astype(f32)

            def prob(f, g):
                return probs[h * 2 + other, f * 4 + g : f * 4 + g + 1]

            grads = [grad[h * 128 : h * 128 + 128, lanes(f, other)] for f in range(4)]
            score = [[None] * 4 for _ in range(4)]
            for f in range(4):
                dprob = [jnp.sum(grads[f] * read(2, g), axis=0, keepdims=True) for g in range(4)]
                mean = sum(dprob[g] * prob(f, g) for g in range(4))
                for g in range(4):
                    score[f][g] = prob(f, g) * (dprob[g] - mean) * INV_ROOT
            for g in range(4):
                value = sum(prob(f, g).astype(bf16).astype(f32) * grads[f] for f in range(4))
                query = sum(score[g][i] * read(1, i) for i in range(4))
                key = sum(score[f][g] * read(0, f) for f in range(4))
                for j, out in enumerate((query, key, value)):
                    row = h * 384 + j * 128
                    delta[row : row + 128, lanes(g, other)] = out.astype(bf16)
    loads[1].wait()
    for h in range(2):
        factor = dot(slope[...], attended[h * 128 : h * 128 + 128].astype(f32), NT, HIGHEST)
        own_factor[h] = factor.astype(bf16)
    loads[2].wait()
    for (h, o), out in zip(FIRST, pieces):
        gradient_piece(delta, normed, own_factor[h], h, (place[h] + o) % 4, out)


def late_kernel(place, delta, own_factor, normed_far, far_x, far_y, own_x, own_y, normed, sems):
    load = pltpu.make_async_copy(normed_far, normed, sems.at[0])
    load.start()
    load.wait()
    for (h, o), out in (((0, 2), far_x), ((1, 2), far_y), ((0, 0), own_x), ((1, 0), own_y)):
        gradient_piece(delta, normed, own_factor[h], h, (place[h] + o) % 4, out)


def add_first_kernel(place, *refs):
    both = refs[16]
    for h in range(2):
        parts, outs = refs[4 * h : 4 * h + 4], refs[8 + 4 * h : 12 + 4 * h]
        total = parts[0][...].astype(f32)
        for part in parts[1:]:
            total = total + part[...].astype(f32)
        both[...] = total.astype(bf16)
        for o, out in enumerate(outs):
            columns = pl.ds(pl.multiple_of(((place[1 - h] + o) % 4) * 128, 128), 128)
            out[:384] = both[:384, columns]
            for i in range(4):
                out[384 + i * 16 : 400 + i * 16] = both[384:, i * 128 : i * 128 + 128]


def add_second_kernel(*refs):
    factor = refs[10]
    for h in range(2):
        parts, owned = refs[4 * h : 4 * h + 4], refs[8 + h]
        total = parts[0][...].astype(f32)
        for part in parts[1:]:
            total = total + part[...].astype(f32)
        for j in range(3):
            owned[j] = total[j * 128 : j * 128 + 128].T.astype(bf16)
        factor[h * 128 : h * 128 + 128] = total[384:].T.astype(bf16)


def line_kernel(place, *refs):
    factor, factor_theirs, lines, both, factors = refs[8], refs[9], refs[10:12], refs[12], refs[13]
    for h in range(2):
        for o in range(4):
            piece = refs[4 * h + o][...]
            lines[h][o] = piece
            both[h, o] = piece
    start = pl.multiple_of(place[2] * 256, 256)
    factors[pl.ds(start, 256)] = factor[...]
    factors[pl.ds(256 - start, 256)] = factor_theirs[...]


def join_kernel(*refs):
    out = refs[-1]
    for k in range(out.shape[0]):
        out[k] = refs[k][...]


def assemble_kernel(tags, aliased, with_out, place, *refs):
    arrays = 1 + max(tag[0] for tag in tags)
    count = len(tags)
    sources, refs = refs[:arrays], refs[arrays + aliased :]
    if with_out:
        factors, head_t, line_x, line_y, out, grad_out, copy_x, copy_y, *refs = refs
        held, ready, done, sems, whole, sent = refs
        copy_x[...] = line_x[...]
        copy_y[...] = line_y[...]
    else:
        out, held, ready, done, sems = refs
    loads = []
    for k, tag in enumerate(tags):
        source = sources[tag[0]] if tag[1] is None else sources[tag[0]].at[tag[1]]
        loads.append(pltpu.make_async_copy(source, held.at[k], sems.at[k]))
        loads[-1].start()
    if with_out:
        whole[...] = dot(factors[...], head_t[...])
        leave = pltpu.make_async_copy(whole, grad_out, sent.at[0])
        leave.start()
    stores = [None, None]
    slot = 1
    for k, tag in enumerate(tags):
        o, theirs, h, inners = tag[2:]
        loads[k].wait()
        if k == 0 or tags[k - 1][2:5] != tag[2:5]:
            slot = 1 - slot
            if stores[slot] is not None:
                stores[slot].wait()
        first = (place[h] + 4 - o) % 4
        for i, inner in enumerate(inners):
            second = (place[1 - h] + 4 - inner) % 4
            ready[slot, :, pl.ds(pl.multiple_of(second * 128, 128), 128)] = held[k, i].astype(f32)
        if k + 1 < count and tags[k + 1][2:5] == tag[2:5]:
            continue
        core = place[2] if theirs == 0 else 1 - place[2]
        stores[slot] = pltpu.make_async_copy(
            ready.at[slot],
            out.at[
                :,
                pl.ds(pl.multiple_of(first * 512, 512), 512),
                pl.ds(pl.multiple_of(core * 256 + h * 128, 128), 128),
            ],
            done.at[slot],
        )
        stores[slot].start()
    for store in stores:
        store.wait()
    if with_out:
        leave.wait()


def assemble(place, arrays, tags, onto=None, product=()):
    tags = tuple(sorted(tags, key=lambda t: t[2:]))
    given = [] if onto is None else [onto]
    out_shape = [shape((3, 2048, 512), f32)]
    out_specs = [HBM]
    scratch = [
        pltpu.VMEM((len(tags), *arrays[0].shape[-4:]), bf16),
        pltpu.VMEM((2, 3, 512, 128), f32),
        pltpu.SemaphoreType.DMA((2,)),
        pltpu.SemaphoreType.DMA((len(tags),)),
    ]
    if product:
        out_shape += [shape((512, 2048), f32)] + [shape((4, 3, 128, 128), bf16)] * 2
        out_specs += [HBM, VMEM, VMEM]
        scratch += [pltpu.VMEM((512, 2048), f32), pltpu.SemaphoreType.DMA((1,))]
    return pl.pallas_call(
        functools.partial(assemble_kernel, tags, len(given), bool(product)),
        in_specs=[SMEM] + [ANY] * len(arrays) + [HBM] * len(given) + [VMEM] * len(product),
        out_specs=out_specs,
        out_shape=out_shape,
        scratch_shapes=scratch,
        input_output_aliases={1 + len(arrays): 0} if given else {},
        compiler_params=params(LARGE),
        cost_estimate=TINY,
    )(place, *arrays, *given, *product)


def call(kernel, out, *operands, scratch=(), mib=8):
    result = pl.pallas_call(
        kernel,
        in_specs=[spec for spec, _ in operands],
        out_specs=[spec for spec, _ in out],
        out_shape=[made for _, made in out],
        scratch_shapes=list(scratch),
        compiler_params=params(mib),
        cost_estimate=TINY,
    )(*(array for _, array in operands))
    return result


def near(*arrays):
    return [(VMEM, a) for a in arrays]


def far(*arrays):
    return [(HBM, a) for a in arrays]


def shards(act, cache_rows, row_dest, time_index, w_embed, norm_gain, w_qkv, w_out, w_head):
    x, y, core, frame = (lax.axis_index(a).astype(jnp.int32) for a in ("x", "y", "core", "frame"))
    here = (SMEM, jnp.stack([frame, core]))
    square = (SMEM, jnp.stack([x, y, core]))
    dma = pltpu.SemaphoreType.DMA

    act8 = lax.all_gather(act, ("core", "frame"), axis=0, tiled=True)
    (sent,) = call(
        bucket_kernel, near(shape((4, 16, 2, 16, 128), bf16)), *near(cache_rows, row_dest.reshape(1, 128))
    )
    arrived = lax.all_to_all(
        sent.reshape(128, 16, 128), ("frame", "y", "x", "core"), 0, 0, tiled=True
    ).reshape(4, 512, 128)
    moment = (time_index.astype(f32) + 0.5) / TIMESTEPS
    moments = jnp.concatenate([moment, shift(moment, "core", 1)])

    head_t = w_head.T
    w_t, mix, mix_t = call(
        prepare_kernel,
        far(shape((768, 2048), bf16)) + near(shape((256, 64), f32), shape((64, 256), f32)),
        here, *far(w_qkv, w_out), *near(head_t),
        scratch=[
            pltpu.VMEM((3, 2048, 256), bf16),
            pltpu.VMEM((256, 2048), bf16),
            pltpu.VMEM((6, 128, 2048), bf16),
            dma((4,)),
            dma((6,)),
        ],
        mib=LARGE,
    )
    (pairs,) = call(fetch_kernel, near(shape((8, 128, 128), bf16)), here, *near(arrived))
    normed, proj, attended, probs, part_own, part_other = call(
        forward_kernel,
        far(shape((1024, 2048), bf16), shape((768, 1024), bf16), shape((256, 1024), bf16))
        + near(shape((4, 16, 128), f32), shape((64, 512), f32), shape((64, 512), f32)),
        here, (SMEM, moments), *far(act8),
        *near(pairs, w_embed, norm_gain.reshape(1, 2048)), *far(w_t), *near(head_t, mix_t),
        scratch=[
            pltpu.VMEM((8, 128, 2048), bf16),
            pltpu.VMEM((768, 2048), bf16),
            pltpu.VMEM((1024, 2048), bf16),
            pltpu.VMEM((768, 1024), bf16),
            pltpu.VMEM((256, 1024), bf16),
            pltpu.VMEM((64, 128), f32),
            dma((4,)),
            dma((8,)),
        ],
        mib=LARGE,
    )

    clip_part = part_own + shift(part_other, "core", 1)
    heard = {0: clip_part, **{o: shift(clip_part, "frame", o) for o in (1, 3, 2)}}
    error_own = jnp.concatenate(
        [
            sum(
                heard[o][:, SPOT[(r - o) % 4] * 128 : SPOT[(r - o) % 4] * 128 + 128]
                for o in range(4)
            )
            for r in ORDER
        ],
        axis=1,
    )
    frame_loss = jnp.mean(error_own[:, :128] * error_own[:, :128]).reshape(1, 1)
    error_other = shift(error_own, "core", 1)

    piece = shape((400, 512), bf16)
    small = shape((448, 128), bf16)
    block = shape((3, 128, 128), bf16)
    line = shape((4, 3, 128, 128), bf16)
    axes = (("x", "y"), ("y", "x"))
    *first, delta, own_factor = call(
        backward_kernel,
        near(*[piece] * 4, shape((768, 1024), bf16), shape((2, 64, 128), bf16)),
        square, *near(error_own, error_other, probs, mix), *far(proj, attended, normed),
        scratch=[
            pltpu.VMEM((64, 1024), f32),
            pltpu.VMEM((256, 1024), f32),
            pltpu.VMEM((768, 1024), bf16),
            pltpu.VMEM((256, 1024), bf16),
            pltpu.VMEM((1024, 2048), bf16),
            dma((3,)),
        ],
        mib=LARGE,
    )
    moved = [[], []]
    for (h, o), p in zip(FIRST, first):
        moved[h].append(shift(p, axes[h][0], o))
    far_x, far_y, own_x, own_y = call(
        late_kernel, near(*[piece] * 4), square, *near(delta, own_factor), *far(normed),
        scratch=[pltpu.VMEM((1024, 2048), bf16), dma((1,))],
        mib=LARGE,
    )
    moved[0].append(shift(far_x, axes[0][0], 2))
    moved[1].append(shift(far_y, axes[1][0], 2))
    second = call(
        add_first_kernel, near(*[small] * 8), square, *near(own_x, *moved[0], own_y, *moved[1]),
        scratch=[pltpu.VMEM((400, 512), bf16)],
    )
    moved = [[shift(second[h * 4 + o], axes[h][1], o) for o in (1, 3, 2)] for h in range(2)]
    *owned, factor = call(
        add_second_kernel, near(block, block, shape((256, 64), bf16)),
        *near(second[0], *moved[0], second[4], *moved[1]),
    )
    back = [
        {0: owned[h], **{o: shift(owned[h], axes[h][1], o) for o in (1, 3, 2)}} for h in range(2)
    ]
    factor_theirs = shift(factor, "core", 1)
    line_x, line_y, lines, factors = call(
        line_kernel, near(line, line, shape((2, 4, 3, 128, 128), bf16), shape((512, 64), bf16)),
        square, *near(*(back[h][o] for h in range(2) for o in range(4)), factor, factor_theirs),
    )
    every = (0, 1, 2, 3)
    beside = [shift((line_x, line_y)[h], axes[h][0], o) for h, o in FIRST]
    grad_qkv, grad_out, copy_x, copy_y = assemble(
        square[1], (lines,), [(0, h, 0, 0, h, every) for h in range(2)], None,
        (factors, head_t, line_x, line_y),
    )
    opposite = [shift((copy_x, copy_y)[h], axes[h][0], 2) for h in range(2)]
    (sides,) = call(
        join_kernel, near(shape((6, 4, 3, 128, 128), bf16)), *near(*beside, copy_x, copy_y)
    )
    sides_theirs = shift(sides, "core", 1)
    side_tags = [(0, k, o, h) for k, (h, o) in enumerate((*FIRST, (0, 0), (1, 0)))]

    def tagged(tags, side):
        return [(array, k, o, side, h, every) for array, k, o, h in tags]

    (grad_qkv,) = assemble(square[1], (sides,), tagged(side_tags[:4], 0), grad_qkv)
    (grad_qkv,) = assemble(square[1], (sides_theirs,), tagged(side_tags, 1), grad_qkv)
    (across,) = call(
        join_kernel, near(shape((2, 4, 3, 128, 128), bf16)), *near(*opposite), *far(grad_qkv), mib=LARGE
    )
    across_theirs = shift(across, "core", 1)
    for side, array in enumerate((across, across_theirs)):
        (grad_qkv,) = assemble(square[1], (array,), tagged([(0, 0, 2, 0), (0, 1, 2, 1)], side), grad_qkv)
    return frame_loss, grad_qkv, grad_out


def solution(mesh):
    fine = Mesh(mesh.devices.reshape(4, 4, 2, 4), ("y", "x", "core", "frame"))
    store = ("y", "x", "core")
    in_specs = (
        P((*store, "frame"), None),
        P((*store, "frame"), None),
        P((*store, "frame")),
        P(store),
        P(),
        P(),
        P(None, None, "frame"),
        P("frame", None),
        P(),
    )
    out_specs = (P(store, "frame"), P(None, None, "frame"), P("frame", None))
    return jax.shard_map(shards, mesh=fine, in_specs=in_specs, out_specs=out_specs, check_vma=False)
```

```python
import functools
import math

import jax
import jax.numpy as jnp
from jax import lax
from jax.experimental import pallas as pl
from jax.experimental.pallas import tpu as pltpu
from jax.sharding import Mesh, PartitionSpec as P

HEAD_DIM = 128
TIMESTEPS = 1000
UNUSED = 64.0
NEAR = ((0, 1), (0, 3), (1, 1), (1, 3))
PIECES = (*NEAR, (0, 2), (1, 2), (0, 0), (1, 0))
f32 = jnp.float32
bf16 = jnp.bfloat16
HIGHEST = lax.Precision.HIGHEST
INV_ROOT = 1.0 / math.sqrt(HEAD_DIM)
NN = (((1,), (0,)), ((), ()))
NT = (((1,), (1,)), ((), ()))
TN = (((0,), (0,)), ((), ()))
ORDER = (0, 1, 3, 2)
SPOT = {r: i for i, r in enumerate(ORDER)}
VMEM = pl.BlockSpec(memory_space=pltpu.VMEM)
SMEM = pl.BlockSpec(memory_space=pltpu.SMEM)
HBM = pl.BlockSpec(memory_space=pltpu.HBM)
ANY = pl.BlockSpec(memory_space=pl.ANY)


LARGE = 52


def params(mib):
    return pltpu.CompilerParams(vmem_limit_bytes=mib << 20)


def cost(flops, moved):
    return pl.CostEstimate(flops=flops, bytes_accessed=moved, transcendentals=0)


TINY = cost(0, 1024)


def dot(a, b, dims=NN, precision=None):
    return lax.dot_general(a, b, dims, preferred_element_type=f32, precision=precision)


def shift(value, axis, offset):
    size = lax.axis_size(axis)
    return lax.ppermute(value, axis, [(i, (i + offset) % size) for i in range(size)])


def shape(dims, kind):
    return jax.ShapeDtypeStruct(dims, kind)


def bucket_kernel(rows, dest_row, out):
    dest_col = jnp.broadcast_to(dest_row[...].astype(f32), (128, 128)).T
    earlier = lax.broadcasted_iota(jnp.int32, (128, 128), 0) < lax.broadcasted_iota(
        jnp.int32, (128, 128), 1
    )
    same = jnp.where((dest_col == dest_row[...].astype(f32)) & earlier, 1.0, 0.0)
    slot = dest_row[...] * 8 + jnp.sum(same, axis=0, keepdims=True).astype(jnp.int32)
    hot = jnp.where(lax.broadcasted_iota(jnp.int32, (256, 128), 0) == slot, 1.0, 0.0)
    used = jnp.max(hot, axis=1, keepdims=True)
    moved = dot(hot.astype(bf16), rows[...]) + (1.0 - used) * UNUSED
    out[...] = moved.astype(bf16).reshape(16, 16, 128)


def prepare_kernel(place, w, w_out, head_t, w_t, mix, mix_t, held, out_rows, turned, sems, leave):
    start = pl.multiple_of(place[1] * 256, 256)
    loads = [
        pltpu.make_async_copy(w.at[j, :, pl.ds(start, 256)], held.at[j], sems.at[j]) for j in range(3)
    ]
    loads.append(pltpu.make_async_copy(w_out.at[pl.ds(start, 256)], out_rows, sems.at[3]))
    for load in loads:
        load.start()
    stores = []
    for j in range(3):
        loads[j].wait()
        for h in range(2):
            k = h * 3 + j
            turned[k] = held[j, :, h * 128 : h * 128 + 128].T
            stores.append(pltpu.make_async_copy(turned.at[k], w_t.at[pl.ds(k * 128, 128)], leave.at[k]))
            stores[-1].start()
    loads[3].wait()
    mix[...] = dot(out_rows[...], head_t[...], NT)
    mix_t[...] = dot(head_t[...], out_rows[...], NT)
    for store in stores:
        store.wait()


def sides_kernel(before, after, arrived, top, bottom, both, spread):
    top[...] = before[:64]
    bottom[...] = after[64:]
    both[0] = before[...]
    both[1] = after[...]
    for k in range(8):
        spread[k] = arrived[...]


def fetch_kernel(place, arrived, pairs):
    frame, core = place[0], place[1]
    slots = 512

    def order_of(i):
        return ((i % 256) // 16) * 32 + (i // 256) * 16 + i % 16

    before = jnp.where(
        order_of(lax.broadcasted_iota(jnp.int32, (slots, slots), 0))
        < order_of(lax.broadcasted_iota(jnp.int32, (slots, slots), 1)),
        1.0,
        0.0,
    ).astype(bf16)
    half = (lax.broadcasted_iota(jnp.int32, (8, slots), 1) // 8) % 2
    which = lax.broadcasted_iota(jnp.int32, (8, slots), 0)
    clip = core + (which % 2) - 2 * core * (which % 2)
    first = jnp.where(lax.broadcasted_iota(jnp.int32, (16, 128), 1) == 0, 1.0, 0.0).astype(bf16)
    rows, values = [], jnp.zeros((8, slots), f32)
    for i, r in enumerate(ORDER):
        from_frame = (frame + 4 - r) % 4
        rows.append(jnp.concatenate([arrived[from_frame], arrived[4 + from_frame]], axis=0))
        values = jnp.where(which // 2 == i, dot(first, rows[i], NT)[:8], values)
    mine = jnp.where((values < 32.0) & (half == clip), 1.0, 0.0)
    doubled = jnp.concatenate([mine, mine], axis=0).astype(bf16)
    rank = jnp.where(mine > 0.5, dot(doubled, before)[:8], -1.0)
    line = lax.broadcasted_iota(jnp.int32, (128, slots), 0).astype(f32)
    for b in range(8):
        pick = jnp.where(rank[b : b + 1] == line, 1.0, 0.0).astype(bf16)
        pairs[b] = dot(pick, rows[b // 2]).astype(bf16)


def lanes(i, other):
    return slice((2 * i + other) * 128, (2 * i + other) * 128 + 128)


def forward_kernel(moments, *refs):
    act_own, act_theirs, sides, sides_theirs, top, top_theirs, bottom, bottom_theirs = refs[:8]
    pairs, w_embed, gain, w_t_far, head_t, mix_t = refs[8:14]
    normed_far, proj_far, attended_far, probs, part_own, part_other = refs[14:20]
    act, w_t, normed, proj, attended, rest, sems, arrive = refs[20:]
    whole, low, high = pl.ds(0, 128), pl.ds(0, 64), pl.ds(64, 64)
    moves = [(act_own, 0, whole), (act_theirs, 1, whole)]
    for side in range(2):
        moves += [(sides.at[side], 2 + 2 * side, whole), (sides_theirs.at[side], 3 + 2 * side, whole)]
    moves += [(top, 6, low), (bottom, 6, high), (top_theirs, 7, low), (bottom_theirs, 7, high)]
    loads = [[] for _ in range(8)]
    for k, (source, b, rows) in enumerate(moves):
        loads[b].append(pltpu.make_async_copy(source, act.at[b, rows], arrive.at[k]))
        loads[b][-1].start()
    weights = pltpu.make_async_copy(w_t_far, w_t, sems.at[0])
    weights.start()
    for b in range(8):
        pair = pairs[b].astype(f32)
        t = moments[b % 2]
        noised = ((1.0 - t) * pair[:, :64] + t * pair[:, 64:]).astype(bf16)
        added = dot(noised, w_embed[...])
        for load in loads[b]:
            load.wait()
        hidden = act[b].astype(f32) + added
        scale = lax.rsqrt(jnp.mean(hidden * hidden, axis=1, keepdims=True) + 1e-06)
        normed[b * 128 : b * 128 + 128] = (hidden * scale * gain[...]).astype(bf16)
        if b == 0:
            turned = pair.T
            own = dot(head_t[...].astype(f32), hidden, NT, HIGHEST)
            rest[...] = own - (turned[64:] - turned[:64])
    leave = [pltpu.make_async_copy(normed, normed_far, sems.at[1])]
    leave[0].start()
    weights.wait()
    for i in range(3):
        rows = slice(i * 256, i * 256 + 256)
        proj[rows] = dot(w_t[rows], normed[...], NT).astype(bf16)
    leave.append(pltpu.make_async_copy(proj, proj_far, sems.at[2]))
    leave[1].start()
    for h in range(2):
        for other in range(2):

            def read(j, f):
                row = h * 384 + j * 128
                return proj[row : row + 128, lanes(f, other)].astype(f32)

            keys = [read(1, g) for g in range(4)]
            values = [read(2, g) for g in range(4)]
            for f in range(4):
                query = read(0, f)
                scores = [jnp.sum(query * k, axis=0, keepdims=True) * INV_ROOT for k in keys]
                peak = jnp.maximum(jnp.maximum(scores[0], scores[1]), jnp.maximum(scores[2], scores[3]))
                powers = [jnp.exp(s - peak) for s in scores]
                whole = powers[0] + powers[1] + powers[2] + powers[3]
                prob = [p / whole for p in powers]
                rounded = [p.astype(bf16).astype(f32) for p in prob]
                out = rounded[0] * values[0]
                for g in range(1, 4):
                    out = out + rounded[g] * values[g]
                attended[h * 128 : h * 128 + 128, lanes(f, other)] = out.astype(bf16)
                for g in range(4):
                    probs[h * 2 + other, f * 4 + g : f * 4 + g + 1] = prob[g]
    leave.append(pltpu.make_async_copy(attended, attended_far, sems.at[3]))
    leave[2].start()
    for other, part in ((0, part_own), (1, part_other)):
        for f in range(4):
            value = dot(mix_t[...], attended[:, lanes(f, other)].astype(f32), NN, HIGHEST)
            if other == 0 and f == 0:
                value = value + rest[...]
            part[:, f * 128 : f * 128 + 128] = value
    for copy in leave:
        copy.wait()


def gradient_piece(delta, normed, factor, h, block, out):
    columns = pl.ds(pl.multiple_of(block * 512, 512), 512)
    out[:384] = dot(delta[h * 384 : h * 384 + 384], normed[:, columns]).astype(bf16)
    for i in range(4):
        out[384:, i * 128 : i * 128 + 128] = factor[i * 16 : i * 16 + 16]


def backward_kernel(place, error_own, error_other, probs, mix, proj_far, attended_far, normed_far, *refs):
    pieces = refs[:8]
    delta, own_factor, slope, grad, proj, attended, normed, sems = refs[8:]
    loads = [
        pltpu.make_async_copy(far, near, sems.at[k])
        for k, (far, near) in enumerate(((proj_far, proj), (attended_far, attended), (normed_far, normed)))
    ]
    for load in loads:
        load.start()
    for i in range(4):
        for other, error in ((0, error_own), (1, error_other)):
            slope[:, lanes(i, other)] = error[:, i * 128 : i * 128 + 128] * (2.0 / 32.0)
    grad[...] = dot(mix[...], slope[...], NN, HIGHEST)
    loads[0].wait()
    for h in range(2):
        for other in range(2):

            def read(j, f):
                row = h * 384 + j * 128
                return proj[row : row + 128, lanes(f, other)].astype(f32)

            def prob(f, g):
                return probs[h * 2 + other, f * 4 + g : f * 4 + g + 1]

            grads = [grad[h * 128 : h * 128 + 128, lanes(f, other)] for f in range(4)]
            score = [[None] * 4 for _ in range(4)]
            for f in range(4):
                dprob = [jnp.sum(grads[f] * read(2, g), axis=0, keepdims=True) for g in range(4)]
                mean = sum(dprob[g] * prob(f, g) for g in range(4))
                for g in range(4):
                    score[f][g] = prob(f, g) * (dprob[g] - mean) * INV_ROOT
            for g in range(4):
                value = sum(prob(f, g).astype(bf16).astype(f32) * grads[f] for f in range(4))
                query = sum(score[g][i] * read(1, i) for i in range(4))
                key = sum(score[f][g] * read(0, f) for f in range(4))
                for j, out in enumerate((query, key, value)):
                    row = h * 384 + j * 128
                    delta[row : row + 128, lanes(g, other)] = out.astype(bf16)
    loads[1].wait()
    for h in range(2):
        factor = dot(slope[...], attended[h * 128 : h * 128 + 128].astype(f32), NT, HIGHEST)
        own_factor[h] = factor.astype(bf16)
    loads[2].wait()
    for (h, o), out in zip(PIECES, pieces):
        gradient_piece(delta, normed, own_factor[h], h, (place[h] + o) % 4, out)


def add_first_kernel(place, *refs):
    both = refs[16]
    for h in range(2):
        parts, outs = refs[4 * h : 4 * h + 4], refs[8 + 4 * h : 12 + 4 * h]
        total = parts[0][...].astype(f32)
        for part in parts[1:]:
            total = total + part[...].astype(f32)
        both[...] = total.astype(bf16)
        for o, out in enumerate(outs):
            columns = pl.ds(pl.multiple_of(((place[1 - h] + o) % 4) * 128, 128), 128)
            out[:384] = both[:384, columns]
            for i in range(4):
                out[384 + i * 16 : 400 + i * 16] = both[384:, i * 128 : i * 128 + 128]


def add_second_kernel(*refs):
    factor = refs[10]
    for h in range(2):
        parts, owned = refs[4 * h : 4 * h + 4], refs[8 + h]
        total = parts[0][...].astype(f32)
        for part in parts[1:]:
            total = total + part[...].astype(f32)
        for j in range(3):
            owned[j] = total[j * 128 : j * 128 + 128].T.astype(bf16)
        factor[h * 128 : h * 128 + 128] = total[384:].T.astype(bf16)


def line_kernel(*refs):
    factor, lines, factor_out = refs[8], refs[9:11], refs[11]
    for h in range(2):
        for o in range(4):
            lines[h][o] = refs[4 * h + o][...]
    factor_out[...] = factor[...]


def join_kernel(*refs):
    out = refs[-1]
    for k in range(out.shape[0]):
        out[k] = refs[k][...]


def assemble_kernel(tags, aliased, with_out, place, *refs):
    arrays = 1 + max(tag[0] for tag in tags)
    count = len(tags)
    sources, refs = refs[:arrays], refs[arrays + aliased :]
    if with_out:
        factor, factor_theirs, head_t, out, grad_out, held, ready, done, sems, whole, sent, factors = refs
        start = pl.multiple_of(place[2] * 256, 256)
        factors[pl.ds(start, 256)] = factor[...]
        factors[pl.ds(pl.multiple_of(256 - start, 256), 256)] = factor_theirs[...]
    else:
        out, held, ready, done, sems = refs
    loads = []
    for k, tag in enumerate(tags):
        source = sources[tag[0]] if tag[1] is None else sources[tag[0]].at[tag[1]]
        loads.append(pltpu.make_async_copy(source, held.at[k], sems.at[k]))
        loads[-1].start()
    if with_out:
        whole[...] = dot(factors[...], head_t[...])
        leave = pltpu.make_async_copy(whole, grad_out, sent.at[0])
        leave.start()
    stores = []
    for k, tag in enumerate(tags):
        o, theirs, h, inners = tag[2:]
        loads[k].wait()
        first = (place[h] + 4 - o) % 4
        for i, inner in enumerate(inners):
            second = (place[1 - h] + 4 - inner) % 4
            ready[k, :, pl.ds(pl.multiple_of(second * 128, 128), 128)] = held[k, i].astype(f32)
        core = place[2] if theirs == 0 else 1 - place[2]
        stores.append(
            pltpu.make_async_copy(
                ready.at[k],
                out.at[
                    :,
                    pl.ds(pl.multiple_of(first * 512, 512), 512),
                    pl.ds(pl.multiple_of(core * 256 + h * 128, 128), 128),
                ],
                done.at[k],
            )
        )
        stores[k].start()
    for store in stores:
        store.wait()
    if with_out:
        leave.wait()


def assemble(place, arrays, tags, onto=None, product=()):
    tags = tuple(sorted(tags, key=lambda t: t[2:]))
    given = [] if onto is None else [onto]
    out_shape = [shape((3, 2048, 512), f32)]
    out_specs = [HBM]
    scratch = [
        pltpu.VMEM((len(tags), *arrays[0].shape[-4:]), bf16),
        pltpu.VMEM((len(tags), 3, 512, 128), f32),
        pltpu.SemaphoreType.DMA((len(tags),)),
        pltpu.SemaphoreType.DMA((len(tags),)),
    ]
    if product:
        out_shape.append(shape((512, 2048), f32))
        out_specs.append(HBM)
        scratch += [
            pltpu.VMEM((512, 2048), f32),
            pltpu.SemaphoreType.DMA((1,)),
            pltpu.VMEM((512, 64), bf16),
        ]
    return pl.pallas_call(
        functools.partial(assemble_kernel, tags, len(given), bool(product)),
        in_specs=[SMEM] + [ANY] * len(arrays) + [HBM] * len(given) + [VMEM] * len(product),
        out_specs=out_specs,
        out_shape=out_shape,
        scratch_shapes=scratch,
        input_output_aliases={1 + len(arrays): 0} if given else {},
        compiler_params=params(LARGE),
        cost_estimate=TINY,
    )(place, *arrays, *given, *product)


def call(kernel, out, *operands, scratch=(), mib=8):
    result = pl.pallas_call(
        kernel,
        in_specs=[spec for spec, _ in operands],
        out_specs=[spec for spec, _ in out],
        out_shape=[made for _, made in out],
        scratch_shapes=list(scratch),
        compiler_params=params(mib),
        cost_estimate=TINY,
    )(*(array for _, array in operands))
    return result


def near(*arrays):
    return [(VMEM, a) for a in arrays]


def far(*arrays):
    return [(HBM, a) for a in arrays]


def shards(act, cache_rows, row_dest, time_index, w_embed, norm_gain, w_qkv, w_out, w_head):
    x, y, core, frame = (lax.axis_index(a).astype(jnp.int32) for a in ("x", "y", "core", "frame"))
    here = (SMEM, jnp.stack([frame, core]))
    square = (SMEM, jnp.stack([x, y, core]))
    dma = pltpu.SemaphoreType.DMA

    before, after = shift(act, "frame", 1), shift(act, "frame", 3)
    act_theirs = shift(act, "core", 1)
    (sent,) = call(
        bucket_kernel, near(shape((16, 16, 128), bf16)), *near(cache_rows, row_dest.reshape(1, 128))
    )
    arrived = lax.all_to_all(sent, ("y", "x"), 0, 0, tiled=True).reshape(256, 128)
    half_act = shape((64, 2048), bf16)
    top, bottom, sides, spread = call(
        sides_kernel,
        near(half_act, half_act, shape((2, 128, 2048), bf16), shape((8, 256, 128), bf16)),
        *near(before, after, arrived),
        mib=LARGE,
    )
    top, bottom = shift(top, "frame", 1), shift(bottom, "frame", 3)
    sides_theirs = shift(sides, "core", 1)
    arrived = lax.all_to_all(spread, ("core", "frame"), 0, 0, tiled=True)
    moment = (time_index.astype(f32) + 0.5) / TIMESTEPS
    moments = jnp.concatenate([moment, shift(moment, "core", 1)])

    head_t = w_head.T
    w_t, mix, mix_t = call(
        prepare_kernel,
        far(shape((768, 2048), bf16)) + near(shape((256, 64), f32), shape((64, 256), f32)),
        here, *far(w_qkv, w_out), *near(head_t),
        scratch=[
            pltpu.VMEM((3, 2048, 256), bf16),
            pltpu.VMEM((256, 2048), bf16),
            pltpu.VMEM((6, 128, 2048), bf16),
            dma((4,)),
            dma((6,)),
        ],
        mib=LARGE,
    )
    (pairs,) = call(fetch_kernel, near(shape((8, 128, 128), bf16)), here, *near(arrived))
    normed, proj, attended, probs, part_own, part_other = call(
        forward_kernel,
        far(shape((1024, 2048), bf16), shape((768, 1024), bf16), shape((256, 1024), bf16))
        + near(shape((4, 16, 128), f32), shape((64, 512), f32), shape((64, 512), f32)),
        (SMEM, moments),
        *far(act, act_theirs, sides, sides_theirs, top, shift(top, "core", 1), bottom, shift(bottom, "core", 1)),
        *near(pairs, w_embed, norm_gain.reshape(1, 2048)), *far(w_t), *near(head_t, mix_t),
        scratch=[
            pltpu.VMEM((8, 128, 2048), bf16),
            pltpu.VMEM((768, 2048), bf16),
            pltpu.VMEM((1024, 2048), bf16),
            pltpu.VMEM((768, 1024), bf16),
            pltpu.VMEM((256, 1024), bf16),
            pltpu.VMEM((64, 128), f32),
            dma((4,)),
            dma((10,)),
        ],
        mib=LARGE,
    )

    clip_part = part_own + shift(part_other, "core", 1)
    heard = {0: clip_part, **{o: shift(clip_part, "frame", o) for o in (1, 3, 2)}}
    error_own = jnp.concatenate(
        [
            sum(
                heard[o][:, SPOT[(r - o) % 4] * 128 : SPOT[(r - o) % 4] * 128 + 128]
                for o in range(4)
            )
            for r in ORDER
        ],
        axis=1,
    )
    frame_loss = jnp.mean(error_own[:, :128] * error_own[:, :128]).reshape(1, 1)
    error_other = shift(error_own, "core", 1)

    piece = shape((400, 512), bf16)
    small = shape((448, 128), bf16)
    block = shape((3, 128, 128), bf16)
    line = shape((4, 3, 128, 128), bf16)
    axes = (("x", "y"), ("y", "x"))
    pieces = call(
        backward_kernel,
        near(*[piece] * 8),
        square, *near(error_own, error_other, probs, mix), *far(proj, attended, normed),
        scratch=[
            pltpu.VMEM((768, 1024), bf16),
            pltpu.VMEM((2, 64, 128), bf16),
            pltpu.VMEM((64, 1024), f32),
            pltpu.VMEM((256, 1024), f32),
            pltpu.VMEM((768, 1024), bf16),
            pltpu.VMEM((256, 1024), bf16),
            pltpu.VMEM((1024, 2048), bf16),
            dma((3,)),
        ],
        mib=LARGE,
    )
    moved = [[], []]
    for (h, o), p in zip(PIECES, pieces[:6]):
        moved[h].append(shift(p, axes[h][0], o))
    own_x, own_y = pieces[6:]
    second = call(
        add_first_kernel, near(*[small] * 8), square, *near(own_x, *moved[0], own_y, *moved[1]),
        scratch=[pltpu.VMEM((400, 512), bf16)],
    )
    moved = [[shift(second[h * 4 + o], axes[h][1], o) for o in (1, 3, 2)] for h in range(2)]
    *owned, factor = call(
        add_second_kernel, near(block, block, shape((256, 64), bf16)),
        *near(second[0], *moved[0], second[4], *moved[1]),
    )
    back = [
        {0: owned[h], **{o: shift(owned[h], axes[h][1], o) for o in (1, 3, 2)}} for h in range(2)
    ]
    line_x, line_y, factor = call(
        line_kernel, near(line, line, shape((256, 64), bf16)),
        *near(*(back[h][o] for h in range(2) for o in range(4)), factor),
    )
    factor_theirs = shift(factor, "core", 1)
    every = (0, 1, 2, 3)
    lines = (line_x, line_y)
    beside = [shift(lines[h], axes[h][0], o) for h, o in NEAR]
    opposite = [shift(lines[h], axes[h][0], 2) for h in range(2)]
    (grad_qkv,) = assemble(square[1], lines, [(h, None, 0, 0, h, every) for h in range(2)])
    (sides,) = call(
        join_kernel, near(shape((6, 4, 3, 128, 128), bf16)), *near(*beside, *lines), *far(grad_qkv),
        mib=LARGE,
    )
    sides_theirs = shift(sides, "core", 1)
    side_tags = [(0, k, o, h) for k, (h, o) in enumerate((*NEAR, (0, 0), (1, 0)))]

    def tagged(tags, side):
        return [(array, k, o, side, h, every) for array, k, o, h in tags]

    grad_qkv, grad_out = assemble(
        square[1], (sides,), tagged(side_tags[:4], 0), grad_qkv, (factor, factor_theirs, head_t)
    )
    (grad_qkv,) = assemble(square[1], (sides_theirs,), tagged(side_tags, 1), grad_qkv)
    (across,) = call(
        join_kernel, near(shape((2, 4, 3, 128, 128), bf16)), *near(*opposite), *far(grad_qkv), mib=LARGE
    )
    across_theirs = shift(across, "core", 1)
    for side, array in enumerate((across, across_theirs)):
        (grad_qkv,) = assemble(square[1], (array,), tagged([(0, 0, 2, 0), (0, 1, 2, 1)], side), grad_qkv)
    return frame_loss, grad_qkv, grad_out


def solution(mesh):
    fine = Mesh(mesh.devices.reshape(4, 4, 2, 4), ("y", "x", "core", "frame"))
    store = ("y", "x", "core")
    in_specs = (
        P((*store, "frame"), None),
        P((*store, "frame"), None),
        P((*store, "frame")),
        P(store),
        P(),
        P(),
        P(None, None, "frame"),
        P("frame", None),
        P(),
    )
    out_specs = (P(store, "frame"), P(None, None, "frame"), P("frame", None))
    return jax.shard_map(shards, mesh=fine, in_specs=in_specs, out_specs=out_specs, check_vma=False)
```

```python
import functools
import math

import jax
import jax.numpy as jnp
from jax import lax
from jax.experimental import pallas as pl
from jax.experimental.pallas import tpu as pltpu
from jax.sharding import Mesh, PartitionSpec as P

HEAD_DIM = 128
TIMESTEPS = 1000
UNUSED = 64.0
NEAR = ((0, 1), (0, 3), (1, 1), (1, 3))
PIECES = ((0, 2), (1, 2), (0, 1), (1, 1), (0, 3), (1, 3), (0, 0), (1, 0))
f32 = jnp.float32
bf16 = jnp.bfloat16
HIGHEST = lax.Precision.HIGHEST
INV_ROOT = 1.0 / math.sqrt(HEAD_DIM)
NN = (((1,), (0,)), ((), ()))
NT = (((1,), (1,)), ((), ()))
TN = (((0,), (0,)), ((), ()))
ORDER = (0, 1, 3, 2)
SPOT = {r: i for i, r in enumerate(ORDER)}
VMEM = pl.BlockSpec(memory_space=pltpu.VMEM)
SMEM = pl.BlockSpec(memory_space=pltpu.SMEM)
HBM = pl.BlockSpec(memory_space=pltpu.HBM)
ANY = pl.BlockSpec(memory_space=pl.ANY)


LARGE = 52


def params(mib):
    return pltpu.CompilerParams(vmem_limit_bytes=mib << 20)


def cost(flops, moved):
    return pl.CostEstimate(flops=flops, bytes_accessed=moved, transcendentals=0)


TINY = cost(0, 1024)


def dot(a, b, dims=NN, precision=None):
    return lax.dot_general(a, b, dims, preferred_element_type=f32, precision=precision)


def shift(value, axis, offset):
    size = lax.axis_size(axis)
    return lax.ppermute(value, axis, [(i, (i + offset) % size) for i in range(size)])


def shape(dims, kind):
    return jax.ShapeDtypeStruct(dims, kind)


def bucket_kernel(rows, dest_row, out):
    dest_col = jnp.broadcast_to(dest_row[...].astype(f32), (128, 128)).T
    earlier = lax.broadcasted_iota(jnp.int32, (128, 128), 0) < lax.broadcasted_iota(
        jnp.int32, (128, 128), 1
    )
    same = jnp.where((dest_col == dest_row[...].astype(f32)) & earlier, 1.0, 0.0)
    slot = dest_row[...] * 8 + jnp.sum(same, axis=0, keepdims=True).astype(jnp.int32)
    hot = jnp.where(lax.broadcasted_iota(jnp.int32, (256, 128), 0) == slot, 1.0, 0.0)
    used = jnp.max(hot, axis=1, keepdims=True)
    moved = dot(hot.astype(bf16), rows[...]) + (1.0 - used) * UNUSED
    out[...] = moved.astype(bf16).reshape(16, 16, 128)


def prepare_kernel(place, w, w_out, head_t, w_t, mix, mix_t, held, out_rows, turned, sems, leave):
    start = pl.multiple_of(place[1] * 256, 256)
    loads = [
        pltpu.make_async_copy(w.at[j, :, pl.ds(start, 256)], held.at[j], sems.at[j]) for j in range(3)
    ]
    loads.append(pltpu.make_async_copy(w_out.at[pl.ds(start, 256)], out_rows, sems.at[3]))
    for load in loads:
        load.start()
    stores = []
    for j in range(3):
        loads[j].wait()
        for h in range(2):
            k = h * 3 + j
            turned[k] = held[j, :, h * 128 : h * 128 + 128].T
            stores.append(pltpu.make_async_copy(turned.at[k], w_t.at[pl.ds(k * 128, 128)], leave.at[k]))
            stores[-1].start()
    loads[3].wait()
    mix[...] = dot(out_rows[...], head_t[...], NT)
    mix_t[...] = dot(head_t[...], out_rows[...], NT)
    for store in stores:
        store.wait()


def sides_kernel(time, before, after, arrived, top, bottom, both, spread):
    column = lax.broadcasted_iota(jnp.int32, (16, 128), 1)
    digits = jnp.where(column == 0, time[0] // 32, jnp.where(column == 1, time[0] % 32, 0))
    top[...] = before[:64]
    bottom[...] = after[64:]
    both[0] = before[...]
    both[1] = after[...]
    for k in range(8):
        spread[k, :256] = arrived[...]
        spread[k, 256:] = digits.astype(f32).astype(bf16)


def fetch_kernel(place, arrived, pairs, moments):
    frame, core = place[0], place[1]
    slots = 512

    def order_of(i):
        return ((i % 256) // 16) * 32 + (i // 256) * 16 + i % 16

    before = jnp.where(
        order_of(lax.broadcasted_iota(jnp.int32, (slots, slots), 0))
        < order_of(lax.broadcasted_iota(jnp.int32, (slots, slots), 1)),
        1.0,
        0.0,
    ).astype(bf16)
    half = (lax.broadcasted_iota(jnp.int32, (8, slots), 1) // 8) % 2
    which = lax.broadcasted_iota(jnp.int32, (8, slots), 0)
    clip = core + (which % 2) - 2 * core * (which % 2)
    first = jnp.where(lax.broadcasted_iota(jnp.int32, (16, 128), 1) == 0, 1.0, 0.0).astype(bf16)
    rows, values = [], jnp.zeros((8, slots), f32)
    for i, r in enumerate(ORDER):
        from_frame = (frame + 4 - r) % 4
        rows.append(jnp.concatenate([arrived[from_frame, :256], arrived[4 + from_frame, :256]], axis=0))
        values = jnp.where(which // 2 == i, dot(first, rows[i], NT)[:8], values)
    mine = jnp.where((values < 32.0) & (half == clip), 1.0, 0.0)
    doubled = jnp.concatenate([mine, mine], axis=0).astype(bf16)
    rank = jnp.where(mine > 0.5, dot(doubled, before)[:8], -1.0)
    line = lax.broadcasted_iota(jnp.int32, (128, slots), 0).astype(f32)
    for b in range(8):
        pick = jnp.where(rank[b : b + 1] == line, 1.0, 0.0).astype(bf16)
        pairs[b] = dot(pick, rows[b // 2]).astype(bf16)
    for other in range(2):
        digits = arrived[(core + other - 2 * core * other) * 4 + frame, 256:].astype(f32)
        time = digits[:, 0:1] * 32.0 + digits[:, 1:2]
        moments[other] = jnp.broadcast_to((time + 0.5) / TIMESTEPS, (16, 128))


def lanes(i, other):
    return slice((2 * i + other) * 128, (2 * i + other) * 128 + 128)


def forward_kernel(moments, *refs):
    act_own, act_theirs, sides, sides_theirs, top, top_theirs, bottom, bottom_theirs = refs[:8]
    pairs, w_embed, gain, w_t_far, head_t, mix_t = refs[8:14]
    normed_far, proj_far, attended_far, probs, part_own, part_other = refs[14:20]
    act, w_t, normed, proj, attended, rest, sems, arrive = refs[20:]
    whole, low, high = pl.ds(0, 128), pl.ds(0, 64), pl.ds(64, 64)
    moves = [(act_own, 0, whole), (act_theirs, 1, whole)]
    for side in range(2):
        moves += [(sides.at[side], 2 + 2 * side, whole), (sides_theirs.at[side], 3 + 2 * side, whole)]
    moves += [(top, 6, low), (bottom, 6, high), (top_theirs, 7, low), (bottom_theirs, 7, high)]
    loads = [[] for _ in range(8)]
    for k, (source, b, rows) in enumerate(moves):
        loads[b].append(pltpu.make_async_copy(source, act.at[b, rows], arrive.at[k]))
        loads[b][-1].start()
    weights = pltpu.make_async_copy(w_t_far, w_t, sems.at[0])
    weights.start()
    for b in range(8):
        pair = pairs[b].astype(f32)
        t = moments[b % 2, 0:1, :64]
        noised = ((1.0 - t) * pair[:, :64] + t * pair[:, 64:]).astype(bf16)
        added = dot(noised, w_embed[...])
        for load in loads[b]:
            load.wait()
        hidden = act[b].astype(f32) + added
        scale = lax.rsqrt(jnp.mean(hidden * hidden, axis=1, keepdims=True) + 1e-06)
        normed[b * 128 : b * 128 + 128] = (hidden * scale * gain[...]).astype(bf16)
        if b == 0:
            turned = pair.T
            own = dot(head_t[...].astype(f32), hidden, NT, HIGHEST)
            rest[...] = own - (turned[64:] - turned[:64])
    leave = [pltpu.make_async_copy(normed, normed_far, sems.at[1])]
    leave[0].start()
    weights.wait()
    for i in range(3):
        rows = slice(i * 256, i * 256 + 256)
        proj[rows] = dot(w_t[rows], normed[...], NT).astype(bf16)
    leave.append(pltpu.make_async_copy(proj, proj_far, sems.at[2]))
    leave[1].start()
    for h in range(2):
        for other in range(2):

            def read(j, f):
                row = h * 384 + j * 128
                return proj[row : row + 128, lanes(f, other)].astype(f32)

            keys = [read(1, g) for g in range(4)]
            values = [read(2, g) for g in range(4)]
            for f in range(4):
                query = read(0, f)
                scores = [jnp.sum(query * k, axis=0, keepdims=True) * INV_ROOT for k in keys]
                peak = jnp.maximum(jnp.maximum(scores[0], scores[1]), jnp.maximum(scores[2], scores[3]))
                powers = [jnp.exp(s - peak) for s in scores]
                whole = powers[0] + powers[1] + powers[2] + powers[3]
                prob = [p / whole for p in powers]
                rounded = [p.astype(bf16).astype(f32) for p in prob]
                out = rounded[0] * values[0]
                for g in range(1, 4):
                    out = out + rounded[g] * values[g]
                attended[h * 128 : h * 128 + 128, lanes(f, other)] = out.astype(bf16)
                for g in range(4):
                    probs[h * 2 + other, f * 4 + g : f * 4 + g + 1] = prob[g]
    leave.append(pltpu.make_async_copy(attended, attended_far, sems.at[3]))
    leave[2].start()
    for other, part in ((0, part_own), (1, part_other)):
        for f in range(4):
            value = dot(mix_t[...], attended[:, lanes(f, other)].astype(f32), NN, HIGHEST)
            if other == 0 and f == 0:
                value = value + rest[...]
            part[:, f * 128 : f * 128 + 128] = value
    for copy in leave:
        copy.wait()


def gradient_piece(delta, normed, factor, h, block, out):
    columns = pl.ds(pl.multiple_of(block * 512, 512), 512)
    out[:384] = dot(delta[h * 384 : h * 384 + 384], normed[:, columns]).astype(bf16)
    for i in range(4):
        out[384:, i * 128 : i * 128 + 128] = factor[i * 16 : i * 16 + 16]


def backward_kernel(place, error_own, error_other, probs, mix, proj_far, attended_far, normed_far, *refs):
    pieces = refs[:8]
    delta, own_factor, slope, grad, proj, attended, normed, sems = refs[8:]
    loads = [
        pltpu.make_async_copy(far, near, sems.at[k])
        for k, (far, near) in enumerate(((proj_far, proj), (attended_far, attended), (normed_far, normed)))
    ]
    for load in loads:
        load.start()
    for i in range(4):
        for other, error in ((0, error_own), (1, error_other)):
            slope[:, lanes(i, other)] = error[:, i * 128 : i * 128 + 128] * (2.0 / 32.0)
    grad[...] = dot(mix[...], slope[...], NN, HIGHEST)
    loads[0].wait()
    for h in range(2):
        for other in range(2):

            def read(j, f):
                row = h * 384 + j * 128
                return proj[row : row + 128, lanes(f, other)].astype(f32)

            def prob(f, g):
                return probs[h * 2 + other, f * 4 + g : f * 4 + g + 1]

            grads = [grad[h * 128 : h * 128 + 128, lanes(f, other)] for f in range(4)]
            score = [[None] * 4 for _ in range(4)]
            for f in range(4):
                dprob = [jnp.sum(grads[f] * read(2, g), axis=0, keepdims=True) for g in range(4)]
                mean = sum(dprob[g] * prob(f, g) for g in range(4))
                for g in range(4):
                    score[f][g] = prob(f, g) * (dprob[g] - mean) * INV_ROOT
            for g in range(4):
                value = sum(prob(f, g).astype(bf16).astype(f32) * grads[f] for f in range(4))
                query = sum(score[g][i] * read(1, i) for i in range(4))
                key = sum(score[f][g] * read(0, f) for f in range(4))
                for j, out in enumerate((query, key, value)):
                    row = h * 384 + j * 128
                    delta[row : row + 128, lanes(g, other)] = out.astype(bf16)
    loads[1].wait()
    for h in range(2):
        factor = dot(slope[...], attended[h * 128 : h * 128 + 128].astype(f32), NT, HIGHEST)
        own_factor[h] = factor.astype(bf16)
    loads[2].wait()
    for (h, o), out in zip(PIECES, pieces):
        gradient_piece(delta, normed, own_factor[h], h, (place[h] + o) % 4, out)


def add_first_kernel(place, *refs):
    both = refs[16]
    for h in range(2):
        parts, outs = refs[h:8:2], refs[8 + 4 * h : 12 + 4 * h]
        total = parts[0][...].astype(f32)
        for part in parts[1:]:
            total = total + part[...].astype(f32)
        both[...] = total.astype(bf16)
        for o, out in enumerate(outs):
            columns = pl.ds(pl.multiple_of(((place[1 - h] + o) % 4) * 128, 128), 128)
            out[:384] = both[:384, columns]
            for i in range(4):
                out[384 + i * 16 : 400 + i * 16] = both[384:, i * 128 : i * 128 + 128]


def add_second_kernel(*refs):
    factor = refs[10]
    for h in range(2):
        parts, owned = refs[h:8:2], refs[8 + h]
        total = parts[0][...].astype(f32)
        for part in parts[1:]:
            total = total + part[...].astype(f32)
        for j in range(3):
            owned[j] = total[j * 128 : j * 128 + 128].T.astype(bf16)
        factor[h * 128 : h * 128 + 128] = total[384:].T.astype(bf16)


def line_kernel(*refs):
    for h in range(2):
        for k, o in enumerate((2, 1, 3, 0)):
            refs[8 + h][o] = refs[2 * k + h][...]


def sides_join_kernel(a, b, c, d, line_x, line_y, factor, token, out):
    for k, ref in enumerate((a, b, c, d, line_x, line_y)):
        out[k] = ref[...]
    out[6, 0] = jnp.zeros((3, 128, 128), bf16)
    for k in range(2):
        out[6, 0, k, :, :64] = factor[k * 128 : k * 128 + 128]
    for k in range(1, 4):
        out[6, k] = jnp.zeros((3, 128, 128), bf16)


def join_kernel(*refs):
    out = refs[-1]
    for k in range(out.shape[0]):
        out[k] = refs[k][...]


def assemble_kernel(tags, arrays, aliased, with_out, place, *refs):
    count = len(tags)
    sources, refs = refs[:arrays], refs[arrays + aliased :]
    if with_out:
        head_t, out, token, grad_out, held, ready, done, sems, whole, sent, factors = refs
        fetched = []
        for k, core in ((0, 1 - place[2]), (1, place[2])):
            target = factors.at[pl.ds(core * 2, 2)]
            fetched.append(pltpu.make_async_copy(sources[k].at[6, 0, 0:2], target, sent.at[1 + k]))
            fetched[k].start()
    else:
        out, token, held, ready, done, sems = refs
    token[...] = jnp.zeros((8, 128), f32)
    loads = []
    for k, tag in enumerate(tags):
        source = sources[tag[0]] if tag[1] is None else sources[tag[0]].at[tag[1]]
        loads.append(pltpu.make_async_copy(source, held.at[k], sems.at[k]))
        loads[-1].start()
    if with_out:
        for copy in fetched:
            copy.wait()
        for k in range(4):
            whole[k * 128 : k * 128 + 128] = dot(factors[k, :, :64], head_t[...])
        leave = pltpu.make_async_copy(whole, grad_out, sent.at[0])
        leave.start()
    stores = []
    for k, tag in enumerate(tags):
        o, theirs, h, inners = tag[2:]
        loads[k].wait()
        first = (place[h] + 4 - o) % 4
        for i, inner in enumerate(inners):
            second = (place[1 - h] + 4 - inner) % 4
            ready[k, :, pl.ds(pl.multiple_of(second * 128, 128), 128)] = held[k, i].astype(f32)
        core = place[2] if theirs == 0 else 1 - place[2]
        stores.append(
            pltpu.make_async_copy(
                ready.at[k],
                out.at[
                    :,
                    pl.ds(pl.multiple_of(first * 512, 512), 512),
                    pl.ds(pl.multiple_of(core * 256 + h * 128, 128), 128),
                ],
                done.at[k],
            )
        )
        stores[k].start()
    for store in stores:
        store.wait()
    if with_out:
        leave.wait()


def assemble(place, arrays, tags, onto=None, product=()):
    tags = tuple(sorted(tags, key=lambda t: t[2:]))
    given = [] if onto is None else [onto]
    out_shape = [shape((3, 2048, 512), f32), shape((8, 128), f32)]
    out_specs = [HBM, VMEM]
    dma = pltpu.SemaphoreType.DMA
    scratch = [
        pltpu.VMEM((len(tags), *arrays[0].shape[-4:]), bf16),
        pltpu.VMEM((len(tags), 3, 512, 128), f32),
        dma((len(tags),)),
        dma((len(tags),)),
    ]
    if product:
        out_shape.append(shape((512, 2048), f32))
        out_specs.append(HBM)
        scratch += [pltpu.VMEM((512, 2048), f32), dma((3,)), pltpu.VMEM((4, 128, 128), bf16)]
    return pl.pallas_call(
        functools.partial(assemble_kernel, tags, len(arrays), len(given), bool(product)),
        in_specs=[SMEM] + [ANY] * len(arrays) + [HBM] * len(given) + [VMEM] * len(product),
        out_specs=out_specs,
        out_shape=out_shape,
        scratch_shapes=scratch,
        input_output_aliases={1 + len(arrays): 0} if given else {},
        compiler_params=params(20),
        cost_estimate=TINY,
    )(place, *arrays, *given, *product)


def call(kernel, out, *operands, scratch=(), mib=8):
    result = pl.pallas_call(
        kernel,
        in_specs=[spec for spec, _ in operands],
        out_specs=[spec for spec, _ in out],
        out_shape=[made for _, made in out],
        scratch_shapes=list(scratch),
        compiler_params=params(mib),
        cost_estimate=TINY,
    )(*(array for _, array in operands))
    return result


def near(*arrays):
    return [(VMEM, a) for a in arrays]


def far(*arrays):
    return [(HBM, a) for a in arrays]


def shards(act, cache_rows, row_dest, time_index, w_embed, norm_gain, w_qkv, w_out, w_head):
    x, y, core, frame = (lax.axis_index(a).astype(jnp.int32) for a in ("x", "y", "core", "frame"))
    here = (SMEM, jnp.stack([frame, core]))
    square = (SMEM, jnp.stack([x, y, core]))
    dma = pltpu.SemaphoreType.DMA

    before, after = shift(act, "frame", 1), shift(act, "frame", 3)
    act_theirs = shift(act, "core", 1)
    (sent,) = call(
        bucket_kernel, near(shape((16, 16, 128), bf16)), *near(cache_rows, row_dest.reshape(1, 128))
    )
    arrived = lax.all_to_all(sent, ("y", "x"), 0, 0, tiled=True).reshape(256, 128)
    half_act = shape((64, 2048), bf16)
    top, bottom, sides, spread = call(
        sides_kernel,
        near(half_act, half_act, shape((2, 128, 2048), bf16), shape((8, 272, 128), bf16)),
        (SMEM, time_index), *near(before, after, arrived),
    )
    top, bottom = shift(top, "frame", 1), shift(bottom, "frame", 3)
    sides_theirs = shift(sides, "core", 1)
    arrived = lax.all_to_all(spread, ("core", "frame"), 0, 0, tiled=True)
    head_t = w_head.T
    w_t, mix, mix_t = call(
        prepare_kernel,
        far(shape((768, 2048), bf16)) + near(shape((256, 64), f32), shape((64, 256), f32)),
        here, *far(w_qkv, w_out), *near(head_t),
        scratch=[
            pltpu.VMEM((3, 2048, 256), bf16),
            pltpu.VMEM((256, 2048), bf16),
            pltpu.VMEM((6, 128, 2048), bf16),
            dma((4,)),
            dma((6,)),
        ],
        mib=LARGE,
    )
    pairs, moments = call(
        fetch_kernel, near(shape((8, 128, 128), bf16), shape((2, 16, 128), f32)), here, *near(arrived)
    )
    normed, proj, attended, probs, part_own, part_other = call(
        forward_kernel,
        far(shape((1024, 2048), bf16), shape((768, 1024), bf16), shape((256, 1024), bf16))
        + near(shape((4, 16, 128), f32), shape((64, 512), f32), shape((64, 512), f32)),
        *near(moments),
        *far(act, act_theirs, sides, sides_theirs, top, shift(top, "core", 1), bottom, shift(bottom, "core", 1)),
        *near(pairs, w_embed, norm_gain.reshape(1, 2048)), *far(w_t), *near(head_t, mix_t),
        scratch=[
            pltpu.VMEM((8, 128, 2048), bf16),
            pltpu.VMEM((768, 2048), bf16),
            pltpu.VMEM((1024, 2048), bf16),
            pltpu.VMEM((768, 1024), bf16),
            pltpu.VMEM((256, 1024), bf16),
            pltpu.VMEM((64, 128), f32),
            dma((4,)),
            dma((10,)),
        ],
        mib=LARGE,
    )

    clip_part = part_own + shift(part_other, "core", 1)
    heard = {0: clip_part, **{o: shift(clip_part, "frame", o) for o in (2, 1, 3)}}
    error_own = jnp.concatenate(
        [
            sum(
                heard[o][:, SPOT[(r - o) % 4] * 128 : SPOT[(r - o) % 4] * 128 + 128]
                for o in range(4)
            )
            for r in ORDER
        ],
        axis=1,
    )
    frame_loss = jnp.mean(error_own[:, :128] * error_own[:, :128]).reshape(1, 1)
    error_other = shift(error_own, "core", 1)

    piece = shape((400, 512), bf16)
    small = shape((448, 128), bf16)
    block = shape((3, 128, 128), bf16)
    line = shape((4, 3, 128, 128), bf16)
    axes = (("x", "y"), ("y", "x"))
    pieces = call(
        backward_kernel,
        near(*[piece] * 8),
        square, *near(error_own, error_other, probs, mix), *far(proj, attended, normed),
        scratch=[
            pltpu.VMEM((768, 1024), bf16),
            pltpu.VMEM((2, 64, 128), bf16),
            pltpu.VMEM((64, 1024), f32),
            pltpu.VMEM((256, 1024), f32),
            pltpu.VMEM((768, 1024), bf16),
            pltpu.VMEM((256, 1024), bf16),
            pltpu.VMEM((1024, 2048), bf16),
            dma((3,)),
        ],
        mib=49,
    )
    moved = [shift(p, axes[h][0], o) for (h, o), p in zip(PIECES[:6], pieces)]
    second = call(
        add_first_kernel, near(*[small] * 8), square, *near(*moved, *pieces[6:]),
        scratch=[pltpu.VMEM((400, 512), bf16)],
    )
    moved = [shift(second[h * 4 + o], axes[h][1], o) for h, o in PIECES[:6]]
    *owned, factor = call(
        add_second_kernel, near(block, block, shape((256, 64), bf16)),
        *near(*moved, second[0], second[4]),
    )
    back = [shift(owned[h], axes[h][1], o) for h, o in PIECES[:6]]
    lines = call(
        line_kernel, near(line, line), *near(*back, *owned),
    )
    every = (0, 1, 2, 3)
    opposite = [shift(lines[h], axes[h][0], 2) for h in range(2)]
    beside = [shift(lines[h], axes[h][0], o) for h, o in NEAR]
    grad_qkv, token = assemble(square[1], lines, [(h, None, 0, 0, h, every) for h in range(2)])
    (sides,) = call(
        sides_join_kernel, near(shape((7, 4, 3, 128, 128), bf16)), *near(*beside, *lines, factor, token)
    )
    sides_theirs = shift(sides, "core", 1)
    side_tags = [(0, k, o, h) for k, (h, o) in enumerate((*NEAR, (0, 0), (1, 0)))]

    def tagged(tags, side):
        return [(array, k, o, side, h, every) for array, k, o, h in tags]

    grad_qkv, token = assemble(square[1], (sides,), tagged(side_tags[:4], 0), grad_qkv)
    grad_qkv, token, grad_out = assemble(
        square[1], (sides_theirs, sides), tagged(side_tags, 1), grad_qkv, (head_t,)
    )
    (across,) = call(
        join_kernel, near(shape((2, 4, 3, 128, 128), bf16)), *near(*opposite, token)
    )
    across_theirs = shift(across, "core", 1)
    for side, array in enumerate((across, across_theirs)):
        grad_qkv, token = assemble(
            square[1], (array,), tagged([(0, 0, 2, 0), (0, 1, 2, 1)], side), grad_qkv
        )
    return frame_loss, grad_qkv, grad_out


def solution(mesh):
    fine = Mesh(mesh.devices.reshape(4, 4, 2, 4), ("y", "x", "core", "frame"))
    store = ("y", "x", "core")
    in_specs = (
        P((*store, "frame"), None),
        P((*store, "frame"), None),
        P((*store, "frame")),
        P(store),
        P(),
        P(),
        P(None, None, "frame"),
        P("frame", None),
        P(),
    )
    out_specs = (P(store, "frame"), P(None, None, "frame"), P("frame", None))
    return jax.shard_map(shards, mesh=fine, in_specs=in_specs, out_specs=out_specs, check_vma=False)
```

```python
import functools
import math

import jax
import jax.numpy as jnp
from jax import lax
from jax.experimental import pallas as pl
from jax.experimental.pallas import tpu as pltpu
from jax.sharding import Mesh, PartitionSpec as P

HEAD_DIM = 128
TIMESTEPS = 1000
UNUSED = 64.0
NEAR = ((0, 1), (0, 3), (1, 1), (1, 3))
PIECES = ((0, 2), (1, 2), (0, 1), (1, 1), (0, 3), (1, 3), (0, 0), (1, 0))
f32 = jnp.float32
bf16 = jnp.bfloat16
HIGHEST = lax.Precision.HIGHEST
INV_ROOT = 1.0 / math.sqrt(HEAD_DIM)
NN = (((1,), (0,)), ((), ()))
NT = (((1,), (1,)), ((), ()))
TN = (((0,), (0,)), ((), ()))
ORDER = (0, 1, 3, 2)
SPOT = {r: i for i, r in enumerate(ORDER)}
VMEM = pl.BlockSpec(memory_space=pltpu.VMEM)
SMEM = pl.BlockSpec(memory_space=pltpu.SMEM)
HBM = pl.BlockSpec(memory_space=pltpu.HBM)
ANY = pl.BlockSpec(memory_space=pl.ANY)


LARGE = 52


def params(mib):
    return pltpu.CompilerParams(vmem_limit_bytes=mib << 20)


def cost(flops, moved):
    return pl.CostEstimate(flops=flops, bytes_accessed=moved, transcendentals=0)


TINY = cost(0, 1024)


def dot(a, b, dims=NN, precision=None):
    return lax.dot_general(a, b, dims, preferred_element_type=f32, precision=precision)


def thirds(value):
    high = value.astype(bf16)
    left = value - high.astype(f32)
    middle = left.astype(bf16)
    return high, middle, (left - middle.astype(f32)).astype(bf16)


def split_dot(value, exact, dims=NN):
    rows = value.shape[0]
    out = dot(jnp.concatenate(thirds(value), axis=0), exact, dims)
    return out[:rows] + out[rows : 2 * rows] + out[2 * rows :]


def shift(value, axis, offset):
    size = lax.axis_size(axis)
    return lax.ppermute(value, axis, [(i, (i + offset) % size) for i in range(size)])


def shape(dims, kind):
    return jax.ShapeDtypeStruct(dims, kind)


def bucket_kernel(rows, dest_row, out):
    dest_col = jnp.broadcast_to(dest_row[...].astype(f32), (128, 128)).T
    earlier = lax.broadcasted_iota(jnp.int32, (128, 128), 0) < lax.broadcasted_iota(
        jnp.int32, (128, 128), 1
    )
    same = jnp.where((dest_col == dest_row[...].astype(f32)) & earlier, 1.0, 0.0)
    slot = dest_row[...] * 8 + jnp.sum(same, axis=0, keepdims=True).astype(jnp.int32)
    hot = jnp.where(lax.broadcasted_iota(jnp.int32, (256, 128), 0) == slot, 1.0, 0.0)
    used = jnp.max(hot, axis=1, keepdims=True)
    moved = dot(hot.astype(bf16), rows[...]) + (1.0 - used) * UNUSED
    out[...] = moved.astype(bf16).reshape(16, 16, 128)


def prepare_kernel(place, w, w_out, head_t, w_t, mix, mix_t, held, out_rows, turned, sems, leave):
    start = pl.multiple_of(place[1] * 256, 256)
    loads = [
        pltpu.make_async_copy(w.at[j, :, pl.ds(start, 256)], held.at[j], sems.at[j]) for j in range(3)
    ]
    loads.append(pltpu.make_async_copy(w_out.at[pl.ds(start, 256)], out_rows, sems.at[3]))
    for load in loads:
        load.start()
    stores = []
    for j in range(3):
        loads[j].wait()
        for h in range(2):
            k = h * 3 + j
            turned[k] = held[j, :, h * 128 : h * 128 + 128].T
            stores.append(pltpu.make_async_copy(turned.at[k], w_t.at[pl.ds(k * 128, 128)], leave.at[k]))
            stores[-1].start()
    loads[3].wait()
    mix[...] = dot(out_rows[...], head_t[...], NT)
    mix_t[...] = dot(head_t[...], out_rows[...], NT)
    for store in stores:
        store.wait()


def sides_kernel(time, before, after, arrived, top, bottom, both, spread):
    column = lax.broadcasted_iota(jnp.int32, (16, 128), 1)
    digits = jnp.where(column == 0, time[0] // 32, jnp.where(column == 1, time[0] % 32, 0))
    top[...] = before[:64]
    bottom[...] = after[64:]
    both[0] = before[...]
    both[1] = after[...]
    for k in range(8):
        spread[k, :256] = arrived[...]
        spread[k, 256:] = digits.astype(f32).astype(bf16)


def fetch_kernel(place, arrived, pairs, moments):
    frame, core = place[0], place[1]
    slots = 512

    def order_of(i):
        return ((i % 256) // 16) * 32 + (i // 256) * 16 + i % 16

    before = jnp.where(
        order_of(lax.broadcasted_iota(jnp.int32, (slots, slots), 0))
        < order_of(lax.broadcasted_iota(jnp.int32, (slots, slots), 1)),
        1.0,
        0.0,
    ).astype(bf16)
    half = (lax.broadcasted_iota(jnp.int32, (8, slots), 1) // 8) % 2
    which = lax.broadcasted_iota(jnp.int32, (8, slots), 0)
    clip = core + (which % 2) - 2 * core * (which % 2)
    first = jnp.where(lax.broadcasted_iota(jnp.int32, (16, 128), 1) == 0, 1.0, 0.0).astype(bf16)
    rows, values = [], jnp.zeros((8, slots), f32)
    for i, r in enumerate(ORDER):
        from_frame = (frame + 4 - r) % 4
        rows.append(jnp.concatenate([arrived[from_frame, :256], arrived[4 + from_frame, :256]], axis=0))
        values = jnp.where(which // 2 == i, dot(first, rows[i], NT)[:8], values)
    mine = jnp.where((values < 32.0) & (half == clip), 1.0, 0.0)
    doubled = jnp.concatenate([mine, mine], axis=0).astype(bf16)
    rank = jnp.where(mine > 0.5, dot(doubled, before)[:8], -1.0)
    line = lax.broadcasted_iota(jnp.int32, (128, slots), 0).astype(f32)
    for b in range(8):
        pick = jnp.where(rank[b : b + 1] == line, 1.0, 0.0).astype(bf16)
        pairs[b] = dot(pick, rows[b // 2]).astype(bf16)
    for other in range(2):
        digits = arrived[(core + other - 2 * core * other) * 4 + frame, 256:].astype(f32)
        time = digits[:, 0:1] * 32.0 + digits[:, 1:2]
        moments[other] = jnp.broadcast_to((time + 0.5) / TIMESTEPS, (16, 128))


def lanes(i, other):
    return slice((2 * i + other) * 128, (2 * i + other) * 128 + 128)


def forward_kernel(moments, *refs):
    act_own, act_theirs, sides, sides_theirs, top, top_theirs, bottom, bottom_theirs = refs[:8]
    pairs, w_embed, gain, w_t_far, head_t, mix_t = refs[8:14]
    normed_far, proj_far, attended_far, probs, part_own, part_other = refs[14:20]
    act, w_t, normed, proj, attended, rest, sems, arrive = refs[20:]
    whole, low, high = pl.ds(0, 128), pl.ds(0, 64), pl.ds(64, 64)
    moves = [(act_own, 0, whole), (act_theirs, 1, whole)]
    for side in range(2):
        moves += [(sides.at[side], 2 + 2 * side, whole), (sides_theirs.at[side], 3 + 2 * side, whole)]
    moves += [(top, 6, low), (bottom, 6, high), (top_theirs, 7, low), (bottom_theirs, 7, high)]
    loads = [[] for _ in range(8)]
    for k, (source, b, rows) in enumerate(moves):
        loads[b].append(pltpu.make_async_copy(source, act.at[b, rows], arrive.at[k]))
        loads[b][-1].start()
    weights = pltpu.make_async_copy(w_t_far, w_t, sems.at[0])
    weights.start()
    for b in range(8):
        pair = pairs[b].astype(f32)
        t = moments[b % 2, 0:1, :64]
        noised = ((1.0 - t) * pair[:, :64] + t * pair[:, 64:]).astype(bf16)
        added = dot(noised, w_embed[...])
        for load in loads[b]:
            load.wait()
        hidden = act[b].astype(f32) + added
        scale = lax.rsqrt(jnp.mean(hidden * hidden, axis=1, keepdims=True) + 1e-06)
        normed[b * 128 : b * 128 + 128] = (hidden * scale * gain[...]).astype(bf16)
        if b == 0:
            turned = pair.T
            own = sum(dot(head_t[...], term, NT) for term in thirds(hidden))
            rest[...] = own - (turned[64:] - turned[:64])
    leave = [pltpu.make_async_copy(normed, normed_far, sems.at[1])]
    leave[0].start()
    weights.wait()
    for i in range(3):
        rows = slice(i * 256, i * 256 + 256)
        proj[rows] = dot(w_t[rows], normed[...], NT).astype(bf16)
    leave.append(pltpu.make_async_copy(proj, proj_far, sems.at[2]))
    leave[1].start()
    for h in range(2):
        for other in range(2):

            def read(j, f):
                row = h * 384 + j * 128
                return proj[row : row + 128, lanes(f, other)].astype(f32)

            keys = [read(1, g) for g in range(4)]
            values = [read(2, g) for g in range(4)]
            for f in range(4):
                query = read(0, f)
                scores = [jnp.sum(query * k, axis=0, keepdims=True) * INV_ROOT for k in keys]
                peak = jnp.maximum(jnp.maximum(scores[0], scores[1]), jnp.maximum(scores[2], scores[3]))
                powers = [jnp.exp(s - peak) for s in scores]
                whole = powers[0] + powers[1] + powers[2] + powers[3]
                prob = [p / whole for p in powers]
                rounded = [p.astype(bf16).astype(f32) for p in prob]
                out = rounded[0] * values[0]
                for g in range(1, 4):
                    out = out + rounded[g] * values[g]
                attended[h * 128 : h * 128 + 128, lanes(f, other)] = out.astype(bf16)
                for g in range(4):
                    probs[h * 2 + other, f * 4 + g : f * 4 + g + 1] = prob[g]
    leave.append(pltpu.make_async_copy(attended, attended_far, sems.at[3]))
    leave[2].start()
    value = split_dot(mix_t[...], attended[...])
    for other, part in ((0, part_own), (1, part_other)):
        for f in range(4):
            added = rest[...] if other == 0 and f == 0 else 0.0
            part[:, f * 128 : f * 128 + 128] = value[:, lanes(f, other)] + added
    for copy in leave:
        copy.wait()


def gradient_piece(delta, normed, factor, h, block, out):
    columns = pl.ds(pl.multiple_of(block * 512, 512), 512)
    out[:384] = dot(delta[h * 384 : h * 384 + 384], normed[:, columns]).astype(bf16)
    for i in range(4):
        out[384:, i * 128 : i * 128 + 128] = factor[i * 16 : i * 16 + 16]


def backward_kernel(place, error_own, error_other, probs, mix, proj_far, attended_far, normed_far, *refs):
    pieces = refs[:8]
    delta, own_factor, slope, grad, proj, attended, normed, sems = refs[8:]
    loads = [
        pltpu.make_async_copy(far, near, sems.at[k])
        for k, (far, near) in enumerate(((proj_far, proj), (attended_far, attended), (normed_far, normed)))
    ]
    for load in loads:
        load.start()
    for i in range(4):
        for other, error in ((0, error_own), (1, error_other)):
            slope[:, lanes(i, other)] = error[:, i * 128 : i * 128 + 128] * (2.0 / 32.0)
    grad[...] = dot(mix[...], slope[...], NN, HIGHEST)
    loads[0].wait()
    for h in range(2):
        for other in range(2):

            def read(j, f):
                row = h * 384 + j * 128
                return proj[row : row + 128, lanes(f, other)].astype(f32)

            def prob(f, g):
                return probs[h * 2 + other, f * 4 + g : f * 4 + g + 1]

            grads = [grad[h * 128 : h * 128 + 128, lanes(f, other)] for f in range(4)]
            score = [[None] * 4 for _ in range(4)]
            for f in range(4):
                dprob = [jnp.sum(grads[f] * read(2, g), axis=0, keepdims=True) for g in range(4)]
                mean = sum(dprob[g] * prob(f, g) for g in range(4))
                for g in range(4):
                    score[f][g] = prob(f, g) * (dprob[g] - mean) * INV_ROOT
            for g in range(4):
                value = sum(prob(f, g).astype(bf16).astype(f32) * grads[f] for f in range(4))
                query = sum(score[g][i] * read(1, i) for i in range(4))
                key = sum(score[f][g] * read(0, f) for f in range(4))
                for j, out in enumerate((query, key, value)):
                    row = h * 384 + j * 128
                    delta[row : row + 128, lanes(g, other)] = out.astype(bf16)
    loads[1].wait()
    factor = split_dot(slope[...], attended[...], NT)
    for h in range(2):
        own_factor[h] = factor[:, h * 128 : h * 128 + 128].astype(bf16)
    loads[2].wait()
    for (h, o), out in zip(PIECES, pieces):
        gradient_piece(delta, normed, own_factor[h], h, (place[h] + o) % 4, out)


def add_first_kernel(place, *refs):
    both = refs[16]
    for h in range(2):
        parts, outs = refs[h:8:2], refs[8 + 4 * h : 12 + 4 * h]
        total = parts[0][...].astype(f32)
        for part in parts[1:]:
            total = total + part[...].astype(f32)
        both[...] = total.astype(bf16)
        for o, out in enumerate(outs):
            columns = pl.ds(pl.multiple_of(((place[1 - h] + o) % 4) * 128, 128), 128)
            out[:384] = both[:384, columns]
            for i in range(4):
                out[384 + i * 16 : 400 + i * 16] = both[384:, i * 128 : i * 128 + 128]


def add_second_kernel(*refs):
    factor = refs[10]
    for h in range(2):
        parts, owned = refs[h:8:2], refs[8 + h]
        total = parts[0][...].astype(f32)
        for part in parts[1:]:
            total = total + part[...].astype(f32)
        for j in range(3):
            owned[j] = total[j * 128 : j * 128 + 128].T.astype(bf16)
        factor[h * 128 : h * 128 + 128] = total[384:].T.astype(bf16)


def line_kernel(*refs):
    for h in range(2):
        for k, o in enumerate((2, 1, 3, 0)):
            refs[8 + h][o] = refs[2 * k + h][...]


def first_join_kernel(a, b, c, line, factor, out):
    for k, ref in enumerate((a, b, c, line)):
        out[k] = ref[...]
    out[4, 0] = jnp.zeros((3, 128, 128), bf16)
    for k in range(2):
        out[4, 0, k, :, :64] = factor[k * 128 : k * 128 + 128]
    for k in range(1, 4):
        out[4, k] = jnp.zeros((3, 128, 128), bf16)


def join_kernel(*refs):
    out = refs[-1]
    for k in range(out.shape[0]):
        out[k] = refs[k][...]


def assemble_kernel(tags, arrays, aliased, with_out, place, *refs):
    count = len(tags)
    sources, refs = refs[:arrays], refs[arrays + aliased :]
    if with_out:
        head_t, out, token, grad_out, held, ready, done, sems, whole, sent, factors = refs
        fetched = []
        for k, core in ((0, 1 - place[2]), (1, place[2])):
            target = factors.at[pl.ds(core * 2, 2)]
            fetched.append(pltpu.make_async_copy(sources[k].at[4, 0, 0:2], target, sent.at[1 + k]))
            fetched[k].start()
    else:
        out, token, held, ready, done, sems = refs
    token[...] = jnp.zeros((8, 128), f32)
    loads = []
    for k, tag in enumerate(tags):
        source = sources[tag[0]] if tag[1] is None else sources[tag[0]].at[tag[1]]
        loads.append(pltpu.make_async_copy(source, held.at[k], sems.at[k]))
        loads[-1].start()
    if with_out:
        for copy in fetched:
            copy.wait()
        for k in range(4):
            whole[k * 128 : k * 128 + 128] = dot(factors[k, :, :64], head_t[...])
        leave = pltpu.make_async_copy(whole, grad_out, sent.at[0])
        leave.start()
    stores = []
    for k, tag in enumerate(tags):
        o, theirs, h, inners = tag[2:]
        loads[k].wait()
        first = (place[h] + 4 - o) % 4
        for i, inner in enumerate(inners):
            second = (place[1 - h] + 4 - inner) % 4
            ready[k, :, pl.ds(pl.multiple_of(second * 128, 128), 128)] = held[k, i].astype(f32)
        core = place[2] if theirs == 0 else 1 - place[2]
        stores.append(
            pltpu.make_async_copy(
                ready.at[k],
                out.at[
                    :,
                    pl.ds(pl.multiple_of(first * 512, 512), 512),
                    pl.ds(pl.multiple_of(core * 256 + h * 128, 128), 128),
                ],
                done.at[k],
            )
        )
        stores[k].start()
    for store in stores:
        store.wait()
    if with_out:
        leave.wait()


def assemble(place, arrays, tags, onto=None, product=()):
    tags = tuple(sorted(tags, key=lambda t: t[2:]))
    given = [] if onto is None else [onto]
    out_shape = [shape((3, 2048, 512), f32), shape((8, 128), f32)]
    out_specs = [HBM, VMEM]
    dma = pltpu.SemaphoreType.DMA
    scratch = [
        pltpu.VMEM((len(tags), *arrays[0].shape[-4:]), bf16),
        pltpu.VMEM((len(tags), 3, 512, 128), f32),
        dma((len(tags),)),
        dma((len(tags),)),
    ]
    if product:
        out_shape.append(shape((512, 2048), f32))
        out_specs.append(HBM)
        scratch += [pltpu.VMEM((512, 2048), f32), dma((3,)), pltpu.VMEM((4, 128, 128), bf16)]
    return pl.pallas_call(
        functools.partial(assemble_kernel, tags, len(arrays), len(given), bool(product)),
        in_specs=[SMEM] + [ANY] * len(arrays) + [HBM] * len(given) + [VMEM] * len(product),
        out_specs=out_specs,
        out_shape=out_shape,
        scratch_shapes=scratch,
        input_output_aliases={1 + len(arrays): 0} if given else {},
        compiler_params=params(20),
        cost_estimate=TINY,
    )(place, *arrays, *given, *product)


def call(kernel, out, *operands, scratch=(), mib=8):
    result = pl.pallas_call(
        kernel,
        in_specs=[spec for spec, _ in operands],
        out_specs=[spec for spec, _ in out],
        out_shape=[made for _, made in out],
        scratch_shapes=list(scratch),
        compiler_params=params(mib),
        cost_estimate=TINY,
    )(*(array for _, array in operands))
    return result


def near(*arrays):
    return [(VMEM, a) for a in arrays]


def far(*arrays):
    return [(HBM, a) for a in arrays]


def shards(act, cache_rows, row_dest, time_index, w_embed, norm_gain, w_qkv, w_out, w_head):
    x, y, core, frame = (lax.axis_index(a).astype(jnp.int32) for a in ("x", "y", "core", "frame"))
    here = (SMEM, jnp.stack([frame, core]))
    square = (SMEM, jnp.stack([x, y, core]))
    dma = pltpu.SemaphoreType.DMA

    before, after = shift(act, "frame", 1), shift(act, "frame", 3)
    act_theirs = shift(act, "core", 1)
    (sent,) = call(
        bucket_kernel, near(shape((16, 16, 128), bf16)), *near(cache_rows, row_dest.reshape(1, 128))
    )
    arrived = lax.all_to_all(sent, ("y", "x"), 0, 0, tiled=True).reshape(256, 128)
    half_act = shape((64, 2048), bf16)
    top, bottom, sides, spread = call(
        sides_kernel,
        near(half_act, half_act, shape((2, 128, 2048), bf16), shape((8, 272, 128), bf16)),
        (SMEM, time_index), *near(before, after, arrived),
    )
    top, bottom = shift(top, "frame", 1), shift(bottom, "frame", 3)
    sides_theirs = shift(sides, "core", 1)
    arrived = lax.all_to_all(spread, ("core", "frame"), 0, 0, tiled=True)
    head_t = w_head.T
    w_t, mix, mix_t = call(
        prepare_kernel,
        far(shape((768, 2048), bf16)) + near(shape((256, 64), f32), shape((64, 256), f32)),
        here, *far(w_qkv, w_out), *near(head_t),
        scratch=[
            pltpu.VMEM((3, 2048, 256), bf16),
            pltpu.VMEM((256, 2048), bf16),
            pltpu.VMEM((6, 128, 2048), bf16),
            dma((4,)),
            dma((6,)),
        ],
        mib=LARGE,
    )
    pairs, moments = call(
        fetch_kernel, near(shape((8, 128, 128), bf16), shape((2, 16, 128), f32)), here, *near(arrived)
    )
    normed, proj, attended, probs, part_own, part_other = call(
        forward_kernel,
        far(shape((1024, 2048), bf16), shape((768, 1024), bf16), shape((256, 1024), bf16))
        + near(shape((4, 16, 128), f32), shape((64, 512), f32), shape((64, 512), f32)),
        *near(moments),
        *far(act, act_theirs, sides, sides_theirs, top, shift(top, "core", 1), bottom, shift(bottom, "core", 1)),
        *near(pairs, w_embed, norm_gain.reshape(1, 2048)), *far(w_t), *near(head_t, mix_t),
        scratch=[
            pltpu.VMEM((8, 128, 2048), bf16),
            pltpu.VMEM((768, 2048), bf16),
            pltpu.VMEM((1024, 2048), bf16),
            pltpu.VMEM((768, 1024), bf16),
            pltpu.VMEM((256, 1024), bf16),
            pltpu.VMEM((64, 128), f32),
            dma((4,)),
            dma((10,)),
        ],
        mib=LARGE,
    )

    clip_part = part_own + shift(part_other, "core", 1)
    heard = {0: clip_part, **{o: shift(clip_part, "frame", o) for o in (2, 1, 3)}}
    error_own = jnp.concatenate(
        [
            sum(
                heard[o][:, SPOT[(r - o) % 4] * 128 : SPOT[(r - o) % 4] * 128 + 128]
                for o in range(4)
            )
            for r in ORDER
        ],
        axis=1,
    )
    frame_loss = jnp.mean(error_own[:, :128] * error_own[:, :128]).reshape(1, 1)
    error_other = shift(error_own, "core", 1)

    piece = shape((400, 512), bf16)
    small = shape((448, 128), bf16)
    block = shape((3, 128, 128), bf16)
    line = shape((4, 3, 128, 128), bf16)
    axes = (("x", "y"), ("y", "x"))
    pieces = call(
        backward_kernel,
        near(*[piece] * 8),
        square, *near(error_own, error_other, probs, mix), *far(proj, attended, normed),
        scratch=[
            pltpu.VMEM((768, 1024), bf16),
            pltpu.VMEM((2, 64, 128), bf16),
            pltpu.VMEM((64, 1024), f32),
            pltpu.VMEM((256, 1024), f32),
            pltpu.VMEM((768, 1024), bf16),
            pltpu.VMEM((256, 1024), bf16),
            pltpu.VMEM((1024, 2048), bf16),
            dma((3,)),
        ],
        mib=49,
    )
    moved = [shift(p, axes[h][0], o) for (h, o), p in zip(PIECES[:6], pieces)]
    second = call(
        add_first_kernel, near(*[small] * 8), square, *near(*moved, *pieces[6:]),
        scratch=[pltpu.VMEM((400, 512), bf16)],
    )
    moved = [shift(second[h * 4 + o], axes[h][1], o) for h, o in PIECES[:6]]
    *owned, factor = call(
        add_second_kernel, near(block, block, shape((256, 64), bf16)),
        *near(*moved, second[0], second[4]),
    )
    back = [shift(owned[h], axes[h][1], o) for h, o in PIECES[:6]]
    lines = call(
        line_kernel, near(line, line), *near(*back, *owned),
    )
    every = (0, 1, 2, 3)
    reach = (2, 1, 3)
    wide = [[shift(lines[h], axes[h][0], o) for o in reach] for h in range(2)]
    (half_x,) = call(
        first_join_kernel, near(shape((5, 4, 3, 128, 128), bf16)),
        *near(*wide[0], lines[0], factor),
    )
    half_x_theirs = shift(half_x, "core", 1)

    def tagged(array, side, h, distances):
        return [(array, k, o, side, h, every) for k, o in enumerate(distances)]

    grad_qkv, token = assemble(
        square[1], (half_x, lines[1]), tagged(0, 0, 0, (*reach, 0)) + [(1, None, 0, 0, 1, every)]
    )
    (half_y,) = call(
        join_kernel, near(shape((4, 4, 3, 128, 128), bf16)), *near(*wide[1], lines[1], token)
    )
    half_y_theirs = shift(half_y, "core", 1)
    grad_qkv, token, grad_out = assemble(
        square[1], (half_x_theirs, half_x, half_y),
        tagged(0, 1, 0, (*reach, 0)) + tagged(2, 0, 1, reach), grad_qkv, (head_t,),
    )
    grad_qkv, token = assemble(square[1], (half_y_theirs,), tagged(0, 1, 1, (*reach, 0)), grad_qkv)
    return frame_loss, grad_qkv, grad_out


def solution(mesh):
    fine = Mesh(mesh.devices.reshape(4, 4, 2, 4), ("y", "x", "core", "frame"))
    store = ("y", "x", "core")
    in_specs = (
        P((*store, "frame"), None),
        P((*store, "frame"), None),
        P((*store, "frame")),
        P(store),
        P(),
        P(),
        P(None, None, "frame"),
        P("frame", None),
        P(),
    )
    out_specs = (P(store, "frame"), P(None, None, "frame"), P("frame", None))
    return jax.shard_map(shards, mesh=fine, in_specs=in_specs, out_specs=out_specs, check_vma=False)
```

```python
import functools
import math

import jax
import jax.numpy as jnp
from jax import lax
from jax.experimental import pallas as pl
from jax.experimental.pallas import tpu as pltpu
from jax.sharding import Mesh, PartitionSpec as P

HEAD_DIM = 128
TIMESTEPS = 1000
UNUSED = 64.0
NEAR = ((0, 1), (0, 3), (1, 1), (1, 3))
PIECES = ((0, 2), (1, 2), (0, 1), (1, 1), (0, 3), (1, 3), (0, 0), (1, 0))
f32 = jnp.float32
bf16 = jnp.bfloat16
HIGHEST = lax.Precision.HIGHEST
INV_ROOT = 1.0 / math.sqrt(HEAD_DIM)
NN = (((1,), (0,)), ((), ()))
NT = (((1,), (1,)), ((), ()))
TN = (((0,), (0,)), ((), ()))
ORDER = (0, 1, 3, 2)
SPOT = {r: i for i, r in enumerate(ORDER)}
VMEM = pl.BlockSpec(memory_space=pltpu.VMEM)
SMEM = pl.BlockSpec(memory_space=pltpu.SMEM)
HBM = pl.BlockSpec(memory_space=pltpu.HBM)
ANY = pl.BlockSpec(memory_space=pl.ANY)


LARGE = 52


def params(mib):
    return pltpu.CompilerParams(vmem_limit_bytes=mib << 20)


def cost(flops, moved):
    return pl.CostEstimate(flops=flops, bytes_accessed=moved, transcendentals=0)


TINY = cost(0, 1024)


def dot(a, b, dims=NN, precision=None):
    return lax.dot_general(a, b, dims, preferred_element_type=f32, precision=precision)


def thirds(value):
    high = value.astype(bf16)
    left = value - high.astype(f32)
    middle = left.astype(bf16)
    return high, middle, (left - middle.astype(f32)).astype(bf16)


def split_dot(value, exact, dims=NN):
    rows = value.shape[0]
    out = dot(jnp.concatenate(thirds(value), axis=0), exact, dims)
    return out[:rows] + out[rows : 2 * rows] + out[2 * rows :]


def shift(value, axis, offset):
    size = lax.axis_size(axis)
    return lax.ppermute(value, axis, [(i, (i + offset) % size) for i in range(size)])


def shape(dims, kind):
    return jax.ShapeDtypeStruct(dims, kind)


def bucket_kernel(rows_far, dest_far, out, rows, dest_row, sems):
    loads = [
        pltpu.make_async_copy(rows_far, rows, sems.at[0]),
        pltpu.make_async_copy(dest_far, dest_row, sems.at[1]),
    ]
    for load in loads:
        load.start()
    for load in loads:
        load.wait()
    dest_col = jnp.broadcast_to(dest_row[...].astype(f32), (128, 128)).T
    earlier = lax.broadcasted_iota(jnp.int32, (128, 128), 0) < lax.broadcasted_iota(
        jnp.int32, (128, 128), 1
    )
    same = jnp.where((dest_col == dest_row[...].astype(f32)) & earlier, 1.0, 0.0)
    slot = dest_row[...] * 8 + jnp.sum(same, axis=0, keepdims=True).astype(jnp.int32)
    hot = jnp.where(lax.broadcasted_iota(jnp.int32, (256, 128), 0) == slot, 1.0, 0.0)
    used = jnp.max(hot, axis=1, keepdims=True)
    moved = dot(hot.astype(bf16), rows[...]) + (1.0 - used) * UNUSED
    out[...] = moved.astype(bf16).reshape(16, 16, 128)


def prepare_kernel(place, w, w_out, head_t, w_t, mix, mix_t, held, out_rows, turned, sems, leave):
    start = pl.multiple_of(place[1] * 256, 256)
    loads = [
        pltpu.make_async_copy(w.at[j, :, pl.ds(start, 256)], held.at[j], sems.at[j]) for j in range(3)
    ]
    loads.append(pltpu.make_async_copy(w_out.at[pl.ds(start, 256)], out_rows, sems.at[3]))
    for load in loads:
        load.start()
    stores = []
    for j in range(3):
        loads[j].wait()
        for h in range(2):
            k = h * 3 + j
            turned[k] = held[j, :, h * 128 : h * 128 + 128].T
            stores.append(pltpu.make_async_copy(turned.at[k], w_t.at[pl.ds(k * 128, 128)], leave.at[k]))
            stores[-1].start()
    loads[3].wait()
    mix[...] = dot(out_rows[...], head_t[...], NT)
    mix_t[...] = dot(head_t[...], out_rows[...], NT)
    for store in stores:
        store.wait()


def sides_kernel(time, before, after, arrived, top, bottom, both, spread):
    column = lax.broadcasted_iota(jnp.int32, (16, 128), 1)
    digits = jnp.where(column == 0, time[0] // 32, jnp.where(column == 1, time[0] % 32, 0))
    top[...] = before[:64]
    bottom[...] = after[64:]
    both[0] = before[...]
    both[1] = after[...]
    for k in range(8):
        spread[k, :256] = arrived[...]
        spread[k, 256:] = digits.astype(f32).astype(bf16)


def fetch_kernel(place, arrived, pairs, moments):
    frame, core = place[0], place[1]
    slots = 512

    def order_of(i):
        return ((i % 256) // 16) * 32 + (i // 256) * 16 + i % 16

    before = jnp.where(
        order_of(lax.broadcasted_iota(jnp.int32, (slots, slots), 0))
        < order_of(lax.broadcasted_iota(jnp.int32, (slots, slots), 1)),
        1.0,
        0.0,
    ).astype(bf16)
    half = (lax.broadcasted_iota(jnp.int32, (8, slots), 1) // 8) % 2
    which = lax.broadcasted_iota(jnp.int32, (8, slots), 0)
    clip = core + (which % 2) - 2 * core * (which % 2)
    first = jnp.where(lax.broadcasted_iota(jnp.int32, (16, 128), 1) == 0, 1.0, 0.0).astype(bf16)
    rows, values = [], jnp.zeros((8, slots), f32)
    for i, r in enumerate(ORDER):
        from_frame = (frame + 4 - r) % 4
        rows.append(jnp.concatenate([arrived[from_frame, :256], arrived[4 + from_frame, :256]], axis=0))
        values = jnp.where(which // 2 == i, dot(first, rows[i], NT)[:8], values)
    mine = jnp.where((values < 32.0) & (half == clip), 1.0, 0.0)
    doubled = jnp.concatenate([mine, mine], axis=0).astype(bf16)
    rank = jnp.where(mine > 0.5, dot(doubled, before)[:8], -1.0)
    line = lax.broadcasted_iota(jnp.int32, (128, slots), 0).astype(f32)
    for b in range(8):
        pick = jnp.where(rank[b : b + 1] == line, 1.0, 0.0).astype(bf16)
        pairs[b] = dot(pick, rows[b // 2]).astype(bf16)
    for other in range(2):
        digits = arrived[(core + other - 2 * core * other) * 4 + frame, 256:].astype(f32)
        time = digits[:, 0:1] * 32.0 + digits[:, 1:2]
        moments[other] = jnp.broadcast_to((time + 0.5) / TIMESTEPS, (16, 128))


def lanes(i, other):
    return slice((2 * i + other) * 128, (2 * i + other) * 128 + 128)


def forward_kernel(moments, *refs):
    act_own, act_theirs, sides, sides_theirs, top, top_theirs, bottom, bottom_theirs = refs[:8]
    pairs, w_embed, gain, w_t_far, head_t, mix_t = refs[8:14]
    normed_far, proj_far, probs, part_own, part_other = refs[14:19]
    act, w_t, normed, proj, rest, sems, arrive = refs[19:]
    attended = proj.at[768:1024]
    whole, low, high = pl.ds(0, 128), pl.ds(0, 64), pl.ds(64, 64)
    moves = [(act_own, 0, whole), (act_theirs, 1, whole)]
    for side in range(2):
        moves += [(sides.at[side], 2 + 2 * side, whole), (sides_theirs.at[side], 3 + 2 * side, whole)]
    moves += [(top, 6, low), (bottom, 6, high), (top_theirs, 7, low), (bottom_theirs, 7, high)]
    loads = [[] for _ in range(8)]
    for k, (source, b, rows) in enumerate(moves):
        loads[b].append(pltpu.make_async_copy(source, act.at[b, rows], arrive.at[k]))
        loads[b][-1].start()
    weights = pltpu.make_async_copy(w_t_far, w_t, sems.at[0])
    weights.start()
    for b in range(8):
        pair = pairs[b].astype(f32)
        t = moments[b % 2, 0:1, :64]
        noised = ((1.0 - t) * pair[:, :64] + t * pair[:, 64:]).astype(bf16)
        added = dot(noised, w_embed[...])
        for load in loads[b]:
            load.wait()
        hidden = act[b].astype(f32) + added
        scale = lax.rsqrt(jnp.mean(hidden * hidden, axis=1, keepdims=True) + 1e-06)
        normed[b * 128 : b * 128 + 128] = (hidden * scale * gain[...]).astype(bf16)
        if b == 0:
            turned = pair.T
            own = sum(dot(head_t[...], term, NT) for term in thirds(hidden))
            rest[...] = own - (turned[64:] - turned[:64])
    leave = [pltpu.make_async_copy(normed, normed_far, sems.at[1])]
    leave[0].start()
    weights.wait()
    for i in range(3):
        rows = slice(i * 256, i * 256 + 256)
        proj[rows] = dot(w_t[rows], normed[...], NT).astype(bf16)
    leave.append(pltpu.make_async_copy(proj.at[:768], proj_far.at[:768], sems.at[2]))
    leave[1].start()
    for h in range(2):
        for other in range(2):

            def read(j, f):
                row = h * 384 + j * 128
                return proj[row : row + 128, lanes(f, other)].astype(f32)

            keys = [read(1, g) for g in range(4)]
            values = [read(2, g) for g in range(4)]
            for f in range(4):
                query = read(0, f)
                scores = [jnp.sum(query * k, axis=0, keepdims=True) * INV_ROOT for k in keys]
                peak = jnp.maximum(jnp.maximum(scores[0], scores[1]), jnp.maximum(scores[2], scores[3]))
                powers = [jnp.exp(s - peak) for s in scores]
                whole = powers[0] + powers[1] + powers[2] + powers[3]
                prob = [p / whole for p in powers]
                rounded = [p.astype(bf16).astype(f32) for p in prob]
                out = rounded[0] * values[0]
                for g in range(1, 4):
                    out = out + rounded[g] * values[g]
                attended[h * 128 : h * 128 + 128, lanes(f, other)] = out.astype(bf16)
                for g in range(4):
                    probs[h * 2 + other, f * 4 + g : f * 4 + g + 1] = prob[g]
    leave.append(pltpu.make_async_copy(attended, proj_far.at[768:1024], sems.at[3]))
    leave[2].start()
    value = split_dot(mix_t[...], attended[...])
    for other, part in ((0, part_own), (1, part_other)):
        for f in range(4):
            added = rest[...] if other == 0 and f == 0 else 0.0
            part[:, f * 128 : f * 128 + 128] = value[:, lanes(f, other)] + added
    for copy in leave:
        copy.wait()


def gradient_piece(delta, normed, factor, h, block, out):
    columns = pl.ds(pl.multiple_of(block * 512, 512), 512)
    out[:384] = dot(delta[h * 384 : h * 384 + 384], normed[:, columns]).astype(bf16)
    for i in range(4):
        out[384:, i * 128 : i * 128 + 128] = factor[i * 16 : i * 16 + 16]


def backward_kernel(place, error_own, error_other, probs, mix, proj_far, normed_far, *refs):
    pieces = refs[:8]
    delta, own_factor, slope, grad, proj, normed, sems = refs[8:]
    attended = proj.at[768:1024]
    loads = [
        pltpu.make_async_copy(far, near, sems.at[k])
        for k, (far, near) in enumerate(((proj_far, proj), (normed_far, normed)))
    ]
    for load in loads:
        load.start()
    for i in range(4):
        for other, error in ((0, error_own), (1, error_other)):
            slope[:, lanes(i, other)] = error[:, i * 128 : i * 128 + 128] * (2.0 / 32.0)
    grad[...] = dot(mix[...], slope[...], NN, HIGHEST)
    loads[0].wait()
    for h in range(2):
        for other in range(2):

            def read(j, f):
                row = h * 384 + j * 128
                return proj[row : row + 128, lanes(f, other)].astype(f32)

            def prob(f, g):
                return probs[h * 2 + other, f * 4 + g : f * 4 + g + 1]

            grads = [grad[h * 128 : h * 128 + 128, lanes(f, other)] for f in range(4)]
            score = [[None] * 4 for _ in range(4)]
            for f in range(4):
                dprob = [jnp.sum(grads[f] * read(2, g), axis=0, keepdims=True) for g in range(4)]
                mean = sum(dprob[g] * prob(f, g) for g in range(4))
                for g in range(4):
                    score[f][g] = prob(f, g) * (dprob[g] - mean) * INV_ROOT
            for g in range(4):
                value = sum(prob(f, g).astype(bf16).astype(f32) * grads[f] for f in range(4))
                query = sum(score[g][i] * read(1, i) for i in range(4))
                key = sum(score[f][g] * read(0, f) for f in range(4))
                for j, out in enumerate((query, key, value)):
                    row = h * 384 + j * 128
                    delta[row : row + 128, lanes(g, other)] = out.astype(bf16)
    factor = split_dot(slope[...], attended[...], NT)
    for h in range(2):
        own_factor[h] = factor[:, h * 128 : h * 128 + 128].astype(bf16)
    loads[1].wait()
    for (h, o), out in zip(PIECES, pieces):
        gradient_piece(delta, normed, own_factor[h], h, (place[h] + o) % 4, out)


def add_first_kernel(place, *refs):
    both = refs[16]
    for h in range(2):
        parts, outs = refs[h:8:2], refs[8 + 4 * h : 12 + 4 * h]
        total = parts[0][...].astype(f32)
        for part in parts[1:]:
            total = total + part[...].astype(f32)
        both[...] = total.astype(bf16)
        for o, out in enumerate(outs):
            columns = pl.ds(pl.multiple_of(((place[1 - h] + o) % 4) * 128, 128), 128)
            out[:384] = both[:384, columns]
            for i in range(4):
                out[384 + i * 16 : 400 + i * 16] = both[384:, i * 128 : i * 128 + 128]


def add_second_kernel(*refs):
    factor = refs[10]
    for h in range(2):
        parts, owned = refs[h:8:2], refs[8 + h]
        total = parts[0][...].astype(f32)
        for part in parts[1:]:
            total = total + part[...].astype(f32)
        for j in range(3):
            owned[j] = total[j * 128 : j * 128 + 128].T.astype(bf16)
        factor[h * 128 : h * 128 + 128] = total[384:].T.astype(bf16)


def line_kernel(*refs):
    for h in range(2):
        for k, o in enumerate((3, 1, 2, 0)):
            refs[8 + h][o] = refs[2 * k + h][...]


def first_join_kernel(a, b, c, line, factor, out):
    for k, ref in enumerate((a, b, c, line)):
        out[k] = ref[...]
    out[4, 0] = jnp.zeros((3, 128, 128), bf16)
    for k in range(2):
        out[4, 0, k, :, :64] = factor[k * 128 : k * 128 + 128]
    for k in range(1, 4):
        out[4, k] = jnp.zeros((3, 128, 128), bf16)


def join_kernel(*refs):
    out = refs[-1]
    for k in range(out.shape[0]):
        out[k] = refs[k][...]


def assemble_kernel(tags, arrays, aliased, with_out, place, *refs):
    count = len(tags)
    sources, refs = refs[:arrays], refs[arrays + aliased :]
    if with_out:
        head_t, out, token, grad_out, held, ready, done, sems, whole, sent, factors = refs
        fetched = []
        for k, core in ((0, 1 - place[2]), (1, place[2])):
            target = factors.at[pl.ds(core * 2, 2)]
            fetched.append(pltpu.make_async_copy(sources[k].at[4, 0, 0:2], target, sent.at[1 + k]))
            fetched[k].start()
    else:
        out, token, held, ready, done, sems = refs
    token[...] = jnp.zeros((8, 128), f32)
    loads = []
    for k, tag in enumerate(tags):
        source = sources[tag[0]] if tag[1] is None else sources[tag[0]].at[tag[1]]
        loads.append(pltpu.make_async_copy(source, held.at[k], sems.at[k]))
        loads[-1].start()
    if with_out:
        for copy in fetched:
            copy.wait()
        for k in range(4):
            whole[k * 128 : k * 128 + 128] = dot(factors[k, :, :64], head_t[...])
        leave = pltpu.make_async_copy(whole, grad_out, sent.at[0])
        leave.start()
    stores = []
    for k, tag in enumerate(tags):
        o, theirs, h, inners = tag[2:]
        loads[k].wait()
        first = (place[h] + 4 - o) % 4
        for i, inner in enumerate(inners):
            second = (place[1 - h] + 4 - inner) % 4
            ready[k, :, pl.ds(pl.multiple_of(second * 128, 128), 128)] = held[k, i].astype(f32)
        core = place[2] if theirs == 0 else 1 - place[2]
        stores.append(
            pltpu.make_async_copy(
                ready.at[k],
                out.at[
                    :,
                    pl.ds(pl.multiple_of(first * 512, 512), 512),
                    pl.ds(pl.multiple_of(core * 256 + h * 128, 128), 128),
                ],
                done.at[k],
            )
        )
        stores[k].start()
    for store in stores:
        store.wait()
    if with_out:
        leave.wait()


def assemble(place, arrays, tags, onto=None, product=()):
    tags = tuple(sorted(tags, key=lambda t: t[2:]))
    given = [] if onto is None else [onto]
    out_shape = [shape((3, 2048, 512), f32), shape((8, 128), f32)]
    out_specs = [HBM, VMEM]
    dma = pltpu.SemaphoreType.DMA
    scratch = [
        pltpu.VMEM((len(tags), *arrays[0].shape[-4:]), bf16),
        pltpu.VMEM((len(tags), 3, 512, 128), f32),
        dma((len(tags),)),
        dma((len(tags),)),
    ]
    if product:
        out_shape.append(shape((512, 2048), f32))
        out_specs.append(HBM)
        scratch += [pltpu.VMEM((512, 2048), f32), dma((3,)), pltpu.VMEM((4, 128, 128), bf16)]
    return pl.pallas_call(
        functools.partial(assemble_kernel, tags, len(arrays), len(given), bool(product)),
        in_specs=[SMEM] + [ANY] * len(arrays) + [HBM] * len(given) + [VMEM] * len(product),
        out_specs=out_specs,
        out_shape=out_shape,
        scratch_shapes=scratch,
        input_output_aliases={1 + len(arrays): 0} if given else {},
        compiler_params=params(20),
        cost_estimate=TINY,
    )(place, *arrays, *given, *product)


def call(kernel, out, *operands, scratch=(), mib=8):
    result = pl.pallas_call(
        kernel,
        in_specs=[spec for spec, _ in operands],
        out_specs=[spec for spec, _ in out],
        out_shape=[made for _, made in out],
        scratch_shapes=list(scratch),
        compiler_params=params(mib),
        cost_estimate=TINY,
    )(*(array for _, array in operands))
    return result


def near(*arrays):
    return [(VMEM, a) for a in arrays]


def far(*arrays):
    return [(HBM, a) for a in arrays]


def shards(act, cache_rows, row_dest, time_index, w_embed, norm_gain, w_qkv, w_out, w_head):
    x, y, core, frame = (lax.axis_index(a).astype(jnp.int32) for a in ("x", "y", "core", "frame"))
    here = (SMEM, jnp.stack([frame, core]))
    square = (SMEM, jnp.stack([x, y, core]))
    dma = pltpu.SemaphoreType.DMA

    before, after = shift(act, "frame", 1), shift(act, "frame", 3)
    act_theirs = shift(act, "core", 1)
    (sent,) = call(
        bucket_kernel, near(shape((16, 16, 128), bf16)), *far(cache_rows, row_dest.reshape(1, 128)),
        scratch=[pltpu.VMEM((128, 128), bf16), pltpu.VMEM((1, 128), jnp.int32), dma((2,))],
        mib=LARGE,
    )
    arrived = lax.all_to_all(sent, ("y", "x"), 0, 0, tiled=True).reshape(256, 128)
    half_act = shape((64, 2048), bf16)
    top, bottom, sides, spread = call(
        sides_kernel,
        near(half_act, half_act, shape((2, 128, 2048), bf16), shape((8, 272, 128), bf16)),
        (SMEM, time_index), *near(before, after, arrived),
    )
    top, bottom = shift(top, "frame", 1), shift(bottom, "frame", 3)
    sides_theirs = shift(sides, "core", 1)
    arrived = lax.all_to_all(spread, ("core", "frame"), 0, 0, tiled=True)
    head_t = w_head.T
    w_t, mix, mix_t = call(
        prepare_kernel,
        far(shape((768, 2048), bf16)) + near(shape((256, 64), f32), shape((64, 256), f32)),
        here, *far(w_qkv, w_out), *near(head_t),
        scratch=[
            pltpu.VMEM((3, 2048, 256), bf16),
            pltpu.VMEM((256, 2048), bf16),
            pltpu.VMEM((6, 128, 2048), bf16),
            dma((4,)),
            dma((6,)),
        ],
        mib=LARGE,
    )
    pairs, moments = call(
        fetch_kernel, near(shape((8, 128, 128), bf16), shape((2, 16, 128), f32)), here, *near(arrived)
    )
    normed, proj, probs, part_own, part_other = call(
        forward_kernel,
        far(shape((1024, 2048), bf16), shape((1024, 1024), bf16))
        + near(shape((4, 16, 128), f32), shape((64, 512), f32), shape((64, 512), f32)),
        *near(moments),
        *far(act, act_theirs, sides, sides_theirs, top, shift(top, "core", 1), bottom, shift(bottom, "core", 1)),
        *near(pairs, w_embed, norm_gain.reshape(1, 2048)), *far(w_t), *near(head_t, mix_t),
        scratch=[
            pltpu.VMEM((8, 128, 2048), bf16),
            pltpu.VMEM((768, 2048), bf16),
            pltpu.VMEM((1024, 2048), bf16),
            pltpu.VMEM((1024, 1024), bf16),
            pltpu.VMEM((64, 128), f32),
            dma((4,)),
            dma((10,)),
        ],
        mib=LARGE,
    )

    clip_part = part_own + shift(part_other, "core", 1)
    heard = {0: clip_part, **{o: shift(clip_part, "frame", o) for o in (2, 1, 3)}}
    error_own = jnp.concatenate(
        [
            sum(
                heard[o][:, SPOT[(r - o) % 4] * 128 : SPOT[(r - o) % 4] * 128 + 128]
                for o in range(4)
            )
            for r in ORDER
        ],
        axis=1,
    )
    frame_loss = jnp.mean(error_own[:, :128] * error_own[:, :128]).reshape(1, 1)
    error_other = shift(error_own, "core", 1)

    piece = shape((400, 512), bf16)
    small = shape((448, 128), bf16)
    block = shape((3, 128, 128), bf16)
    line = shape((4, 3, 128, 128), bf16)
    axes = (("x", "y"), ("y", "x"))
    reach = (3, 1, 2)
    pieces = call(
        backward_kernel,
        near(*[piece] * 8),
        square, *near(error_own, error_other, probs, mix), *far(proj, normed),
        scratch=[
            pltpu.VMEM((768, 1024), bf16),
            pltpu.VMEM((2, 64, 128), bf16),
            pltpu.VMEM((64, 1024), f32),
            pltpu.VMEM((256, 1024), f32),
            pltpu.VMEM((1024, 1024), bf16),
            pltpu.VMEM((1024, 2048), bf16),
            dma((2,)),
        ],
        mib=49,
    )
    moved = [shift(p, axes[h][0], o) for (h, o), p in zip(PIECES[:6], pieces)]
    second = call(
        add_first_kernel, near(*[small] * 8), square, *near(*moved, *pieces[6:]),
        scratch=[pltpu.VMEM((400, 512), bf16)],
    )
    moved = [shift(second[h * 4 + o], axes[h][1], o) for h, o in PIECES[:6]]
    *owned, factor = call(
        add_second_kernel, near(block, block, shape((256, 64), bf16)),
        *near(*moved, second[0], second[4]),
    )
    back = [shift(owned[h], axes[h][1], o) for o in reach for h in range(2)]
    lines = call(
        line_kernel, near(line, line), *near(*back, *owned),
    )
    every = (0, 1, 2, 3)
    wide = [[shift(lines[h], axes[h][0], o) for o in reach] for h in range(2)]
    (half_x,) = call(
        first_join_kernel, near(shape((5, 4, 3, 128, 128), bf16)),
        *near(*wide[0], lines[0], factor),
    )
    half_x_theirs = shift(half_x, "core", 1)

    def tagged(array, side, h, distances):
        return [(array, k, o, side, h, every) for k, o in enumerate(distances)]

    grad_qkv, token = assemble(
        square[1], (half_x, lines[1]), tagged(0, 0, 0, (*reach, 0)) + [(1, None, 0, 0, 1, every)]
    )
    (half_y,) = call(
        join_kernel, near(shape((4, 4, 3, 128, 128), bf16)), *near(*wide[1], lines[1], token)
    )
    half_y_theirs = shift(half_y, "core", 1)
    grad_qkv, token, grad_out = assemble(
        square[1], (half_x_theirs, half_x, half_y),
        tagged(0, 1, 0, (*reach, 0)) + tagged(2, 0, 1, reach), grad_qkv, (head_t,),
    )
    grad_qkv, token = assemble(square[1], (half_y_theirs,), tagged(0, 1, 1, (*reach, 0)), grad_qkv)
    return frame_loss, grad_qkv, grad_out


def solution(mesh):
    fine = Mesh(mesh.devices.reshape(4, 4, 2, 4), ("y", "x", "core", "frame"))
    store = ("y", "x", "core")
    in_specs = (
        P((*store, "frame"), None),
        P((*store, "frame"), None),
        P((*store, "frame")),
        P(store),
        P(),
        P(),
        P(None, None, "frame"),
        P("frame", None),
        P(),
    )
    out_specs = (P(store, "frame"), P(None, None, "frame"), P("frame", None))
    return jax.shard_map(shards, mesh=fine, in_specs=in_specs, out_specs=out_specs, check_vma=False)
```

```python
import functools
import math

import jax
import jax.numpy as jnp
from jax import lax
from jax.experimental import pallas as pl
from jax.experimental.pallas import tpu as pltpu
from jax.sharding import Mesh, PartitionSpec as P

HEAD_DIM = 128
TIMESTEPS = 1000
UNUSED = 64.0
NEAR = ((0, 1), (0, 3), (1, 1), (1, 3))
PIECES = ((0, 2), (1, 2), (0, 1), (1, 1), (0, 3), (1, 3), (0, 0), (1, 0))
f32 = jnp.float32
bf16 = jnp.bfloat16
HIGHEST = lax.Precision.HIGHEST
INV_ROOT = 1.0 / math.sqrt(HEAD_DIM)
NN = (((1,), (0,)), ((), ()))
NT = (((1,), (1,)), ((), ()))
TN = (((0,), (0,)), ((), ()))
ORDER = (0, 1, 3, 2)
SPOT = {r: i for i, r in enumerate(ORDER)}
VMEM = pl.BlockSpec(memory_space=pltpu.VMEM)
SMEM = pl.BlockSpec(memory_space=pltpu.SMEM)
HBM = pl.BlockSpec(memory_space=pltpu.HBM)
ANY = pl.BlockSpec(memory_space=pl.ANY)


LARGE = 52


def params(mib):
    return pltpu.CompilerParams(vmem_limit_bytes=mib << 20)


def cost(flops, moved):
    return pl.CostEstimate(flops=flops, bytes_accessed=moved, transcendentals=0)


TINY = cost(0, 1024)


def dot(a, b, dims=NN, precision=None):
    return lax.dot_general(a, b, dims, preferred_element_type=f32, precision=precision)


def thirds(value):
    high = value.astype(bf16)
    left = value - high.astype(f32)
    middle = left.astype(bf16)
    return high, middle, (left - middle.astype(f32)).astype(bf16)


def split_dot(value, exact, dims=NN):
    rows = value.shape[0]
    out = dot(jnp.concatenate(thirds(value), axis=0), exact, dims)
    return out[:rows] + out[rows : 2 * rows] + out[2 * rows :]


def shift(value, axis, offset):
    size = lax.axis_size(axis)
    return lax.ppermute(value, axis, [(i, (i + offset) % size) for i in range(size)])


def shape(dims, kind):
    return jax.ShapeDtypeStruct(dims, kind)


def bucket_kernel(rows_far, dest_far, unused, out, rows, dest_row, sems):
    loads = [
        pltpu.make_async_copy(rows_far, rows, sems.at[0]),
        pltpu.make_async_copy(dest_far, dest_row, sems.at[1]),
    ]
    for load in loads:
        load.start()
    for load in loads:
        load.wait()
    dest_col = jnp.broadcast_to(dest_row[...].astype(f32), (128, 128)).T
    earlier = lax.broadcasted_iota(jnp.int32, (128, 128), 0) < lax.broadcasted_iota(
        jnp.int32, (128, 128), 1
    )
    same = jnp.where((dest_col == dest_row[...].astype(f32)) & earlier, 1.0, 0.0)
    slot = dest_row[...] * 8 + jnp.sum(same, axis=0, keepdims=True).astype(jnp.int32)
    hot = jnp.where(lax.broadcasted_iota(jnp.int32, (256, 128), 0) == slot, 1.0, 0.0)
    used = jnp.max(hot, axis=1, keepdims=True)
    moved = dot(hot.astype(bf16), rows[...]) + (1.0 - used) * UNUSED
    bucket = moved.astype(bf16).reshape(16, 16, 128)
    for frame in range(4):
        for core in range(2):
            out[frame, :, core] = bucket


def prepare_kernel(place, w, w_out, head_t, w_t, mix, mix_t, held, out_rows, turned, sems, leave):
    start = pl.multiple_of(place[1] * 256, 256)
    loads = [
        pltpu.make_async_copy(w.at[j, :, pl.ds(start, 256)], held.at[j], sems.at[j]) for j in range(3)
    ]
    loads.append(pltpu.make_async_copy(w_out.at[pl.ds(start, 256)], out_rows, sems.at[3]))
    for load in loads:
        load.start()
    stores = []
    for j in range(3):
        loads[j].wait()
        for h in range(2):
            k = h * 3 + j
            turned[k] = held[j, :, h * 128 : h * 128 + 128].T
            stores.append(pltpu.make_async_copy(turned.at[k], w_t.at[pl.ds(k * 128, 128)], leave.at[k]))
            stores[-1].start()
    loads[3].wait()
    mix[...] = dot(out_rows[...], head_t[...], NT)
    mix_t[...] = dot(head_t[...], out_rows[...], NT)
    for store in stores:
        store.wait()


def sides_kernel(time, before, across, after, unused, both):
    both[:128] = before[...]
    both[128:256] = after[...]
    both[256:384] = across[...]
    column = lax.broadcasted_iota(jnp.int32, (16, 2048), 1)
    digits = jnp.where(column == 0, time[0] // 32, jnp.where(column == 1, time[0] % 32, 0))
    both[384:] = digits.astype(f32).astype(bf16)


def fetch_kernel(place, arrived, pairs):
    frame, core = place[0], place[1]
    slots = 512
    before = jnp.where(
        lax.broadcasted_iota(jnp.int32, (slots, slots), 0)
        < lax.broadcasted_iota(jnp.int32, (slots, slots), 1),
        1.0,
        0.0,
    ).astype(bf16)
    half = (lax.broadcasted_iota(jnp.int32, (8, slots), 1) // 8) % 2
    which = lax.broadcasted_iota(jnp.int32, (8, slots), 0)
    clip = core + (which % 2) - 2 * core * (which % 2)
    first = jnp.where(lax.broadcasted_iota(jnp.int32, (16, 128), 1) == 0, 1.0, 0.0).astype(bf16)
    rows, values = [], jnp.zeros((8, slots), f32)
    for i, r in enumerate(ORDER):
        rows.append(arrived[(frame + 4 - r) % 4])
        values = jnp.where(which // 2 == i, dot(first, rows[i], NT)[:8], values)
    mine = jnp.where((values < 32.0) & (half == clip), 1.0, 0.0)
    doubled = jnp.concatenate([mine, mine], axis=0).astype(bf16)
    rank = jnp.where(mine > 0.5, dot(doubled, before)[:8], -1.0)
    line = lax.broadcasted_iota(jnp.int32, (128, slots), 0).astype(f32)
    for b in range(8):
        pick = jnp.where(rank[b : b + 1] == line, 1.0, 0.0).astype(bf16)
        pairs[b] = dot(pick, rows[b // 2]).astype(bf16)


def lanes(i, other):
    return slice((2 * i + other) * 128, (2 * i + other) * 128 + 128)


def forward_kernel(act_own, act_theirs, sides, sides_theirs, *refs):
    pairs, w_embed, gain, w_t_far, head_t, mix_t = refs[:6]
    normed_far, proj_far, probs, part_own, part_other = refs[6:11]
    act, w_t, normed, proj, rest, digits, sems, arrive = refs[11:]
    attended = proj.at[768:1024]
    loads = []
    for i in range(4):
        for other, (first, later) in enumerate(((act_own, sides), (act_theirs, sides_theirs))):
            source = first if i == 0 else later.at[pl.ds((i - 1) * 128, 128)]
            loads.append(pltpu.make_async_copy(source, act.at[2 * i + other], arrive.at[2 * i + other]))
            loads[-1].start()
    times = [
        pltpu.make_async_copy(source.at[pl.ds(384, 16), pl.ds(0, 128)], digits.at[k], arrive.at[8 + k])
        for k, source in enumerate((sides, sides_theirs))
    ]
    for time in times:
        time.start()
    weights = pltpu.make_async_copy(w_t_far, w_t, sems.at[0])
    weights.start()
    moments = []
    for k, time in enumerate(times):
        time.wait()
        pair_of = digits[k].astype(f32)
        index = pair_of[0:1, 0:1] * 32.0 + pair_of[0:1, 1:2]
        moments.append(jnp.broadcast_to((index + 0.5) / TIMESTEPS, (128, 64)))
    for b in range(8):
        pair = pairs[b].astype(f32)
        t = moments[b % 2]
        noised = ((1.0 - t) * pair[:, :64] + t * pair[:, 64:]).astype(bf16)
        added = dot(noised, w_embed[...])
        loads[b].wait()
        hidden = act[b].astype(f32) + added
        scale = lax.rsqrt(jnp.mean(hidden * hidden, axis=1, keepdims=True) + 1e-06)
        normed[b * 128 : b * 128 + 128] = (hidden * scale * gain[...]).astype(bf16)
        if b == 0:
            turned = pair.T
            own = sum(dot(head_t[...], term, NT) for term in thirds(hidden))
            rest[...] = own - (turned[64:] - turned[:64])
    leave = [pltpu.make_async_copy(normed, normed_far, sems.at[1])]
    leave[0].start()
    weights.wait()
    for i in range(3):
        rows = slice(i * 256, i * 256 + 256)
        proj[rows] = dot(w_t[rows], normed[...], NT).astype(bf16)
    leave.append(pltpu.make_async_copy(proj.at[:768], proj_far.at[:768], sems.at[2]))
    leave[1].start()
    for h in range(2):
        for other in range(2):

            def read(j, f):
                row = h * 384 + j * 128
                return proj[row : row + 128, lanes(f, other)].astype(f32)

            keys = [read(1, g) for g in range(4)]
            values = [read(2, g) for g in range(4)]
            for f in range(4):
                query = read(0, f)
                scores = [jnp.sum(query * k, axis=0, keepdims=True) * INV_ROOT for k in keys]
                peak = jnp.maximum(jnp.maximum(scores[0], scores[1]), jnp.maximum(scores[2], scores[3]))
                powers = [jnp.exp(s - peak) for s in scores]
                whole = powers[0] + powers[1] + powers[2] + powers[3]
                prob = [p / whole for p in powers]
                rounded = [p.astype(bf16).astype(f32) for p in prob]
                out = rounded[0] * values[0]
                for g in range(1, 4):
                    out = out + rounded[g] * values[g]
                attended[h * 128 : h * 128 + 128, lanes(f, other)] = out.astype(bf16)
                for g in range(4):
                    probs[h * 2 + other, f * 4 + g : f * 4 + g + 1] = prob[g]
    leave.append(pltpu.make_async_copy(attended, proj_far.at[768:1024], sems.at[3]))
    leave[2].start()
    value = split_dot(mix_t[...], attended[...])
    for other, part in ((0, part_own), (1, part_other)):
        for f in range(4):
            added = rest[...] if other == 0 and f == 0 else 0.0
            part[:, f * 128 : f * 128 + 128] = value[:, lanes(f, other)] + added
    for copy in leave:
        copy.wait()


def gradient_piece(delta, normed, factor, h, block, out):
    columns = pl.ds(pl.multiple_of(block * 512, 512), 512)
    out[:384] = dot(delta[h * 384 : h * 384 + 384], normed[:, columns]).astype(bf16)
    for i in range(4):
        out[384:, i * 128 : i * 128 + 128] = factor[i * 16 : i * 16 + 16]


def backward_kernel(place, error_own, error_other, probs, mix, proj_far, normed_far, *refs):
    pieces = refs[:8]
    delta, own_factor, slope, grad, proj, normed, sems = refs[8:]
    attended = proj.at[768:1024]
    loads = [
        pltpu.make_async_copy(far, near, sems.at[k])
        for k, (far, near) in enumerate(((proj_far, proj), (normed_far, normed)))
    ]
    for load in loads:
        load.start()
    for i in range(4):
        for other, error in ((0, error_own), (1, error_other)):
            slope[:, lanes(i, other)] = error[:, i * 128 : i * 128 + 128] * (2.0 / 32.0)
    grad[...] = dot(mix[...], slope[...], NN, HIGHEST)
    loads[0].wait()
    for h in range(2):
        for other in range(2):

            def read(j, f):
                row = h * 384 + j * 128
                return proj[row : row + 128, lanes(f, other)].astype(f32)

            def prob(f, g):
                return probs[h * 2 + other, f * 4 + g : f * 4 + g + 1]

            grads = [grad[h * 128 : h * 128 + 128, lanes(f, other)] for f in range(4)]
            score = [[None] * 4 for _ in range(4)]
            for f in range(4):
                dprob = [jnp.sum(grads[f] * read(2, g), axis=0, keepdims=True) for g in range(4)]
                mean = sum(dprob[g] * prob(f, g) for g in range(4))
                for g in range(4):
                    score[f][g] = prob(f, g) * (dprob[g] - mean) * INV_ROOT
            for g in range(4):
                value = sum(prob(f, g).astype(bf16).astype(f32) * grads[f] for f in range(4))
                query = sum(score[g][i] * read(1, i) for i in range(4))
                key = sum(score[f][g] * read(0, f) for f in range(4))
                for j, out in enumerate((query, key, value)):
                    row = h * 384 + j * 128
                    delta[row : row + 128, lanes(g, other)] = out.astype(bf16)
    factor = split_dot(slope[...], attended[...], NT)
    for h in range(2):
        own_factor[h] = factor[:, h * 128 : h * 128 + 128].astype(bf16)
    loads[1].wait()
    for (h, o), out in zip(PIECES, pieces):
        gradient_piece(delta, normed, own_factor[h], h, (place[h] + o) % 4, out)


def add_first_kernel(place, *refs):
    both = refs[16]
    for h in range(2):
        parts, outs = refs[h:8:2], refs[8 + 4 * h : 12 + 4 * h]
        total = parts[0][...].astype(f32)
        for part in parts[1:]:
            total = total + part[...].astype(f32)
        both[...] = total.astype(bf16)
        for o, out in enumerate(outs):
            columns = pl.ds(pl.multiple_of(((place[1 - h] + o) % 4) * 128, 128), 128)
            out[:384] = both[:384, columns]
            for i in range(4):
                out[384 + i * 16 : 400 + i * 16] = both[384:, i * 128 : i * 128 + 128]


def add_second_kernel(*refs):
    factor = refs[10]
    for h in range(2):
        parts, owned = refs[h:8:2], refs[8 + h]
        total = parts[0][...].astype(f32)
        for part in parts[1:]:
            total = total + part[...].astype(f32)
        for j in range(3):
            owned[j] = total[j * 128 : j * 128 + 128].T.astype(bf16)
        factor[h * 128 : h * 128 + 128] = total[384:].T.astype(bf16)


def line_kernel(*refs):
    for h in range(2):
        for k, o in enumerate((3, 1, 2, 0)):
            refs[8 + h][o] = refs[2 * k + h][...]


def first_join_kernel(a, b, c, line, factor, out):
    for k, ref in enumerate((a, b, c, line)):
        out[k] = ref[...]
    out[4, 0] = jnp.zeros((3, 128, 128), bf16)
    for k in range(2):
        out[4, 0, k, :, :64] = factor[k * 128 : k * 128 + 128]
    for k in range(1, 4):
        out[4, k] = jnp.zeros((3, 128, 128), bf16)


def join_kernel(*refs):
    out = refs[-1]
    for k in range(out.shape[0]):
        out[k] = refs[k][...]


def assemble_kernel(tags, arrays, aliased, with_out, place, *refs):
    count = len(tags)
    sources, refs = refs[:arrays], refs[arrays + aliased :]
    if with_out:
        head_far, out, token, grad_out, held, ready, done, sems, whole, sent, factors, head_t = refs
        fetched = [pltpu.make_async_copy(head_far, head_t, sent.at[3])]
        fetched[0].start()
        for k, core in ((0, 1 - place[2]), (1, place[2])):
            target = factors.at[pl.ds(core * 2, 2)]
            fetched.append(pltpu.make_async_copy(sources[k].at[4, 0, 0:2], target, sent.at[1 + k]))
            fetched[k + 1].start()
    else:
        out, token, held, ready, done, sems = refs
    token[...] = jnp.zeros((8, 128), f32)
    loads = []
    for k, tag in enumerate(tags):
        source = sources[tag[0]] if tag[1] is None else sources[tag[0]].at[tag[1]]
        loads.append(pltpu.make_async_copy(source, held.at[k], sems.at[k]))
        loads[-1].start()
    if with_out:
        for copy in fetched:
            copy.wait()
        for k in range(4):
            whole[k * 128 : k * 128 + 128] = dot(factors[k, :, :64], head_t[...])
        leave = pltpu.make_async_copy(whole, grad_out, sent.at[0])
        leave.start()
    stores = []
    for k, tag in enumerate(tags):
        o, theirs, h, inners = tag[2:]
        loads[k].wait()
        first = (place[h] + 4 - o) % 4
        for i, inner in enumerate(inners):
            second = (place[1 - h] + 4 - inner) % 4
            ready[k, :, pl.ds(pl.multiple_of(second * 128, 128), 128)] = held[k, i].astype(f32)
        core = place[2] if theirs == 0 else 1 - place[2]
        stores.append(
            pltpu.make_async_copy(
                ready.at[k],
                out.at[
                    :,
                    pl.ds(pl.multiple_of(first * 512, 512), 512),
                    pl.ds(pl.multiple_of(core * 256 + h * 128, 128), 128),
                ],
                done.at[k],
            )
        )
        stores[k].start()
    for store in stores:
        store.wait()
    if with_out:
        leave.wait()


def assemble(place, arrays, tags, onto=None, product=()):
    tags = tuple(sorted(tags, key=lambda t: t[2:]))
    given = [] if onto is None else [onto]
    out_shape = [shape((3, 2048, 512), f32), shape((8, 128), f32)]
    out_specs = [HBM, VMEM]
    dma = pltpu.SemaphoreType.DMA
    scratch = [
        pltpu.VMEM((len(tags), *arrays[0].shape[-4:]), bf16),
        pltpu.VMEM((len(tags), 3, 512, 128), f32),
        dma((len(tags),)),
        dma((len(tags),)),
    ]
    if product:
        out_shape.append(shape((512, 2048), f32))
        out_specs.append(HBM)
        scratch += [pltpu.VMEM((512, 2048), f32), dma((4,)), pltpu.VMEM((4, 128, 128), bf16)]
        scratch.append(pltpu.VMEM((64, 2048), bf16))
    return pl.pallas_call(
        functools.partial(assemble_kernel, tags, len(arrays), len(given), bool(product)),
        in_specs=[SMEM] + [ANY] * len(arrays) + [HBM] * (len(given) + len(product)),
        out_specs=out_specs,
        out_shape=out_shape,
        scratch_shapes=scratch,
        input_output_aliases={1 + len(arrays): 0} if given else {},
        compiler_params=params(20),
        cost_estimate=TINY,
    )(place, *arrays, *given, *product)


def call(kernel, out, *operands, scratch=(), mib=8):
    result = pl.pallas_call(
        kernel,
        in_specs=[spec for spec, _ in operands],
        out_specs=[spec for spec, _ in out],
        out_shape=[made for _, made in out],
        scratch_shapes=list(scratch),
        compiler_params=params(mib),
        cost_estimate=TINY,
    )(*(array for _, array in operands))
    return result


def near(*arrays):
    return [(VMEM, a) for a in arrays]


def far(*arrays):
    return [(HBM, a) for a in arrays]


def shards(act, cache_rows, row_dest, time_index, w_embed, norm_gain, w_qkv, w_out, w_head):
    x, y, core, frame = (lax.axis_index(a).astype(jnp.int32) for a in ("x", "y", "core", "frame"))
    here = (SMEM, jnp.stack([frame, core]))
    square = (SMEM, jnp.stack([x, y, core]))
    dma = pltpu.SemaphoreType.DMA

    before, after, across = (shift(act, "frame", o) for o in (1, 3, 2))
    act_theirs = shift(act, "core", 1)
    head_t = w_head.T
    w_t, mix, mix_t = call(
        prepare_kernel,
        far(shape((768, 2048), bf16)) + near(shape((256, 64), f32), shape((64, 256), f32)),
        here, *far(w_qkv, w_out), *near(head_t),
        scratch=[
            pltpu.VMEM((3, 2048, 256), bf16),
            pltpu.VMEM((256, 2048), bf16),
            pltpu.VMEM((6, 128, 2048), bf16),
            dma((4,)),
            dma((6,)),
        ],
        mib=LARGE,
    )
    (sent,) = call(
        bucket_kernel, near(shape((4, 16, 2, 16, 128), bf16)),
        *far(cache_rows, row_dest.reshape(1, 128)), (ANY, mix),
        scratch=[pltpu.VMEM((128, 128), bf16), pltpu.VMEM((1, 128), jnp.int32), dma((2,))],
        mib=LARGE,
    )
    arrived = lax.all_to_all(
        sent.reshape(128, 16, 128), ("frame", "y", "x", "core"), 0, 0, tiled=True
    ).reshape(4, 512, 128)
    (sides,) = call(
        sides_kernel, near(shape((400, 2048), bf16)), (SMEM, time_index), *near(before, across, after), (ANY, arrived)
    )
    sides_theirs = shift(sides, "core", 1)
    (pairs,) = call(fetch_kernel, near(shape((8, 128, 128), bf16)), here, *near(arrived))
    normed, proj, probs, part_own, part_other = call(
        forward_kernel,
        far(shape((1024, 2048), bf16), shape((1024, 1024), bf16))
        + near(shape((4, 16, 128), f32), shape((64, 512), f32), shape((64, 512), f32)),
        *((ANY, a) for a in (act, act_theirs, sides, sides_theirs)),
        *near(pairs, w_embed, norm_gain.reshape(1, 2048)), *far(w_t), *near(head_t, mix_t),
        scratch=[
            pltpu.VMEM((8, 128, 2048), bf16),
            pltpu.VMEM((768, 2048), bf16),
            pltpu.VMEM((1024, 2048), bf16),
            pltpu.VMEM((1024, 1024), bf16),
            pltpu.VMEM((64, 128), f32),
            pltpu.VMEM((2, 16, 128), bf16),
            dma((4,)),
            dma((10,)),
        ],
        mib=LARGE,
    )

    clip_part = part_own + shift(part_other, "core", 1)
    heard = {0: clip_part, **{o: shift(clip_part, "frame", o) for o in (2, 1, 3)}}
    error_own = jnp.concatenate(
        [
            sum(
                heard[o][:, SPOT[(r - o) % 4] * 128 : SPOT[(r - o) % 4] * 128 + 128]
                for o in range(4)
            )
            for r in ORDER
        ],
        axis=1,
    )
    frame_loss = jnp.mean(error_own[:, :128] * error_own[:, :128]).reshape(1, 1)
    error_other = shift(error_own, "core", 1)

    piece = shape((400, 512), bf16)
    small = shape((448, 128), bf16)
    block = shape((3, 128, 128), bf16)
    line = shape((4, 3, 128, 128), bf16)
    axes = (("x", "y"), ("y", "x"))
    reach = (3, 1, 2)
    pieces = call(
        backward_kernel,
        near(*[piece] * 8),
        square, *near(error_own, error_other, probs, mix), *far(proj, normed),
        scratch=[
            pltpu.VMEM((768, 1024), bf16),
            pltpu.VMEM((2, 64, 128), bf16),
            pltpu.VMEM((64, 1024), f32),
            pltpu.VMEM((256, 1024), f32),
            pltpu.VMEM((1024, 1024), bf16),
            pltpu.VMEM((1024, 2048), bf16),
            dma((2,)),
        ],
        mib=49,
    )
    moved = [shift(p, axes[h][0], o) for (h, o), p in zip(PIECES[:6], pieces)]
    second = call(
        add_first_kernel, near(*[small] * 8), square, *near(*moved, *pieces[6:]),
        scratch=[pltpu.VMEM((400, 512), bf16)],
    )
    moved = [shift(second[h * 4 + o], axes[h][1], o) for h, o in PIECES[:6]]
    *owned, factor = call(
        add_second_kernel, near(block, block, shape((256, 64), bf16)),
        *near(*moved, second[0], second[4]),
    )
    back = [shift(owned[h], axes[h][1], o) for o in reach for h in range(2)]
    lines = call(
        line_kernel, near(line, line), *near(*back, *owned),
    )
    every = (0, 1, 2, 3)
    wide = [[shift(lines[h], axes[h][0], o) for o in reach] for h in range(2)]
    (half_x,) = call(
        first_join_kernel, near(shape((5, 4, 3, 128, 128), bf16)),
        *near(*wide[0], lines[0], factor),
    )
    half_x_theirs = shift(half_x, "core", 1)

    def tagged(array, side, h, distances):
        return [(array, k, o, side, h, every) for k, o in enumerate(distances)]

    grad_qkv, token = assemble(
        square[1], (half_x, lines[1]), tagged(0, 0, 0, (*reach, 0)) + [(1, None, 0, 0, 1, every)]
    )
    (half_y,) = call(
        join_kernel, near(shape((4, 4, 3, 128, 128), bf16)), *near(*wide[1], lines[1], token)
    )
    half_y_theirs = shift(half_y, "core", 1)
    grad_qkv, token, grad_out = assemble(
        square[1], (half_x_theirs, half_x, half_y),
        tagged(0, 1, 0, (*reach, 0)) + tagged(2, 0, 1, reach), grad_qkv, (head_t,),
    )
    grad_qkv, token = assemble(square[1], (half_y_theirs,), tagged(0, 1, 1, (*reach, 0)), grad_qkv)
    return frame_loss, grad_qkv, grad_out


def solution(mesh):
    fine = Mesh(mesh.devices.reshape(4, 4, 2, 4), ("y", "x", "core", "frame"))
    store = ("y", "x", "core")
    in_specs = (
        P((*store, "frame"), None),
        P((*store, "frame"), None),
        P((*store, "frame")),
        P(store),
        P(),
        P(),
        P(None, None, "frame"),
        P("frame", None),
        P(),
    )
    out_specs = (P(store, "frame"), P(None, None, "frame"), P("frame", None))
    return jax.shard_map(shards, mesh=fine, in_specs=in_specs, out_specs=out_specs, check_vma=False)
```

```python
import functools
import math

import jax
import jax.numpy as jnp
from jax import lax
from jax.experimental import pallas as pl
from jax.experimental.pallas import tpu as pltpu
from jax.sharding import Mesh, PartitionSpec as P

HEAD_DIM = 128
TIMESTEPS = 1000
UNUSED = 64.0
NEAR = ((0, 1), (0, 3), (1, 1), (1, 3))
PIECES = ((0, 2), (1, 2), (0, 1), (1, 1), (0, 3), (1, 3), (0, 0), (1, 0))
f32 = jnp.float32
bf16 = jnp.bfloat16
HIGHEST = lax.Precision.HIGHEST
INV_ROOT = 1.0 / math.sqrt(HEAD_DIM)
NN = (((1,), (0,)), ((), ()))
NT = (((1,), (1,)), ((), ()))
TN = (((0,), (0,)), ((), ()))
ORDER = (0, 1, 3, 2)
SPOT = {r: i for i, r in enumerate(ORDER)}
VMEM = pl.BlockSpec(memory_space=pltpu.VMEM)
SMEM = pl.BlockSpec(memory_space=pltpu.SMEM)
HBM = pl.BlockSpec(memory_space=pltpu.HBM)
ANY = pl.BlockSpec(memory_space=pl.ANY)


LARGE = 52


def params(mib):
    return pltpu.CompilerParams(vmem_limit_bytes=mib << 20)


def cost(flops, moved):
    return pl.CostEstimate(flops=flops, bytes_accessed=moved, transcendentals=0)


TINY = cost(0, 1024)


def dot(a, b, dims=NN, precision=None):
    return lax.dot_general(a, b, dims, preferred_element_type=f32, precision=precision)


def thirds(value):
    high = value.astype(bf16)
    left = value - high.astype(f32)
    middle = left.astype(bf16)
    return high, middle, (left - middle.astype(f32)).astype(bf16)


def split_dot(value, exact, dims=NN):
    rows = value.shape[0]
    out = dot(jnp.concatenate(thirds(value), axis=0), exact, dims)
    return out[:rows] + out[rows : 2 * rows] + out[2 * rows :]


def shift(value, axis, offset):
    size = lax.axis_size(axis)
    return lax.ppermute(value, axis, [(i, (i + offset) % size) for i in range(size)])


def shape(dims, kind):
    return jax.ShapeDtypeStruct(dims, kind)


def bucket_kernel(rows_far, dest_far, unused, out, rows, dest_row, sems):
    loads = [
        pltpu.make_async_copy(rows_far, rows, sems.at[0]),
        pltpu.make_async_copy(dest_far, dest_row, sems.at[1]),
    ]
    for load in loads:
        load.start()
    for load in loads:
        load.wait()
    dest_col = jnp.broadcast_to(dest_row[...].astype(f32), (128, 128)).T
    earlier = lax.broadcasted_iota(jnp.int32, (128, 128), 0) < lax.broadcasted_iota(
        jnp.int32, (128, 128), 1
    )
    same = jnp.where((dest_col == dest_row[...].astype(f32)) & earlier, 1.0, 0.0)
    slot = dest_row[...] * 8 + jnp.sum(same, axis=0, keepdims=True).astype(jnp.int32)
    hot = jnp.where(lax.broadcasted_iota(jnp.int32, (256, 128), 0) == slot, 1.0, 0.0)
    used = jnp.max(hot, axis=1, keepdims=True)
    moved = dot(hot.astype(bf16), rows[...]) + (1.0 - used) * UNUSED
    bucket = moved.astype(bf16).reshape(16, 16, 128)
    for frame in range(4):
        for core in range(2):
            out[frame, :, core] = bucket


def prepare_kernel(place, w, w_out, head_t, w_t, mix, mix_t, held, out_rows, turned, sems, leave):
    start = pl.multiple_of(place[1] * 256, 256)
    loads = [
        pltpu.make_async_copy(w.at[j, :, pl.ds(start, 256)], held.at[j], sems.at[j]) for j in range(3)
    ]
    loads.append(pltpu.make_async_copy(w_out.at[pl.ds(start, 256)], out_rows, sems.at[3]))
    for load in loads:
        load.start()
    stores = []
    for j in range(3):
        loads[j].wait()
        for h in range(2):
            k = h * 3 + j
            turned[k] = held[j, :, h * 128 : h * 128 + 128].T
            stores.append(pltpu.make_async_copy(turned.at[k], w_t.at[pl.ds(k * 128, 128)], leave.at[k]))
            stores[-1].start()
    loads[3].wait()
    mix[...] = dot(out_rows[...], head_t[...], NT)
    mix_t[...] = dot(head_t[...], out_rows[...], NT)
    for store in stores:
        store.wait()


def sides_kernel(time, before, across, after, unused, both):
    both[:128] = before[...]
    both[128:256] = after[...]
    both[256:384] = across[...]
    column = lax.broadcasted_iota(jnp.int32, (16, 2048), 1)
    digits = jnp.where(column == 0, time[0] // 32, jnp.where(column == 1, time[0] % 32, 0))
    both[384:] = digits.astype(f32).astype(bf16)


def fetch_kernel(place, arrived, pairs):
    frame, core = place[0], place[1]
    slots = 512
    before = jnp.where(
        lax.broadcasted_iota(jnp.int32, (slots, slots), 0)
        < lax.broadcasted_iota(jnp.int32, (slots, slots), 1),
        1.0,
        0.0,
    ).astype(bf16)
    half = (lax.broadcasted_iota(jnp.int32, (8, slots), 1) // 8) % 2
    which = lax.broadcasted_iota(jnp.int32, (8, slots), 0)
    clip = core + (which % 2) - 2 * core * (which % 2)
    first = jnp.where(lax.broadcasted_iota(jnp.int32, (16, 128), 1) == 0, 1.0, 0.0).astype(bf16)
    rows, values = [], jnp.zeros((8, slots), f32)
    for i, r in enumerate(ORDER):
        rows.append(arrived[(frame + 4 - r) % 4])
        values = jnp.where(which // 2 == i, dot(first, rows[i], NT)[:8], values)
    mine = jnp.where((values < 32.0) & (half == clip), 1.0, 0.0)
    doubled = jnp.concatenate([mine, mine], axis=0).astype(bf16)
    rank = jnp.where(mine > 0.5, dot(doubled, before)[:8], -1.0)
    line = lax.broadcasted_iota(jnp.int32, (128, slots), 0).astype(f32)
    for b in range(8):
        pick = jnp.where(rank[b : b + 1] == line, 1.0, 0.0).astype(bf16)
        pairs[b] = dot(pick, rows[b // 2]).astype(bf16)


def lanes(i, other):
    return slice((2 * i + other) * 128, (2 * i + other) * 128 + 128)


def forward_kernel(act_own, act_theirs, sides, sides_theirs, *refs):
    pairs, w_embed, gain, w_t_far, head_t, mix_t = refs[:6]
    normed_far, proj_far, probs, part_own, part_other = refs[6:11]
    act, w_t, normed, proj, rest, digits, sems, arrive = refs[11:]
    attended = proj.at[768:1024]
    loads = []
    for i in range(4):
        for other, (first, later) in enumerate(((act_own, sides), (act_theirs, sides_theirs))):
            source = first if i == 0 else later.at[pl.ds((i - 1) * 128, 128)]
            loads.append(pltpu.make_async_copy(source, act.at[2 * i + other], arrive.at[2 * i + other]))
            loads[-1].start()
    times = [
        pltpu.make_async_copy(source.at[pl.ds(384, 16), pl.ds(0, 128)], digits.at[k], arrive.at[8 + k])
        for k, source in enumerate((sides, sides_theirs))
    ]
    for time in times:
        time.start()
    weights = pltpu.make_async_copy(w_t_far, w_t, sems.at[0])
    weights.start()
    moments = []
    for k, time in enumerate(times):
        time.wait()
        pair_of = digits[k].astype(f32)
        index = pair_of[0:1, 0:1] * 32.0 + pair_of[0:1, 1:2]
        moments.append(jnp.broadcast_to((index + 0.5) / TIMESTEPS, (128, 64)))
    for b in range(8):
        pair = pairs[b].astype(f32)
        t = moments[b % 2]
        noised = ((1.0 - t) * pair[:, :64] + t * pair[:, 64:]).astype(bf16)
        added = dot(noised, w_embed[...])
        loads[b].wait()
        hidden = act[b].astype(f32) + added
        scale = lax.rsqrt(jnp.mean(hidden * hidden, axis=1, keepdims=True) + 1e-06)
        normed[b * 128 : b * 128 + 128] = (hidden * scale * gain[...]).astype(bf16)
        if b == 0:
            turned = pair.T
            own = sum(dot(head_t[...], term, NT) for term in thirds(hidden))
            rest[...] = own - (turned[64:] - turned[:64])
    leave = [pltpu.make_async_copy(normed, normed_far, sems.at[1])]
    leave[0].start()
    weights.wait()
    for i in range(3):
        rows = slice(i * 256, i * 256 + 256)
        proj[rows] = dot(w_t[rows], normed[...], NT).astype(bf16)
    leave.append(pltpu.make_async_copy(proj.at[:768], proj_far.at[:768], sems.at[2]))
    leave[1].start()
    for h in range(2):
        for other in range(2):

            def read(j, f):
                row = h * 384 + j * 128
                return proj[row : row + 128, lanes(f, other)].astype(f32)

            keys = [read(1, g) for g in range(4)]
            values = [read(2, g) for g in range(4)]
            for f in range(4):
                query = read(0, f)
                scores = [jnp.sum(query * k, axis=0, keepdims=True) * INV_ROOT for k in keys]
                peak = jnp.maximum(jnp.maximum(scores[0], scores[1]), jnp.maximum(scores[2], scores[3]))
                powers = [jnp.exp(s - peak) for s in scores]
                whole = powers[0] + powers[1] + powers[2] + powers[3]
                prob = [p / whole for p in powers]
                rounded = [p.astype(bf16).astype(f32) for p in prob]
                out = rounded[0] * values[0]
                for g in range(1, 4):
                    out = out + rounded[g] * values[g]
                attended[h * 128 : h * 128 + 128, lanes(f, other)] = out.astype(bf16)
                for g in range(4):
                    probs[h * 2 + other, f * 4 + g : f * 4 + g + 1] = prob[g]
    leave.append(pltpu.make_async_copy(attended, proj_far.at[768:1024], sems.at[3]))
    leave[2].start()
    value = split_dot(mix_t[...], attended[...])
    for other, part in ((0, part_own), (1, part_other)):
        for f in range(4):
            added = rest[...] if other == 0 and f == 0 else 0.0
            part[:, f * 128 : f * 128 + 128] = value[:, lanes(f, other)] + added
    for copy in leave:
        copy.wait()


def error_kernel(own, three, one, two, error, loss):
    heard = (own, one, two, three)
    for i, r in enumerate(ORDER):
        total = heard[0][:, i * 128 : i * 128 + 128]
        for o in range(1, 4):
            spot = SPOT[(r - o) % 4]
            total = total + heard[o][:, spot * 128 : spot * 128 + 128]
        error[:, i * 128 : i * 128 + 128] = total
        if r == 0:
            rows = jnp.sum(total * total, axis=1, keepdims=True)
            loss[...] = jnp.sum(rows, axis=0, keepdims=True) / total.size


def gradient_piece(delta, normed, factor, h, block, out):
    columns = pl.ds(pl.multiple_of(block * 512, 512), 512)
    out[:384] = dot(delta[h * 384 : h * 384 + 384], normed[:, columns]).astype(bf16)
    for i in range(4):
        out[384:, i * 128 : i * 128 + 128] = factor[i * 16 : i * 16 + 16]


def backward_kernel(place, error_own, error_other, probs, mix, proj_far, normed_far, *refs):
    pieces = refs[:8]
    delta, own_factor, slope, grad, proj, normed, sems = refs[8:]
    attended = proj.at[768:1024]
    loads = [
        pltpu.make_async_copy(far, near, sems.at[k])
        for k, (far, near) in enumerate(((proj_far, proj), (normed_far, normed)))
    ]
    for load in loads:
        load.start()
    for i in range(4):
        for other, error in ((0, error_own), (1, error_other)):
            slope[:, lanes(i, other)] = error[:, i * 128 : i * 128 + 128] * (2.0 / 32.0)
    grad[...] = dot(mix[...], slope[...], NN, HIGHEST)
    loads[0].wait()
    for h in range(2):
        for other in range(2):

            def read(j, f):
                row = h * 384 + j * 128
                return proj[row : row + 128, lanes(f, other)].astype(f32)

            def prob(f, g):
                return probs[h * 2 + other, f * 4 + g : f * 4 + g + 1]

            grads = [grad[h * 128 : h * 128 + 128, lanes(f, other)] for f in range(4)]
            score = [[None] * 4 for _ in range(4)]
            for f in range(4):
                dprob = [jnp.sum(grads[f] * read(2, g), axis=0, keepdims=True) for g in range(4)]
                mean = sum(dprob[g] * prob(f, g) for g in range(4))
                for g in range(4):
                    score[f][g] = prob(f, g) * (dprob[g] - mean) * INV_ROOT
            for g in range(4):
                value = sum(prob(f, g).astype(bf16).astype(f32) * grads[f] for f in range(4))
                query = sum(score[g][i] * read(1, i) for i in range(4))
                key = sum(score[f][g] * read(0, f) for f in range(4))
                for j, out in enumerate((query, key, value)):
                    row = h * 384 + j * 128
                    delta[row : row + 128, lanes(g, other)] = out.astype(bf16)
    factor = split_dot(slope[...], attended[...], NT)
    for h in range(2):
        own_factor[h] = factor[:, h * 128 : h * 128 + 128].astype(bf16)
    loads[1].wait()
    for (h, o), out in zip(PIECES, pieces):
        gradient_piece(delta, normed, own_factor[h], h, (place[h] + o) % 4, out)


def add_first_kernel(place, *refs):
    both = refs[16]
    for h in range(2):
        parts, outs = refs[h:8:2], refs[8 + 4 * h : 12 + 4 * h]
        total = parts[0][...].astype(f32)
        for part in parts[1:]:
            total = total + part[...].astype(f32)
        both[...] = total.astype(bf16)
        for o, out in enumerate(outs):
            columns = pl.ds(pl.multiple_of(((place[1 - h] + o) % 4) * 128, 128), 128)
            out[:384] = both[:384, columns]
            for i in range(4):
                out[384 + i * 16 : 400 + i * 16] = both[384:, i * 128 : i * 128 + 128]


def add_second_kernel(*refs):
    factor = refs[10]
    for h in range(2):
        parts, owned = refs[h:8:2], refs[8 + h]
        total = parts[0][...].astype(f32)
        for part in parts[1:]:
            total = total + part[...].astype(f32)
        for j in range(3):
            owned[j] = total[j * 128 : j * 128 + 128].T.astype(bf16)
        factor[h * 128 : h * 128 + 128] = total[384:].T.astype(bf16)


def line_kernel(*refs):
    for h in range(2):
        for k, o in enumerate((3, 1, 2, 0)):
            refs[8 + h][o] = refs[2 * k + h][...]


def first_join_kernel(a, b, c, line, factor, out):
    for k, ref in enumerate((a, b, c, line)):
        out[k] = ref[...]
    out[4, 0] = jnp.zeros((3, 128, 128), bf16)
    for k in range(2):
        out[4, 0, k, :, :64] = factor[k * 128 : k * 128 + 128]
    for k in range(1, 4):
        out[4, k] = jnp.zeros((3, 128, 128), bf16)


def join_kernel(*refs):
    out = refs[-1]
    for k in range(out.shape[0]):
        out[k] = refs[k][...]


def assemble_kernel(tags, arrays, aliased, with_out, place, *refs):
    count = len(tags)
    sources, refs = refs[:arrays], refs[arrays + aliased :]
    if with_out:
        head_far, out, token, grad_out, held, ready, done, sems, whole, sent, factors, head_t = refs
        fetched = [pltpu.make_async_copy(head_far, head_t, sent.at[3])]
        fetched[0].start()
        for k, core in ((0, 1 - place[2]), (1, place[2])):
            target = factors.at[pl.ds(core * 2, 2)]
            fetched.append(pltpu.make_async_copy(sources[k].at[4, 0, 0:2], target, sent.at[1 + k]))
            fetched[k + 1].start()
    else:
        out, token, held, ready, done, sems = refs
    token[...] = jnp.zeros((8, 128), f32)
    loads = []
    for k, tag in enumerate(tags):
        source = sources[tag[0]] if tag[1] is None else sources[tag[0]].at[tag[1]]
        loads.append(pltpu.make_async_copy(source, held.at[k], sems.at[k]))
        loads[-1].start()
    if with_out:
        for copy in fetched:
            copy.wait()
        for k in range(4):
            whole[k * 128 : k * 128 + 128] = dot(factors[k, :, :64], head_t[...])
        leave = pltpu.make_async_copy(whole, grad_out, sent.at[0])
        leave.start()
    stores = []
    for k, tag in enumerate(tags):
        o, theirs, h, inners = tag[2:]
        loads[k].wait()
        first = (place[h] + 4 - o) % 4
        for i, inner in enumerate(inners):
            second = (place[1 - h] + 4 - inner) % 4
            ready[k, :, pl.ds(pl.multiple_of(second * 128, 128), 128)] = held[k, i].astype(f32)
        core = place[2] if theirs == 0 else 1 - place[2]
        stores.append(
            pltpu.make_async_copy(
                ready.at[k],
                out.at[
                    :,
                    pl.ds(pl.multiple_of(first * 512, 512), 512),
                    pl.ds(pl.multiple_of(core * 256 + h * 128, 128), 128),
                ],
                done.at[k],
            )
        )
        stores[k].start()
    for store in stores:
        store.wait()
    if with_out:
        leave.wait()


def assemble(place, arrays, tags, onto=None, product=()):
    tags = tuple(sorted(tags, key=lambda t: t[2:]))
    given = [] if onto is None else [onto]
    out_shape = [shape((3, 2048, 512), f32), shape((8, 128), f32)]
    out_specs = [HBM, VMEM]
    dma = pltpu.SemaphoreType.DMA
    scratch = [
        pltpu.VMEM((len(tags), *arrays[0].shape[-4:]), bf16),
        pltpu.VMEM((len(tags), 3, 512, 128), f32),
        dma((len(tags),)),
        dma((len(tags),)),
    ]
    if product:
        out_shape.append(shape((512, 2048), f32))
        out_specs.append(HBM)
        scratch += [pltpu.VMEM((512, 2048), f32), dma((4,)), pltpu.VMEM((4, 128, 128), bf16)]
        scratch.append(pltpu.VMEM((64, 2048), bf16))
    return pl.pallas_call(
        functools.partial(assemble_kernel, tags, len(arrays), len(given), bool(product)),
        in_specs=[SMEM] + [ANY] * len(arrays) + [HBM] * (len(given) + len(product)),
        out_specs=out_specs,
        out_shape=out_shape,
        scratch_shapes=scratch,
        input_output_aliases={1 + len(arrays): 0} if given else {},
        compiler_params=params(20),
        cost_estimate=TINY,
    )(place, *arrays, *given, *product)


def call(kernel, out, *operands, scratch=(), mib=8):
    result = pl.pallas_call(
        kernel,
        in_specs=[spec for spec, _ in operands],
        out_specs=[spec for spec, _ in out],
        out_shape=[made for _, made in out],
        scratch_shapes=list(scratch),
        compiler_params=params(mib),
        cost_estimate=TINY,
    )(*(array for _, array in operands))
    return result


def near(*arrays):
    return [(VMEM, a) for a in arrays]


def far(*arrays):
    return [(HBM, a) for a in arrays]


def shards(act, cache_rows, row_dest, time_index, w_embed, norm_gain, w_qkv, w_out, w_head):
    x, y, core, frame = (lax.axis_index(a).astype(jnp.int32) for a in ("x", "y", "core", "frame"))
    here = (SMEM, jnp.stack([frame, core]))
    square = (SMEM, jnp.stack([x, y, core]))
    dma = pltpu.SemaphoreType.DMA

    before, after, across = (shift(act, "frame", o) for o in (1, 3, 2))
    act_theirs = shift(act, "core", 1)
    head_t = w_head.T
    w_t, mix, mix_t = call(
        prepare_kernel,
        far(shape((768, 2048), bf16)) + near(shape((256, 64), f32), shape((64, 256), f32)),
        here, *far(w_qkv, w_out), *near(head_t),
        scratch=[
            pltpu.VMEM((3, 2048, 256), bf16),
            pltpu.VMEM((256, 2048), bf16),
            pltpu.VMEM((6, 128, 2048), bf16),
            dma((4,)),
            dma((6,)),
        ],
        mib=LARGE,
    )
    (sent,) = call(
        bucket_kernel, near(shape((4, 16, 2, 16, 128), bf16)),
        *far(cache_rows, row_dest.reshape(1, 128)), (ANY, mix),
        scratch=[pltpu.VMEM((128, 128), bf16), pltpu.VMEM((1, 128), jnp.int32), dma((2,))],
        mib=LARGE,
    )
    arrived = lax.all_to_all(
        sent.reshape(128, 16, 128), ("frame", "y", "x", "core"), 0, 0, tiled=True
    ).reshape(4, 512, 128)
    (sides,) = call(
        sides_kernel, near(shape((400, 2048), bf16)), (SMEM, time_index), *near(before, across, after), (ANY, arrived)
    )
    sides_theirs = shift(sides, "core", 1)
    (pairs,) = call(fetch_kernel, near(shape((8, 128, 128), bf16)), here, *near(arrived))
    normed, proj, probs, part_own, part_other = call(
        forward_kernel,
        far(shape((1024, 2048), bf16), shape((1024, 1024), bf16))
        + near(shape((4, 16, 128), f32), shape((64, 512), f32), shape((64, 512), f32)),
        *((ANY, a) for a in (act, act_theirs, sides, sides_theirs)),
        *near(pairs, w_embed, norm_gain.reshape(1, 2048)), *far(w_t), *near(head_t, mix_t),
        scratch=[
            pltpu.VMEM((8, 128, 2048), bf16),
            pltpu.VMEM((768, 2048), bf16),
            pltpu.VMEM((1024, 2048), bf16),
            pltpu.VMEM((1024, 1024), bf16),
            pltpu.VMEM((64, 128), f32),
            pltpu.VMEM((2, 16, 128), bf16),
            dma((4,)),
            dma((10,)),
        ],
        mib=LARGE,
    )

    clip_part = part_own + shift(part_other, "core", 1)
    error_own, frame_loss = call(
        error_kernel, near(shape((64, 512), f32), shape((1, 1), f32)),
        *near(clip_part, *(shift(clip_part, "frame", o) for o in (3, 1, 2))),
    )
    error_other = shift(error_own, "core", 1)

    piece = shape((400, 512), bf16)
    small = shape((448, 128), bf16)
    block = shape((3, 128, 128), bf16)
    line = shape((4, 3, 128, 128), bf16)
    axes = (("x", "y"), ("y", "x"))
    reach = (3, 1, 2)
    pieces = call(
        backward_kernel,
        near(*[piece] * 8),
        square, *near(error_own, error_other, probs, mix), *far(proj, normed),
        scratch=[
            pltpu.VMEM((768, 1024), bf16),
            pltpu.VMEM((2, 64, 128), bf16),
            pltpu.VMEM((64, 1024), f32),
            pltpu.VMEM((256, 1024), f32),
            pltpu.VMEM((1024, 1024), bf16),
            pltpu.VMEM((1024, 2048), bf16),
            dma((2,)),
        ],
        mib=49,
    )
    moved = [shift(p, axes[h][0], o) for (h, o), p in zip(PIECES[:6], pieces)]
    second = call(
        add_first_kernel, near(*[small] * 8), square, *near(*moved, *pieces[6:]),
        scratch=[pltpu.VMEM((400, 512), bf16)],
    )
    moved = [shift(second[h * 4 + o], axes[h][1], o) for h, o in PIECES[:6]]
    *owned, factor = call(
        add_second_kernel, near(block, block, shape((256, 64), bf16)),
        *near(*moved, second[0], second[4]),
    )
    back = [shift(owned[h], axes[h][1], o) for o in reach for h in range(2)]
    lines = call(
        line_kernel, near(line, line), *near(*back, *owned),
    )
    every = (0, 1, 2, 3)
    wide = [[shift(lines[h], axes[h][0], o) for o in reach] for h in range(2)]
    (half_x,) = call(
        first_join_kernel, near(shape((5, 4, 3, 128, 128), bf16)),
        *near(*wide[0], lines[0], factor),
    )
    half_x_theirs = shift(half_x, "core", 1)

    def tagged(array, side, h, distances):
        return [(array, k, o, side, h, every) for k, o in enumerate(distances)]

    grad_qkv, token = assemble(
        square[1], (half_x, lines[1]), tagged(0, 0, 0, (*reach, 0)) + [(1, None, 0, 0, 1, every)]
    )
    (half_y,) = call(
        join_kernel, near(shape((4, 4, 3, 128, 128), bf16)), *near(*wide[1], lines[1], token)
    )
    half_y_theirs = shift(half_y, "core", 1)
    grad_qkv, token, grad_out = assemble(
        square[1], (half_x_theirs, half_x, half_y),
        tagged(0, 1, 0, (*reach, 0)) + tagged(2, 0, 1, reach), grad_qkv, (head_t,),
    )
    grad_qkv, token = assemble(square[1], (half_y_theirs,), tagged(0, 1, 1, (*reach, 0)), grad_qkv)
    return frame_loss, grad_qkv, grad_out


def solution(mesh):
    fine = Mesh(mesh.devices.reshape(4, 4, 2, 4), ("y", "x", "core", "frame"))
    store = ("y", "x", "core")
    in_specs = (
        P((*store, "frame"), None),
        P((*store, "frame"), None),
        P((*store, "frame")),
        P(store),
        P(),
        P(),
        P(None, None, "frame"),
        P("frame", None),
        P(),
    )
    out_specs = (P(store, "frame"), P(None, None, "frame"), P("frame", None))
    return jax.shard_map(shards, mesh=fine, in_specs=in_specs, out_specs=out_specs, check_vma=False)
```

```python
import functools
import math

import jax
import jax.numpy as jnp
from jax import lax
from jax.experimental import pallas as pl
from jax.experimental.pallas import tpu as pltpu
from jax.sharding import Mesh, PartitionSpec as P

HEAD_DIM = 128
TIMESTEPS = 1000
UNUSED = 64.0
NEAR = ((0, 1), (0, 3), (1, 1), (1, 3))
PIECES = ((0, 2), (1, 2), (0, 1), (1, 1), (0, 3), (1, 3), (0, 0), (1, 0))
f32 = jnp.float32
bf16 = jnp.bfloat16
HIGHEST = lax.Precision.HIGHEST
INV_ROOT = 1.0 / math.sqrt(HEAD_DIM)
NN = (((1,), (0,)), ((), ()))
NT = (((1,), (1,)), ((), ()))
TN = (((0,), (0,)), ((), ()))
ORDER = (0, 1, 3, 2)
SPOT = {r: i for i, r in enumerate(ORDER)}
VMEM = pl.BlockSpec(memory_space=pltpu.VMEM)
SMEM = pl.BlockSpec(memory_space=pltpu.SMEM)
HBM = pl.BlockSpec(memory_space=pltpu.HBM)
ANY = pl.BlockSpec(memory_space=pl.ANY)


LARGE = 52


def params(mib):
    return pltpu.CompilerParams(vmem_limit_bytes=mib << 20)


def cost(flops, moved):
    return pl.CostEstimate(flops=flops, bytes_accessed=moved, transcendentals=0)


TINY = cost(0, 1024)


def dot(a, b, dims=NN, precision=None):
    return lax.dot_general(a, b, dims, preferred_element_type=f32, precision=precision)


def thirds(value):
    high = value.astype(bf16)
    left = value - high.astype(f32)
    middle = left.astype(bf16)
    return high, middle, (left - middle.astype(f32)).astype(bf16)


def split_dot(value, exact, dims=NN):
    rows = value.shape[0]
    out = dot(jnp.concatenate(thirds(value), axis=0), exact, dims)
    return out[:rows] + out[rows : 2 * rows] + out[2 * rows :]


def shift(value, axis, offset):
    size = lax.axis_size(axis)
    return lax.ppermute(value, axis, [(i, (i + offset) % size) for i in range(size)])


def shape(dims, kind):
    return jax.ShapeDtypeStruct(dims, kind)


def bucket_kernel(rows_far, dest_far, out, rows, dest_row, sems):
    loads = [
        pltpu.make_async_copy(rows_far, rows, sems.at[0]),
        pltpu.make_async_copy(dest_far, dest_row, sems.at[1]),
    ]
    for load in loads:
        load.start()
    for load in loads:
        load.wait()
    dest_col = jnp.broadcast_to(dest_row[...].astype(f32), (128, 128)).T
    earlier = lax.broadcasted_iota(jnp.int32, (128, 128), 0) < lax.broadcasted_iota(
        jnp.int32, (128, 128), 1
    )
    same = jnp.where((dest_col == dest_row[...].astype(f32)) & earlier, 1.0, 0.0)
    slot = dest_row[...] * 8 + jnp.sum(same, axis=0, keepdims=True).astype(jnp.int32)
    hot = jnp.where(lax.broadcasted_iota(jnp.int32, (256, 128), 0) == slot, 1.0, 0.0)
    used = jnp.max(hot, axis=1, keepdims=True)
    moved = dot(hot.astype(bf16), rows[...]) + (1.0 - used) * UNUSED
    bucket = moved.astype(bf16).reshape(16, 16, 128)
    for frame in range(4):
        for core in range(2):
            out[frame, :, core] = bucket


def prepare_kernel(place, w, w_out, head_t, w_t, mix, mix_t, held, out_rows, turned, sems, leave):
    start = pl.multiple_of(place[1] * 256, 256)
    loads = [
        pltpu.make_async_copy(w.at[j, :, pl.ds(start, 256)], held.at[j], sems.at[j]) for j in range(3)
    ]
    loads.append(pltpu.make_async_copy(w_out.at[pl.ds(start, 256)], out_rows, sems.at[3]))
    for load in loads:
        load.start()
    stores = []
    for j in range(3):
        loads[j].wait()
        for h in range(2):
            k = h * 3 + j
            turned[k] = held[j, :, h * 128 : h * 128 + 128].T
            stores.append(pltpu.make_async_copy(turned.at[k], w_t.at[pl.ds(k * 128, 128)], leave.at[k]))
            stores[-1].start()
    loads[3].wait()
    mix[...] = dot(out_rows[...], head_t[...], NT)
    mix_t[...] = dot(head_t[...], out_rows[...], NT)
    for store in stores:
        store.wait()


def sides_kernel(time, before, across, after, unused, both):
    both[:128] = before[...]
    both[128:256] = after[...]
    both[256:384] = across[...]
    column = lax.broadcasted_iota(jnp.int32, (16, 2048), 1)
    digits = jnp.where(column == 0, time[0] // 32, jnp.where(column == 1, time[0] % 32, 0))
    both[384:] = digits.astype(f32).astype(bf16)


def fetch_kernel(place, arrived, pairs):
    frame, core = place[0], place[1]
    slots = 512
    before = jnp.where(
        lax.broadcasted_iota(jnp.int32, (slots, slots), 0)
        < lax.broadcasted_iota(jnp.int32, (slots, slots), 1),
        1.0,
        0.0,
    ).astype(bf16)
    half = (lax.broadcasted_iota(jnp.int32, (8, slots), 1) // 8) % 2
    which = lax.broadcasted_iota(jnp.int32, (8, slots), 0)
    clip = core + (which % 2) - 2 * core * (which % 2)
    first = jnp.where(lax.broadcasted_iota(jnp.int32, (16, 128), 1) == 0, 1.0, 0.0).astype(bf16)
    rows, values = [], jnp.zeros((8, slots), f32)
    for i, r in enumerate(ORDER):
        rows.append(arrived[(frame + 4 - r) % 4])
        values = jnp.where(which // 2 == i, dot(first, rows[i], NT)[:8], values)
    mine = jnp.where((values < 32.0) & (half == clip), 1.0, 0.0)
    doubled = jnp.concatenate([mine, mine], axis=0).astype(bf16)
    rank = jnp.where(mine > 0.5, dot(doubled, before)[:8], -1.0)
    line = lax.broadcasted_iota(jnp.int32, (128, slots), 0).astype(f32)
    for b in range(8):
        pick = jnp.where(rank[b : b + 1] == line, 1.0, 0.0).astype(bf16)
        pairs[b] = dot(pick, rows[b // 2]).astype(bf16)


def lanes(i, other):
    return slice((2 * i + other) * 128, (2 * i + other) * 128 + 128)


def forward_kernel(act_own, act_theirs, sides, sides_theirs, *refs):
    pairs, w_embed, gain, w_t_far, head_t, mix_t = refs[:6]
    normed_far, proj_far, probs, part_own, part_other = refs[6:11]
    act, w_t, normed, proj, rest, digits, sems, arrive = refs[11:]
    attended = proj.at[768:1024]
    loads = []
    for i in range(4):
        for other, (first, later) in enumerate(((act_own, sides), (act_theirs, sides_theirs))):
            source = first if i == 0 else later.at[pl.ds((i - 1) * 128, 128)]
            loads.append(pltpu.make_async_copy(source, act.at[2 * i + other], arrive.at[2 * i + other]))
            loads[-1].start()
    times = [
        pltpu.make_async_copy(source.at[pl.ds(384, 16), pl.ds(0, 128)], digits.at[k], arrive.at[8 + k])
        for k, source in enumerate((sides, sides_theirs))
    ]
    for time in times:
        time.start()
    weights = pltpu.make_async_copy(w_t_far, w_t, sems.at[0])
    weights.start()
    moments = []
    for k, time in enumerate(times):
        time.wait()
        pair_of = digits[k].astype(f32)
        index = pair_of[0:1, 0:1] * 32.0 + pair_of[0:1, 1:2]
        moments.append(jnp.broadcast_to((index + 0.5) / TIMESTEPS, (128, 64)))
    for b in range(8):
        pair = pairs[b].astype(f32)
        t = moments[b % 2]
        noised = ((1.0 - t) * pair[:, :64] + t * pair[:, 64:]).astype(bf16)
        added = dot(noised, w_embed[...])
        loads[b].wait()
        hidden = act[b].astype(f32) + added
        scale = lax.rsqrt(jnp.mean(hidden * hidden, axis=1, keepdims=True) + 1e-06)
        normed[b * 128 : b * 128 + 128] = (hidden * scale * gain[...]).astype(bf16)
        if b == 0:
            turned = pair.T
            own = sum(dot(head_t[...], term, NT) for term in thirds(hidden))
            rest[...] = own - (turned[64:] - turned[:64])
    leave = [pltpu.make_async_copy(normed, normed_far, sems.at[1])]
    leave[0].start()
    weights.wait()
    for i in range(3):
        rows = slice(i * 256, i * 256 + 256)
        proj[rows] = dot(w_t[rows], normed[...], NT).astype(bf16)
    leave.append(pltpu.make_async_copy(proj.at[:768], proj_far.at[:768], sems.at[2]))
    leave[1].start()
    for h in range(2):
        for other in range(2):

            def read(j, f):
                row = h * 384 + j * 128
                return proj[row : row + 128, lanes(f, other)].astype(f32)

            keys = [read(1, g) for g in range(4)]
            values = [read(2, g) for g in range(4)]
            for f in range(4):
                query = read(0, f)
                scores = [jnp.sum(query * k, axis=0, keepdims=True) * INV_ROOT for k in keys]
                peak = jnp.maximum(jnp.maximum(scores[0], scores[1]), jnp.maximum(scores[2], scores[3]))
                powers = [jnp.exp(s - peak) for s in scores]
                whole = powers[0] + powers[1] + powers[2] + powers[3]
                prob = [p / whole for p in powers]
                rounded = [p.astype(bf16).astype(f32) for p in prob]
                out = rounded[0] * values[0]
                for g in range(1, 4):
                    out = out + rounded[g] * values[g]
                attended[h * 128 : h * 128 + 128, lanes(f, other)] = out.astype(bf16)
                for g in range(4):
                    probs[h * 2 + other, f * 4 + g : f * 4 + g + 1] = prob[g]
    leave.append(pltpu.make_async_copy(attended, proj_far.at[768:1024], sems.at[3]))
    leave[2].start()
    value = split_dot(mix_t[...], attended[...])
    for other, part in ((0, part_own), (1, part_other)):
        for f in range(4):
            added = rest[...] if other == 0 and f == 0 else 0.0
            part[:, f * 128 : f * 128 + 128] = value[:, lanes(f, other)] + added
    for copy in leave:
        copy.wait()


def error_kernel(own, three, one, two, error, loss):
    heard = (own, one, two, three)
    for i, r in enumerate(ORDER):
        total = heard[0][:, i * 128 : i * 128 + 128]
        for o in range(1, 4):
            spot = SPOT[(r - o) % 4]
            total = total + heard[o][:, spot * 128 : spot * 128 + 128]
        error[:, i * 128 : i * 128 + 128] = total
        if r == 0:
            rows = jnp.sum(total * total, axis=1, keepdims=True)
            loss[...] = jnp.sum(rows, axis=0, keepdims=True) / total.size


def gradient_piece(delta, normed, factor, h, block, out):
    columns = pl.ds(pl.multiple_of(block * 512, 512), 512)
    out[:384] = dot(delta[h * 384 : h * 384 + 384], normed[:, columns]).astype(bf16)
    for i in range(4):
        out[384:, i * 128 : i * 128 + 128] = factor[i * 16 : i * 16 + 16]


def backward_kernel(place, error_own, error_other, probs, mix, proj_far, normed_far, *refs):
    pieces = refs[:8]
    delta, own_factor, slope, grad, proj, normed, sems = refs[8:]
    attended = proj.at[768:1024]
    loads = [
        pltpu.make_async_copy(far, near, sems.at[k])
        for k, (far, near) in enumerate(((proj_far, proj), (normed_far, normed)))
    ]
    for load in loads:
        load.start()
    for i in range(4):
        for other, error in ((0, error_own), (1, error_other)):
            slope[:, lanes(i, other)] = error[:, i * 128 : i * 128 + 128] * (2.0 / 32.0)
    grad[...] = dot(mix[...], slope[...], NN, HIGHEST)
    loads[0].wait()
    for h in range(2):
        for other in range(2):

            def read(j, f):
                row = h * 384 + j * 128
                return proj[row : row + 128, lanes(f, other)].astype(f32)

            def prob(f, g):
                return probs[h * 2 + other, f * 4 + g : f * 4 + g + 1]

            grads = [grad[h * 128 : h * 128 + 128, lanes(f, other)] for f in range(4)]
            score = [[None] * 4 for _ in range(4)]
            for f in range(4):
                dprob = [jnp.sum(grads[f] * read(2, g), axis=0, keepdims=True) for g in range(4)]
                mean = sum(dprob[g] * prob(f, g) for g in range(4))
                for g in range(4):
                    score[f][g] = prob(f, g) * (dprob[g] - mean) * INV_ROOT
            for g in range(4):
                value = sum(prob(f, g).astype(bf16).astype(f32) * grads[f] for f in range(4))
                query = sum(score[g][i] * read(1, i) for i in range(4))
                key = sum(score[f][g] * read(0, f) for f in range(4))
                for j, out in enumerate((query, key, value)):
                    row = h * 384 + j * 128
                    delta[row : row + 128, lanes(g, other)] = out.astype(bf16)
    factor = split_dot(slope[...], attended[...], NT)
    for h in range(2):
        own_factor[h] = factor[:, h * 128 : h * 128 + 128].astype(bf16)
    loads[1].wait()
    for (h, o), out in zip(PIECES, pieces):
        gradient_piece(delta, normed, own_factor[h], h, (place[h] + o) % 4, out)


def add_first_kernel(place, *refs):
    both = refs[16]
    for h in range(2):
        parts, outs = refs[h:8:2], refs[8 + 4 * h : 12 + 4 * h]
        total = parts[0][...].astype(f32)
        for part in parts[1:]:
            total = total + part[...].astype(f32)
        both[...] = total.astype(bf16)
        for o, out in enumerate(outs):
            columns = pl.ds(pl.multiple_of(((place[1 - h] + o) % 4) * 128, 128), 128)
            out[:384] = both[:384, columns]
            for i in range(4):
                out[384 + i * 16 : 400 + i * 16] = both[384:, i * 128 : i * 128 + 128]


def add_second_kernel(*refs):
    factor = refs[10]
    for h in range(2):
        parts, owned = refs[h:8:2], refs[8 + h]
        total = parts[0][...].astype(f32)
        for part in parts[1:]:
            total = total + part[...].astype(f32)
        for j in range(3):
            owned[j] = total[j * 128 : j * 128 + 128].T.astype(bf16)
        factor[h * 128 : h * 128 + 128] = total[384:].T.astype(bf16)


def line_kernel(*refs):
    for h in range(2):
        for k, o in enumerate((3, 1, 2, 0)):
            refs[8 + h][o] = refs[2 * k + h][...]


def first_join_kernel(a, b, c, line, factor, out):
    for k, ref in enumerate((a, b, c, line)):
        out[k] = ref[...]
    out[4, 0] = jnp.zeros((3, 128, 128), bf16)
    for k in range(2):
        out[4, 0, k, :, :64] = factor[k * 128 : k * 128 + 128]
    for k in range(1, 4):
        out[4, k] = jnp.zeros((3, 128, 128), bf16)


def join_kernel(*refs):
    out = refs[-1]
    for k in range(out.shape[0]):
        out[k] = refs[k][...]


def assemble_kernel(tags, arrays, aliased, with_out, place, *refs):
    count = len(tags)
    sources, refs = refs[:arrays], refs[arrays + aliased :]
    if with_out:
        head_far, out, token, grad_out, held, ready, done, sems, whole, sent, factors, head_t = refs
        fetched = [pltpu.make_async_copy(head_far, head_t, sent.at[3])]
        fetched[0].start()
        for k, core in ((0, 1 - place[2]), (1, place[2])):
            target = factors.at[pl.ds(core * 2, 2)]
            fetched.append(pltpu.make_async_copy(sources[k].at[4, 0, 0:2], target, sent.at[1 + k]))
            fetched[k + 1].start()
    else:
        out, token, held, ready, done, sems = refs
    token[...] = jnp.zeros((8, 128), f32)
    loads = []
    for k, tag in enumerate(tags):
        source = sources[tag[0]] if tag[1] is None else sources[tag[0]].at[tag[1]]
        loads.append(pltpu.make_async_copy(source, held.at[k], sems.at[k]))
        loads[-1].start()
    if with_out:
        for copy in fetched:
            copy.wait()
        for k in range(4):
            whole[k * 128 : k * 128 + 128] = dot(factors[k, :, :64], head_t[...])
        leave = pltpu.make_async_copy(whole, grad_out, sent.at[0])
        leave.start()
    stores = []
    for k, tag in enumerate(tags):
        o, theirs, h, inners = tag[2:]
        loads[k].wait()
        first = (place[h] + 4 - o) % 4
        for i, inner in enumerate(inners):
            second = (place[1 - h] + 4 - inner) % 4
            ready[k, :, pl.ds(pl.multiple_of(second * 128, 128), 128)] = held[k, i].astype(f32)
        core = place[2] if theirs == 0 else 1 - place[2]
        stores.append(
            pltpu.make_async_copy(
                ready.at[k],
                out.at[
                    :,
                    pl.ds(pl.multiple_of(first * 512, 512), 512),
                    pl.ds(pl.multiple_of(core * 256 + h * 128, 128), 128),
                ],
                done.at[k],
            )
        )
        stores[k].start()
    for store in stores:
        store.wait()
    if with_out:
        leave.wait()


def assemble(place, arrays, tags, onto=None, product=()):
    tags = tuple(sorted(tags, key=lambda t: t[2:]))
    given = [] if onto is None else [onto]
    out_shape = [shape((3, 2048, 512), f32), shape((8, 128), f32)]
    out_specs = [HBM, VMEM]
    dma = pltpu.SemaphoreType.DMA
    scratch = [
        pltpu.VMEM((len(tags), *arrays[0].shape[-4:]), bf16),
        pltpu.VMEM((len(tags), 3, 512, 128), f32),
        dma((len(tags),)),
        dma((len(tags),)),
    ]
    if product:
        out_shape.append(shape((512, 2048), f32))
        out_specs.append(HBM)
        scratch += [pltpu.VMEM((512, 2048), f32), dma((4,)), pltpu.VMEM((4, 128, 128), bf16)]
        scratch.append(pltpu.VMEM((64, 2048), bf16))
    return pl.pallas_call(
        functools.partial(assemble_kernel, tags, len(arrays), len(given), bool(product)),
        in_specs=[SMEM] + [ANY] * len(arrays) + [HBM] * (len(given) + len(product)),
        out_specs=out_specs,
        out_shape=out_shape,
        scratch_shapes=scratch,
        input_output_aliases={1 + len(arrays): 0} if given else {},
        compiler_params=params(20),
        cost_estimate=TINY,
    )(place, *arrays, *given, *product)


def call(kernel, out, *operands, scratch=(), mib=8):
    result = pl.pallas_call(
        kernel,
        in_specs=[spec for spec, _ in operands],
        out_specs=[spec for spec, _ in out],
        out_shape=[made for _, made in out],
        scratch_shapes=list(scratch),
        compiler_params=params(mib),
        cost_estimate=TINY,
    )(*(array for _, array in operands))
    return result


def near(*arrays):
    return [(VMEM, a) for a in arrays]


def far(*arrays):
    return [(HBM, a) for a in arrays]


def shards(act, cache_rows, row_dest, time_index, w_embed, norm_gain, w_qkv, w_out, w_head):
    x, y, core, frame = (lax.axis_index(a).astype(jnp.int32) for a in ("x", "y", "core", "frame"))
    here = (SMEM, jnp.stack([frame, core]))
    square = (SMEM, jnp.stack([x, y, core]))
    dma = pltpu.SemaphoreType.DMA

    before, after, across = (shift(act, "frame", o) for o in (1, 3, 2))
    act_theirs = shift(act, "core", 1)
    head_t = w_head.T
    w_t, mix, mix_t = call(
        prepare_kernel,
        far(shape((768, 2048), bf16)) + near(shape((256, 64), f32), shape((64, 256), f32)),
        here, *far(w_qkv, w_out), *near(head_t),
        scratch=[
            pltpu.VMEM((3, 2048, 256), bf16),
            pltpu.VMEM((256, 2048), bf16),
            pltpu.VMEM((6, 128, 2048), bf16),
            dma((4,)),
            dma((6,)),
        ],
        mib=LARGE,
    )
    (sent,) = call(
        bucket_kernel, near(shape((4, 16, 2, 16, 128), bf16)),
        *far(cache_rows, row_dest.reshape(1, 128)),
        scratch=[pltpu.VMEM((128, 128), bf16), pltpu.VMEM((1, 128), jnp.int32), dma((2,))],
        mib=LARGE,
    )
    arrived = lax.all_to_all(
        sent.reshape(128, 16, 128), ("frame", "y", "x", "core"), 0, 0, tiled=True
    ).reshape(4, 512, 128)
    (sides,) = call(
        sides_kernel, near(shape((400, 2048), bf16)), (SMEM, time_index), *near(before, across, after), (ANY, arrived)
    )
    sides_theirs = shift(sides, "core", 1)
    (pairs,) = call(fetch_kernel, near(shape((8, 128, 128), bf16)), here, *near(arrived))
    normed, proj, probs, part_own, part_other = call(
        forward_kernel,
        far(shape((1024, 2048), bf16), shape((1024, 1024), bf16))
        + near(shape((4, 16, 128), f32), shape((64, 512), f32), shape((64, 512), f32)),
        *((ANY, a) for a in (act, act_theirs, sides, sides_theirs)),
        *near(pairs, w_embed, norm_gain.reshape(1, 2048)), *far(w_t), *near(head_t, mix_t),
        scratch=[
            pltpu.VMEM((8, 128, 2048), bf16),
            pltpu.VMEM((768, 2048), bf16),
            pltpu.VMEM((1024, 2048), bf16),
            pltpu.VMEM((1024, 1024), bf16),
            pltpu.VMEM((64, 128), f32),
            pltpu.VMEM((2, 16, 128), bf16),
            dma((4,)),
            dma((10,)),
        ],
        mib=LARGE,
    )

    clip_part = part_own + shift(part_other, "core", 1)
    error_own, frame_loss = call(
        error_kernel, near(shape((64, 512), f32), shape((1, 1), f32)),
        *near(clip_part, *(shift(clip_part, "frame", o) for o in (3, 1, 2))),
    )
    error_other = shift(error_own, "core", 1)

    piece = shape((400, 512), bf16)
    small = shape((448, 128), bf16)
    block = shape((3, 128, 128), bf16)
    line = shape((4, 3, 128, 128), bf16)
    axes = (("x", "y"), ("y", "x"))
    reach = (3, 1, 2)
    pieces = call(
        backward_kernel,
        near(*[piece] * 8),
        square, *near(error_own, error_other, probs, mix), *far(proj, normed),
        scratch=[
            pltpu.VMEM((768, 1024), bf16),
            pltpu.VMEM((2, 64, 128), bf16),
            pltpu.VMEM((64, 1024), f32),
            pltpu.VMEM((256, 1024), f32),
            pltpu.VMEM((1024, 1024), bf16),
            pltpu.VMEM((1024, 2048), bf16),
            dma((2,)),
        ],
        mib=49,
    )
    moved = [shift(p, axes[h][0], o) for (h, o), p in zip(PIECES[:6], pieces)]
    second = call(
        add_first_kernel, near(*[small] * 8), square, *near(*moved, *pieces[6:]),
        scratch=[pltpu.VMEM((400, 512), bf16)],
    )
    moved = [shift(second[h * 4 + o], axes[h][1], o) for h, o in PIECES[:6]]
    *owned, factor = call(
        add_second_kernel, near(block, block, shape((256, 64), bf16)),
        *near(*moved, second[0], second[4]),
    )
    back = [shift(owned[h], axes[h][1], o) for o in reach for h in range(2)]
    lines = call(
        line_kernel, near(line, line), *near(*back, *owned),
    )
    every = (0, 1, 2, 3)
    wide = [[shift(lines[h], axes[h][0], o) for o in reach] for h in range(2)]
    (half_x,) = call(
        first_join_kernel, near(shape((5, 4, 3, 128, 128), bf16)),
        *near(*wide[0], lines[0], factor),
    )
    half_x_theirs = shift(half_x, "core", 1)

    def tagged(array, side, h, distances):
        return [(array, k, o, side, h, every) for k, o in enumerate(distances)]

    grad_qkv, token = assemble(
        square[1], (half_x, lines[1]), tagged(0, 0, 0, (*reach, 0)) + [(1, None, 0, 0, 1, every)]
    )
    (half_y,) = call(
        join_kernel, near(shape((4, 4, 3, 128, 128), bf16)), *near(*wide[1], lines[1], token)
    )
    half_y_theirs = shift(half_y, "core", 1)
    grad_qkv, token, grad_out = assemble(
        square[1], (half_x_theirs, half_x, half_y),
        tagged(0, 1, 0, (*reach, 0)) + tagged(2, 0, 1, reach), grad_qkv, (head_t,),
    )
    grad_qkv, token = assemble(square[1], (half_y_theirs,), tagged(0, 1, 1, (*reach, 0)), grad_qkv)
    return frame_loss, grad_qkv, grad_out


def solution(mesh):
    fine = Mesh(mesh.devices.reshape(4, 4, 2, 4), ("y", "x", "core", "frame"))
    store = ("y", "x", "core")
    in_specs = (
        P((*store, "frame"), None),
        P((*store, "frame"), None),
        P((*store, "frame")),
        P(store),
        P(),
        P(),
        P(None, None, "frame"),
        P("frame", None),
        P(),
    )
    out_specs = (P(store, "frame"), P(None, None, "frame"), P("frame", None))
    return jax.shard_map(shards, mesh=fine, in_specs=in_specs, out_specs=out_specs, check_vma=False)
```
